32 devices in a mesh: segment: 4 (over x, core), th: 4 (over z), tw: 2 (over y).
Axes of the slice: x: 2, y: 2, z: 4, core: 2. Of those that a mesh axis runs over, the one named last changes fastest.
Arguments:
- tokens: bfloat16 [16, 16, 12, 2048], P(None, 'th', 'tw'), may hold values from -6 to 6
- frame_order: int32 [16], replicated, may hold values from 0 to 15, each once
- tile_pattern: int32 [4, 2, 9], P('th', 'tw'), may hold values from 0 to 1, as said below
- qkv_weight: bfloat16 [4, 2048, 4608], P('segment'), may hold values from -0.125 to 0.125
- out_weight: bfloat16 [4, 1536, 2048], P('segment'), may hold values from -0.15625 to 0.15625
- modulation: float32 [4, 3, 2048], P('segment'), may hold values from -4 to 4
Outputs:
- hidden_states: bfloat16 [16, 16, 12, 2048], P('segment', 'th', 'tw')
The draws below stay inside these ranges and needn't reach their ends.
Inputs may be any that keep to these rules, and one draw needn't show every extreme that they name: `tile_pattern`: each entry is 0 or 1; entry 4 (the tile itself) is 1 for every tile.
All inputs are finite; a program needn't handle non-finite values.
Results may differ from the reference program's by a relative error of at most 0.01.
Values may be sent and summed in bfloat16 or wider, within the bound.
No kernel may reach another device: no remote copies, remote signals or barrier semaphores. Data moves between devices by JAX's collectives and lax.ppermute only.
A program may use at most 128 MiB of HBM per device.

```python
import math
import jax
import jax.numpy as jnp
from jax import lax

D = 2048
HEADS = 12
HEAD = 128
TILE_H = 4
TILE_W = 6
HALO = 1
FRAME_PATCH = 4
PATCHES = 4
SECTIONS = 4
FRAMES = 16
TILES_H = 4
TILES_W = 2
GRID_H = 16
GRID_W = 12


def draw_tile_pattern(key, part):
    draws = jax.random.randint(key, (TILES_H, TILES_W, 9), 0, 4)
    flags = (draws > 0).astype(jnp.int32)
    centre = jnp.arange(9) == 4
    return jnp.where(centre[None, None, :], 1, flags).astype(jnp.int32)


def levels(stream_key, extent, cuts, low, top_value):
    loudness, own = 1.0, jax.random.fold_in(stream_key, 6)
    for position, blocks in cuts:
        steps = jnp.exp(jax.random.uniform(jax.random.fold_in(own, position), (blocks,), jnp.float32, low / len(cuts), top_value / len(cuts)))
        loudness = loudness * jnp.repeat(steps, extent[position] // blocks).reshape([-1 if axis == position else 1 for axis in range(len(extent))])
    return loudness


def bell_draw(own_key, extent, spread, bound, cuts=(), kind=jnp.bfloat16):
    level = levels(own_key, extent, cuts, -0.22, 0.18) if cuts else 1.0
    drawn = jax.random.normal(own_key, extent, jnp.float32) * spread * level
    return jnp.minimum(jnp.maximum(drawn, -bound), bound).astype(kind)


def setup_inputs(seed: int = 0) -> dict:
    seeds = jax.random.split(jax.random.key(seed), 7)
    tokens = bell_draw(seeds[0], (FRAMES, GRID_H, GRID_W, D), 1.0, 6.0, ((1, 4), (2, 2)))
    frame_order = jax.random.permutation(seeds[1], FRAMES).astype(jnp.int32)
    tile_pattern = draw_tile_pattern(jax.random.fold_in(seeds[6], 71), 0)
    qkv_weight = bell_draw(seeds[3], (SECTIONS, D, 3 * HEADS * HEAD), D ** -0.5, 0.125, ((0, 4),))
    out_weight = bell_draw(seeds[4], (SECTIONS, HEADS * HEAD, D), (HEADS * HEAD) ** -0.5, 0.15625, ((0, 4),))
    modulation = bell_draw(seeds[5], (SECTIONS, 3, D), 1.0, 4.0, ((0, 4),), jnp.float32)
    return dict(tokens=tokens, frame_order=frame_order, tile_pattern=tile_pattern, qkv_weight=qkv_weight, out_weight=out_weight, modulation=modulation)


def modulate(hidden, shift_row, scale_row):
    values = hidden.astype(jnp.float32)
    average = lax.optimization_barrier(jnp.mean(values, axis=-1, keepdims=True))
    centred = values - average
    variance = lax.optimization_barrier(jnp.mean(centred * centred, axis=-1, keepdims=True))
    normed = centred * lax.rsqrt(variance + 1e-06)
    return (normed * (1.0 + scale_row) + shift_row).astype(jnp.bfloat16)

def head_norm(values):
    shaped = values.reshape(values.shape[:-1] + (HEADS, HEAD))
    mean_square = lax.optimization_barrier(jnp.mean(shaped * shaped, axis=-1, keepdims=True))
    return (shaped * lax.rsqrt(mean_square + 1e-06)).reshape(values.shape).astype(jnp.bfloat16)

def block_ids(tile_h, tile_w, reach):
    row_range = jnp.arange(tile_h + 2 * reach).astype(jnp.int32)
    col_range = jnp.arange(tile_w + 2 * reach).astype(jnp.int32)
    row_part = (row_range >= reach).astype(jnp.int32) + (row_range >= tile_h + reach).astype(jnp.int32)
    col_part = (col_range >= reach).astype(jnp.int32) + (col_range >= tile_w + reach).astype(jnp.int32)
    return row_part[:, None] * 3 + col_part[None, :]

def attend(queries, key_rows, value_rows, allowed):
    group_count, query_count, inner_width = queries.shape
    key_count = key_rows.shape[1]
    query_heads = queries.reshape(group_count, query_count, HEADS, HEAD).astype(jnp.float32)
    key_heads = key_rows.reshape(group_count, key_count, HEADS, HEAD).astype(jnp.float32)
    value_heads = value_rows.reshape(group_count, key_count, HEADS, HEAD).astype(jnp.float32)
    scores = jnp.einsum('gqhd,gkhd->ghqk', query_heads, key_heads) * (1.0 / math.sqrt(HEAD))
    weighted = jnp.exp(scores) * allowed
    softmax_w = (weighted / lax.optimization_barrier(jnp.sum(weighted, axis=-1, keepdims=True))).astype(jnp.bfloat16)
    attended = jnp.einsum('ghqk,gkhd->gqhd', softmax_w.astype(jnp.float32), value_heads)
    return attended.reshape(group_count, query_count, inner_width).astype(jnp.bfloat16)

def section(hidden, qkv_w, out_w, modulation, tile_pattern):
    inner_width = HEADS * HEAD
    modded = modulate(hidden, modulation[0], modulation[1])
    projected = jnp.dot(modded.reshape(-1, D), qkv_w, preferred_element_type=jnp.float32)
    grid_shape = (PATCHES, FRAME_PATCH, GRID_H, GRID_W, inner_width)
    queries = head_norm(projected[:, :inner_width]).reshape(grid_shape)
    key_rows = head_norm(projected[:, inner_width:2 * inner_width]).reshape(grid_shape)
    value_rows = projected[:, 2 * inner_width:].astype(jnp.bfloat16).reshape(grid_shape)
    padding = ((0, 0), (0, 0), (HALO, HALO), (HALO, HALO), (0, 0))
    key_pad = jnp.pad(key_rows, padding)
    value_pad = jnp.pad(value_rows, padding)
    inside = jnp.pad(jnp.ones((GRID_H, GRID_W), jnp.float32), ((HALO, HALO), (HALO, HALO)))
    ext_rows = TILE_H + 2 * HALO
    ext_cols = TILE_W + 2 * HALO
    block_map = block_ids(TILE_H, TILE_W, HALO)
    nine = jnp.arange(9).astype(jnp.int32)

    def one_tile(tile_index):
        tile_row = tile_index // TILES_W
        tile_col = tile_index % TILES_W
        row_start = (tile_row * TILE_H).astype(jnp.int32)
        col_start = (tile_col * TILE_W).astype(jnp.int32)
        anchor = jnp.zeros((), jnp.int32)
        query_tile = lax.dynamic_slice(queries, (anchor, anchor, row_start, col_start, anchor), (PATCHES, FRAME_PATCH, TILE_H, TILE_W, inner_width))
        key_tile = lax.dynamic_slice(key_pad, (anchor, anchor, row_start, col_start, anchor), (PATCHES, FRAME_PATCH, ext_rows, ext_cols, inner_width))
        value_tile = lax.dynamic_slice(value_pad, (anchor, anchor, row_start, col_start, anchor), (PATCHES, FRAME_PATCH, ext_rows, ext_cols, inner_width))
        inside_tile = lax.dynamic_slice(inside, (row_start, col_start), (ext_rows, ext_cols))
        tile_flags = tile_pattern[tile_row, tile_col]
        chosen = lax.optimization_barrier(jnp.sum(jnp.where(block_map[:, :, None] == nine[None, None, :], tile_flags[None, None, :], 0), axis=-1))
        allowed_grid = inside_tile * chosen.astype(jnp.float32)
        allowed = jnp.broadcast_to(allowed_grid[None], (FRAME_PATCH, ext_rows, ext_cols)).reshape(-1)
        return attend(query_tile.reshape(PATCHES, -1, inner_width), key_tile.reshape(PATCHES, -1, inner_width), value_tile.reshape(PATCHES, -1, inner_width), allowed)
    tile_out = lax.map(one_tile, jnp.arange(TILES_H * TILES_W).astype(jnp.int32))
    tile_out = tile_out.reshape(TILES_H, TILES_W, PATCHES, FRAME_PATCH, TILE_H, TILE_W, inner_width)
    attended = tile_out.transpose(2, 3, 0, 4, 1, 5, 6).reshape(-1, inner_width)
    projected_out = jnp.dot(attended, out_w, preferred_element_type=jnp.float32)
    updated = hidden.astype(jnp.float32).reshape(-1, D) + modulation[2] * projected_out
    return updated.astype(jnp.bfloat16).reshape(hidden.shape)

def reference(tokens, frame_order, tile_pattern, qkv_weight, out_weight, modulation):
    ordered = jnp.take(tokens, frame_order, axis=0)
    hidden = ordered.reshape(PATCHES, FRAME_PATCH, GRID_H, GRID_W, D)
    for section_id in reversed(range(SECTIONS)):
        hidden = section(hidden, qkv_weight[section_id], out_weight[section_id], modulation[section_id], tile_pattern)
    return hidden.reshape(FRAMES, GRID_H, GRID_W, D)
```

```python
import functools
import math

import jax
import jax.numpy as jnp
from jax import lax
from jax.experimental import pallas as pl
from jax.experimental.pallas import tpu as pltpu
from jax.sharding import PartitionSpec as P

HEAD = 128
HALO = 1
FRAME_PATCH = 4
CHUNK = 512
VMEM_BYTES = 28 * 2**20
AXES = ("segment", "th", "tw")
ACTIVE, SOURCE, LOW_FIRST, VALID_A, VALID_B = range(5)


def head_norm(values):
    mean_square = jnp.mean(values * values, axis=-1, keepdims=True)
    return values * lax.rsqrt(mean_square + 1e-06)


def per_head(values, fn):
    heads = values.shape[-1] // HEAD
    return jnp.concatenate(
        [fn(values[:, h * HEAD : (h + 1) * HEAD]) for h in range(heads)], axis=-1
    )


def key_value_kernel(step, layout, sources, flags, *refs):
    count = sum(sources)
    parts, (mod, weight) = refs[:count], refs[count : count + 2]
    x_out, modded, kv, send_a, send_b = refs[count + 2 :]
    sides, tile_rows, edge_rows = layout
    inner = kv.shape[1] // 2

    @pl.when(flags[step, ACTIVE] != 0)
    def _():
        source = flags[step, SOURCE]
        for side in range(sides):
            rows = pl.ds(side * tile_rows, tile_rows)
            value, first = None, 0
            for index, pieces in enumerate(sources):
                part = parts[first + side][...] if pieces > 1 else parts[first][rows, :]
                part = part.astype(jnp.float32)
                value = part if value is None else jnp.where(source == index, part, value)
                first += pieces
            x_out[rows, :] = value.astype(jnp.bfloat16)
            centred = value - jnp.mean(value, axis=-1, keepdims=True)
            variance = jnp.mean(centred * centred, axis=-1, keepdims=True)
            normed = centred * lax.rsqrt(variance + 1e-06)
            modded[rows, :] = (normed * (1.0 + mod[1:2, :]) + mod[0:1, :]).astype(jnp.bfloat16)
        low_first = flags[step, LOW_FIRST] != 0
        for start in range(0, 2 * inner, CHUNK):
            columns = pl.ds(start, CHUNK)
            projected = jnp.dot(
                modded[...],
                weight[:, inner + start : inner + start + CHUNK],
                preferred_element_type=jnp.float32,
            )
            if start < inner:
                projected = per_head(projected, head_norm)
            kv[:, columns] = projected.astype(jnp.bfloat16)
            top, low = [], []
            for side in range(sides):
                base = side * tile_rows
                top.append(projected[base : base + edge_rows])
                low.append(projected[base + tile_rows - edge_rows : base + tile_rows])
            top, low = jnp.concatenate(top, axis=0), jnp.concatenate(low, axis=0)
            send_a[:, columns] = jnp.where(low_first, low, top).astype(jnp.bfloat16)
            send_b[:, columns] = jnp.where(low_first, top, low).astype(jnp.bfloat16)


def masked(mask_ref, sides, tile_rows):
    keys = mask_ref.shape[1]
    return jnp.concatenate(
        [jnp.broadcast_to(mask_ref[s : s + 1, :], (tile_rows, keys)) for s in range(sides)], axis=0
    )


def weigh(query, key, value, mask):
    scores = lax.dot_general(
        query, key, (((1,), (1,)), ((), ())), preferred_element_type=jnp.float32
    ) * (1.0 / math.sqrt(HEAD))
    weights = (jnp.exp(scores) * mask).astype(jnp.bfloat16)
    ones = jnp.ones((value.shape[0], HEAD), jnp.bfloat16)
    both = jnp.dot(
        weights, jnp.concatenate([value, ones], axis=1), preferred_element_type=jnp.float32
    )
    return both[:, :HEAD], both[:, HEAD:]


def query_kernel(step, layout, flags, modded, weight, kv, mask_ref, queries, top, bottom):
    sides, tile_rows, _ = layout
    inner = queries.shape[1]

    @pl.when(flags[step, ACTIVE] != 0)
    def _():
        mask = masked(mask_ref, sides, tile_rows)
        for start in range(0, inner, CHUNK):
            projected = jnp.dot(
                modded[...], weight[:, start : start + CHUNK], preferred_element_type=jnp.float32
            )
            for low in range(0, CHUNK, HEAD):
                columns = pl.ds(start + low, HEAD)
                query = head_norm(projected[:, low : low + HEAD]).astype(jnp.bfloat16)
                queries[:, columns] = query
                above, below = weigh(
                    query, kv[:, columns], kv[:, pl.ds(inner + start + low, HEAD)], mask
                )
                top[:, columns] = above
                bottom[:, columns] = below


def output_kernel(step, layout, extra_count, flags, *refs):
    extras, refs = refs[:extra_count], refs[extra_count:]
    queries, top, bottom, mask_ref, x, mod, weight, y, attended = refs
    sides, tile_rows, _ = layout
    inner, width = weight.shape

    @pl.when(flags[step, ACTIVE] != 0)
    def _():
        mask = masked(mask_ref, sides, tile_rows)
        valid = [flags[step, VALID_A] != 0, flags[step, VALID_B] != 0]

        def received(columns):
            pieces = []
            for index, extra in enumerate(extras):
                piece = extra[:, columns]
                if index < 2:
                    piece = jnp.where(valid[index], piece, jnp.zeros_like(piece))
                pieces.append(piece)
            return jnp.concatenate(pieces, axis=0)

        for low in range(0, inner, HEAD):
            columns = pl.ds(low, HEAD)
            above, below = weigh(
                queries[:, columns], received(columns), received(pl.ds(inner + low, HEAD)), mask
            )
            total = (top[:, columns] + above) / (bottom[:, columns] + below)
            attended[:, columns] = total.astype(jnp.bfloat16)
        for start in range(0, width, CHUNK):
            columns = pl.ds(start, CHUNK)
            projected = jnp.dot(
                attended[...], weight[:, start : start + CHUNK], preferred_element_type=jnp.float32
            )
            updated = x[:, columns].astype(jnp.float32) + mod[2:3, start : start + CHUNK] * projected
            y[:, columns] = updated.astype(jnp.bfloat16)


def run(kernel, flags, operands, outs, scratch, flops, name):
    vmem = pl.BlockSpec(memory_space=pltpu.VMEM)
    return pl.pallas_call(
        kernel,
        out_shape=outs,
        in_specs=[pl.BlockSpec(memory_space=pltpu.SMEM)] + [vmem] * len(operands),
        out_specs=jax.tree.map(lambda _: vmem, outs),
        scratch_shapes=scratch,
        compiler_params=pltpu.CompilerParams(vmem_limit_bytes=VMEM_BYTES),
        cost_estimate=pl.CostEstimate(flops=flops, bytes_accessed=2**20, transcendentals=0),
        name=name,
    )(flags, *operands)


def arrays(*shapes):
    return tuple(jax.ShapeDtypeStruct(shape, dtype) for shape, dtype in shapes)


def exchange(value, partner):
    sizes = [lax.axis_size(axis) for axis in AXES]
    places = [(s, t, w) for s in range(sizes[0]) for t in range(sizes[1]) for w in range(sizes[2])]
    number = {place: index for index, place in enumerate(places)}
    links = [(number[p], number[partner(*p)]) for p in places if partner(*p) in number]
    return lax.ppermute(value, AXES, links)


def on_device(tokens, frame_order, tile_pattern, qkv_weight, out_weight, modulation):
    n_seg, n_th, n_tw = [lax.axis_size(axis) for axis in AXES]
    seg, row_tile, col_tile = [lax.axis_index(axis) for axis in AXES]
    frames, tile_h, tile_w, width = tokens.shape
    inner = out_weight.shape[1]
    patches = frames // FRAME_PATCH
    sides = 2 if n_tw % 2 == 0 and patches % 2 == 0 else 1
    rounds = patches // sides
    tile_rows = FRAME_PATCH * tile_h * tile_w
    edge_rows = FRAME_PATCH * tile_w
    strip_rows = sides * tile_rows
    layout = (sides, tile_rows, edge_rows)
    lane = col_tile % sides

    def patch_of(turn, member):
        return (rounds - 1 - turn) * sides + member

    wanted = []
    for turn in range(rounds):
        for other in range(sides):
            start = patch_of(turn, (lane + other) % sides) * FRAME_PATCH
            wanted.append(lax.dynamic_slice_in_dim(frame_order, start, FRAME_PATCH))

    def tile_tokens(index):
        picked = jnp.take(tokens, wanted[index], axis=0)
        return picked.transpose(1, 0, 2, 3).reshape(tile_rows, width)

    def side_swap(s, t, w):
        return (s, t, w + 1 - 2 * (w % 2))

    fresh = []
    for turn in range(rounds):
        mine = [tile_tokens(turn * sides)]
        if sides == 2:
            mine.append(exchange(tile_tokens(turn * sides + 1), side_swap))
        fresh.append(mine)

    patterns = [tile_pattern[0, 0]]
    if sides == 2:
        patterns.append(exchange(tile_pattern[0, 0], side_swap))
    patterns = jnp.stack(patterns)
    tile_cols = jnp.stack([col_tile, col_tile + 1 - 2 * lane][:sides])
    paired_rows = n_th % 2 == 0
    low_first = (row_tile % 2 == 0) if paired_rows else jnp.array(True)
    row_a = jnp.where(low_first, tile_h, -1) if paired_rows else jnp.array(-1)
    row_b = jnp.where(low_first, -1, tile_h) if paired_rows else jnp.array(tile_h)
    frame_zero = jnp.zeros((FRAME_PATCH, 1), jnp.int32)
    strip_cols = (tile_cols[:, None, None] * tile_w + frame_zero + jnp.arange(tile_w)).reshape(-1)
    tile_key_rows = jnp.arange(tile_rows) // edge_rows
    own_rows = jnp.tile(tile_key_rows, sides)
    own_cols = (
        (tile_cols[:, None, None, None] * tile_w + frame_zero + jnp.arange(tile_w))
        + jnp.zeros((1, tile_h, 1, 1), jnp.int32)
    ).reshape(-1)
    side_halo = n_tw > sides
    extra_rows = [jnp.full((sides * edge_rows,), 1, jnp.int32) * row for row in (row_a, row_b)]
    extra_cols = [strip_cols, strip_cols]
    strip_left = (col_tile - lane) * tile_w
    if side_halo:
        tall = jnp.repeat(jnp.arange(-HALO, tile_h + HALO), FRAME_PATCH)
        for col in (strip_left - 1, strip_left + sides * tile_w):
            extra_rows.append(tall)
            extra_cols.append(jnp.zeros_like(tall) + col)

    def mask_of(key_rows, key_cols):
        cols = key_cols[None, :] - tile_cols[:, None] * tile_w
        rows = key_rows[None, :]
        block = (
            ((rows >= 0).astype(jnp.int32) + (rows >= tile_h)) * 3
            + (cols >= 0).astype(jnp.int32)
            + (cols >= tile_w)
        )
        flags = jnp.sum(
            jnp.where(block[..., None] == jnp.arange(9), patterns[:, None, :], 0), axis=-1
        )
        global_rows = rows + row_tile * tile_h
        near = (cols >= -HALO) & (cols < tile_w + HALO)
        inside = (global_rows >= 0) & (global_rows < n_th * tile_h)
        inside &= (key_cols >= 0)[None, :] & (key_cols < n_tw * tile_w)[None, :]
        return jnp.where(near & inside, flags, 0).astype(jnp.float32)

    own_mask = mask_of(own_rows, own_cols)
    extra_mask = mask_of(jnp.concatenate(extra_rows), jnp.concatenate(extra_cols))

    first = {n_seg - 1: 0}
    for s in range(n_seg - 1, 0, -1):
        first[s - 1] = first[s] + (1 if s % 2 else 2)
    steps = first[0] + rounds

    def running(step):
        return [s for s in range(n_seg) if 0 <= step - first[s] < rounds]

    valid_a = (row_tile + jnp.where(row_a < 0, -1, 1) >= 0) & (
        row_tile + jnp.where(row_a < 0, -1, 1) < n_th
    )
    valid_b = (row_tile + jnp.where(row_b < 0, -1, 1) >= 0) & (
        row_tile + jnp.where(row_b < 0, -1, 1) < n_th
    )
    entry = seg == n_seg - 1
    kinds = []
    table = []
    for step in range(steps):
        live = running(step)
        kind = []
        if n_seg - 1 in live:
            kind.append("fresh")
        if any(s % 2 == 0 and s != n_seg - 1 for s in live):
            kind.append("near")
        if any(s % 2 == 1 and s != n_seg - 1 for s in live):
            kind.append("far")
        kinds.append(kind)
        mine = jnp.where(entry, kind.index("fresh") if "fresh" in kind else 0, 0)
        if "near" in kind:
            mine = jnp.where((seg % 2 == 0) & ~entry, kind.index("near"), mine)
        if "far" in kind:
            mine = jnp.where((seg % 2 == 1) & ~entry, kind.index("far"), mine)
        active = functools.reduce(jnp.logical_or, [seg == s for s in live])
        row = [active, mine, low_first, valid_a, valid_b]
        table.append(jnp.stack([jnp.asarray(v).astype(jnp.int32) for v in row]))
    flags = jnp.stack(table)

    qkv_w = pltpu.with_memory_space_constraint(qkv_weight[0], pltpu.VMEM)
    out_w = pltpu.with_memory_space_constraint(out_weight[0], pltpu.VMEM)
    mod = modulation[0]

    def rows_a(s, t, w):
        return (s, t + 1 - 2 * (t % 2), w) if paired_rows else (s, t + 1, w)

    def rows_b(s, t, w):
        return (s, t - 1 + 2 * (t % 2), w) if paired_rows else (s, t - 1, w)

    def edge_column(kv, above, below, which):
        body = kv.reshape(sides, tile_h, FRAME_PATCH, tile_w, 2 * inner)
        ends = [part.reshape(sides, 1, FRAME_PATCH, tile_w, 2 * inner) for part in (above, below)]
        tall = jnp.concatenate([ends[0], body, ends[1]], axis=1)
        if which == 0:
            column = jnp.where(lane == 0, tall[0, :, :, 0], tall[sides - 1, :, :, 0])
        else:
            column = jnp.where(lane == 0, tall[sides - 1, :, :, -1], tall[0, :, :, -1])
        return column.reshape(-1, 2 * inner)

    def layer(step, sources):
        operands = [part for source in sources for part in source]
        counts = tuple(len(source) for source in sources)
        bf16, f32 = jnp.bfloat16, jnp.float32
        x, modded, kv, send_a, send_b = run(
            functools.partial(key_value_kernel, step, layout, counts),
            flags,
            operands + [mod, qkv_w],
            arrays(
                ((strip_rows, width), bf16),
                ((strip_rows, width), bf16),
                ((strip_rows, 2 * inner), bf16),
                ((sides * edge_rows, 2 * inner), bf16),
                ((sides * edge_rows, 2 * inner), bf16),
            ),
            [],
            4 * strip_rows * width * inner,
            "key_value",
        )
        extra_a = exchange(send_a, rows_a)
        extra_b = exchange(send_b, rows_b)
        queries, top, bottom = run(
            functools.partial(query_kernel, step, layout),
            flags,
            [modded, qkv_w, kv, own_mask],
            arrays(
                ((strip_rows, inner), bf16), ((strip_rows, inner), f32), ((strip_rows, inner), f32)
            ),
            [],
            4 * strip_rows * width * inner,
            "query",
        )
        extras = [extra_a, extra_b]
        if side_halo:
            flip = (row_a < 0) if paired_rows else jnp.array(True)
            above = jnp.where(flip, extra_a, extra_b)
            below = jnp.where(flip, extra_b, extra_a)
            above = jnp.where(row_tile > 0, above, jnp.zeros_like(above))
            below = jnp.where(row_tile < n_th - 1, below, jnp.zeros_like(below))
            left = edge_column(kv, above, below, 0)
            right = edge_column(kv, above, below, 1)
            extras.append(exchange(right, lambda s, t, w: (s, t, w + sides)))
            extras.append(exchange(left, lambda s, t, w: (s, t, w - sides)))
        (y,) = run(
            functools.partial(output_kernel, step, layout, len(extras)),
            flags,
            extras + [queries, top, bottom, extra_mask, x, mod, out_w],
            arrays(((strip_rows, width), bf16)),
            [pltpu.VMEM((strip_rows, inner), bf16)],
            4 * strip_rows * width * inner,
            "output",
        )
        return y

    held_patches = patches // n_seg
    pieces = {}
    near = far = far_next = None
    for step in range(steps):
        live = running(step)
        options = {"near": [near], "far": [far]}
        if step < rounds:
            options["fresh"] = fresh[step]
        y = layer(step, [options[kind] for kind in kinds[step]])
        near, far, far_next = None, far_next, None
        if any(s % 2 == 1 for s in live):
            near = exchange(y, lambda s, t, w: (s ^ 1, t, w))
        if any(s % 2 == 0 and s > 0 for s in live):
            far_next = exchange(
                y, lambda s, t, w: (s - 1, t, w) if s % 2 == 0 and s > 0 else None
            )
        if 0 in live:
            turn = step - first[0]
            halves = [y[:tile_rows]]
            if sides == 2:
                got = exchange(y[tile_rows:], side_swap)
                halves = [
                    jnp.where(lane == 0, y[:tile_rows], got),
                    jnp.where(lane == 0, got, y[:tile_rows]),
                ]
            for member, half in enumerate(halves):
                patch = patch_of(turn, member)
                owner = patch // held_patches
                if owner == 1:
                    half = exchange(half, lambda s, t, w: (s ^ 1, t, w))
                elif owner > 0:
                    half = exchange(half, lambda s, t, w: (owner, t, w) if s == 0 else None)
                pieces[patch] = half
    outputs = []
    for place in range(held_patches):
        chosen = pieces[place]
        for owner in range(1, n_seg):
            chosen = jnp.where(seg == owner, pieces[owner * held_patches + place], chosen)
        shaped = chosen.reshape(tile_h, FRAME_PATCH, tile_w, width).transpose(1, 0, 2, 3)
        outputs.append(shaped)
    return jnp.concatenate(outputs, axis=0)


def solution(mesh):
    in_specs = (
        P(None, "th", "tw", None),
        P(),
        P("th", "tw", None),
        P("segment", None, None),
        P("segment", None, None),
        P("segment", None, None),
    )
    out_specs = P("segment", "th", "tw", None)
    return jax.shard_map(
        on_device, mesh=mesh, in_specs=in_specs, out_specs=out_specs, check_vma=False
    )
```

```python
import functools
import math

import jax
import jax.numpy as jnp
import numpy as np
from jax import lax
from jax.experimental import pallas as pl
from jax.experimental.pallas import tpu as pltpu
from jax.sharding import PartitionSpec as P

HEAD = 128
HALO = 1
FRAME_PATCH = 4
CHUNK = 512
VMEM_BYTES = 10 * 2**20
AXES = ("segment", "th", "tw")
SEG, ROW, COL = range(3)


def head_norm(values):
    mean_square = jnp.mean(values * values, axis=-1, keepdims=True)
    return values * lax.rsqrt(mean_square + 1e-06)


def is_active(place, live):
    return functools.reduce(jnp.logical_or, [place[SEG] == s for s in live])


def neighbour_rows(place, n_th, tile_h):
    below_first = place[ROW] % 2 == 0 if n_th % 2 == 0 else place[ROW] < 0
    row_a = jnp.where(below_first, tile_h, -1)
    row_b = jnp.where(below_first, -1, tile_h)
    valid = []
    for row in (row_a, row_b):
        tile = place[ROW] + jnp.where(row < 0, -1, 1)
        valid.append((tile >= 0) & (tile < n_th))
    return row_a, row_b, valid


def write_masks(spec, place, patterns, tables, outs):
    sides, tile_h, tile_w, n_th, n_tw = spec
    row_a, row_b, _ = neighbour_rows(place, n_th, tile_h)
    lane = place[COL] % sides
    for table, out in zip(tables, outs):
        side, kind = table[0:1, :], table[1:2, :]
        col, row = table[2:3, :], table[3:4, :]
        row = jnp.where(kind == 1, row_a, jnp.where(kind == 2, row_b, row))
        for query_side in range(sides):
            spot = lane if query_side == 0 else 1 - lane
            tile_col = place[COL] - lane + spot
            cols = (side - query_side) * (1 - 2 * lane) * tile_w + col
            cols = jnp.where(kind == 3, -1 - spot * tile_w, cols)
            cols = jnp.where(kind == 4, (sides - spot) * tile_w, cols)
            block = (
                ((row >= 0).astype(jnp.int32) + (row >= tile_h).astype(jnp.int32)) * 3
                + (cols >= 0).astype(jnp.int32)
                + (cols >= tile_w).astype(jnp.int32)
            )
            flag = jnp.zeros(block.shape, jnp.int32)
            for index in range(9):
                flag = jnp.where(block == index, patterns[query_side][0, index], flag)
            grid_row, grid_col = row + place[ROW] * tile_h, cols + tile_col * tile_w
            inside = (grid_row >= 0) & (grid_row < n_th * tile_h)
            inside &= (grid_col >= 0) & (grid_col < n_tw * tile_w)
            inside &= (cols >= -HALO) & (cols < tile_w + HALO)
            out[query_side : query_side + 1, :] = jnp.where(inside, flag, 0).astype(jnp.float32)


def key_value_kernel(live, spec, sources, masks, place, *refs):
    sides, tile_h, _, n_th, _ = spec
    count = sum(pieces for _, pieces in sources)
    parts, (mod, weight), refs = refs[:count], refs[count : count + 2], refs[count + 2 :]
    if masks:
        patterns, tables, refs = refs[:sides], refs[sides : sides + 2], refs[sides + 2 :]
        write_masks(spec, place, patterns, tables, refs[5:7])
    x_out, modded, kv, send_a, send_b = refs[:5]
    wide = refs[-1]
    inner = kv.shape[1] // 2
    tile_rows = kv.shape[0] // sides
    edges = kv.shape[0] // tile_h

    @pl.when(is_active(place, live))
    def _():
        for side in range(sides):
            rows = pl.ds(side * tile_rows, tile_rows)
            value, first = None, 0
            for holders, pieces in sources:
                part = parts[first + side][...] if pieces == sides else parts[first][rows, :]
                part = part.astype(jnp.float32).reshape(tile_rows, part.shape[-1])
                value = part if value is None else jnp.where(is_active(place, holders), part, value)
                first += pieces
            x_out[rows, :] = value.astype(jnp.bfloat16)
            centred = value - jnp.mean(value, axis=-1, keepdims=True)
            variance = jnp.mean(centred * centred, axis=-1, keepdims=True)
            normed = centred * lax.rsqrt(variance + 1e-06)
            modded[rows, :] = (normed * (1.0 + mod[1:2, :]) + mod[0:1, :]).astype(jnp.bfloat16)
        row_a, row_b, _ = neighbour_rows(place, n_th, tile_h)
        offset_a = jnp.where(row_a < 0, 0, tile_h - 1)
        offset_b = jnp.where(row_b < 0, 0, tile_h - 1)
        if n_th % 2:
            offset_a, offset_b = offset_b, offset_a
        for start in range(0, 2 * inner, CHUNK):
            projected = jnp.dot(
                modded[...], weight[:, start : start + CHUNK], preferred_element_type=jnp.float32
            )
            for low in range(0, CHUNK, HEAD):
                columns = pl.ds(start + low, HEAD)
                head = projected[:, low : low + HEAD]
                if start < inner:
                    head = head_norm(head)
                kv[:, columns] = head.astype(jnp.bfloat16)
                slot = wide.at[(start + low) // HEAD % wide.shape[0]]
                slot[...] = head
                send_a[:, columns] = slot[pl.ds(offset_a, edges, stride=tile_h), :].astype(
                    jnp.bfloat16
                )
                send_b[:, columns] = slot[pl.ds(offset_b, edges, stride=tile_h), :].astype(
                    jnp.bfloat16
                )


def masked(mask_ref, sides, tile_rows):
    keys = mask_ref.shape[1]
    return jnp.concatenate(
        [jnp.broadcast_to(mask_ref[s : s + 1, :], (tile_rows, keys)) for s in range(sides)], axis=0
    )


def weigh(query, key, value, mask):
    scores = lax.dot_general(
        query, key, (((1,), (1,)), ((), ())), preferred_element_type=jnp.float32
    ) * (1.0 / math.sqrt(HEAD))
    weights = (jnp.exp(scores) * mask).astype(jnp.bfloat16)
    ones = jnp.ones((value.shape[0], HEAD), jnp.bfloat16)
    both = jnp.dot(
        weights, jnp.concatenate([value, ones], axis=1), preferred_element_type=jnp.float32
    )
    return both[:, :HEAD], both[:, HEAD:]


def query_kernel(live, spec, place, modded, weight, kv, mask_ref, queries, top, bottom):
    sides = spec[0]
    tile_rows, inner = queries.shape[0] // sides, queries.shape[1]

    @pl.when(is_active(place, live))
    def _():
        mask = masked(mask_ref, sides, tile_rows)
        for start in range(0, inner, CHUNK):
            projected = jnp.dot(
                modded[...], weight[:, start : start + CHUNK], preferred_element_type=jnp.float32
            )
            for low in range(0, CHUNK, HEAD):
                columns = pl.ds(start + low, HEAD)
                query = head_norm(projected[:, low : low + HEAD]).astype(jnp.bfloat16)
                queries[:, columns] = query
                above, below = weigh(
                    query, kv[:, columns], kv[:, pl.ds(inner + start + low, HEAD)], mask
                )
                top[:, columns] = above
                bottom[:, columns] = below


def output_kernel(live, spec, extra_count, place, *refs):
    extras, refs = refs[:extra_count], refs[extra_count:]
    (queries, top, bottom, mask_ref, x, mod, weight), outs = refs[:7], refs[7:-1]
    attended = refs[-1]
    sides, tile_h, _, n_th, _ = spec
    inner, width = weight.shape
    tile_rows = queries.shape[0] // sides

    @pl.when(is_active(place, live))
    def _():
        mask = masked(mask_ref, sides, tile_rows)
        valid = neighbour_rows(place, n_th, tile_h)[2]

        def received(columns):
            pieces = []
            for index, extra in enumerate(extras):
                piece = extra[:, columns]
                if index < 2:
                    piece = jnp.where(valid[index], piece, jnp.zeros_like(piece))
                pieces.append(piece)
            return jnp.concatenate(pieces, axis=0)

        for low in range(0, inner, HEAD):
            columns = pl.ds(low, HEAD)
            above, below = weigh(
                queries[:, columns], received(columns), received(pl.ds(inner + low, HEAD)), mask
            )
            total = (top[:, columns] + above) / (bottom[:, columns] + below)
            attended[:, columns] = total.astype(jnp.bfloat16)
        for start in range(0, width, CHUNK):
            columns = pl.ds(start, CHUNK)
            projected = jnp.dot(
                attended[...], weight[:, start : start + CHUNK], preferred_element_type=jnp.float32
            )
            updated = x[:, columns].astype(jnp.float32) + mod[2:3, start : start + CHUNK] * projected
            updated = updated.astype(jnp.bfloat16)
            for index, y in enumerate(outs):
                y[:, columns] = updated[index * y.shape[0] : (index + 1) * y.shape[0]]


def choose_kernel(wanted, place, *refs):
    pieces, out = refs[:-1], refs[-1]
    rows = out.shape[0] // len(wanted)
    for index, options in enumerate(wanted):
        for segment, lane, sides, source in options:

            @pl.when((place[SEG] == segment) & (place[COL] % sides == lane))
            def _(index=index, source=source):
                value = pieces[source][...].astype(jnp.float32).reshape(rows, *out.shape[1:])
                out[index * rows : (index + 1) * rows] = value.astype(jnp.bfloat16)


def gather_copies(place, order, tokens, outs, wanted, sides, sems):
    copies = []
    for slot, (out, (base, other)) in enumerate(zip(outs, wanted)):
        patch = base + (place[COL] + other) % sides
        rows = out.shape[0] // FRAME_PATCH
        for frame in range(FRAME_PATCH):
            source = order[patch * FRAME_PATCH + frame]
            copies.append(
                pltpu.make_async_copy(
                    tokens.at[pl.ds(source * rows, rows)],
                    out.at[pl.ds(frame * rows, rows)],
                    sems.at[slot, frame],
                )
            )
    for copy in copies:
        copy.start()
    return copies


def gather_kernel(wanted, sides, place, order, tokens, *refs):
    for copy in gather_copies(place, order, tokens, refs[:-1], wanted, sides, refs[-1]):
        copy.wait()


def load_kernel(wanted, sides, place, order, tokens, qkv, kv_out, q_out, *refs):
    outs, frame_sems, sems = refs[:-2], refs[-2], refs[-1]
    inner = q_out.shape[1]
    copies = gather_copies(place, order, tokens, outs, wanted, sides, frame_sems)
    copies += [
        pltpu.make_async_copy(qkv.at[:, pl.ds(inner, 2 * inner)], kv_out, sems.at[0]),
        pltpu.make_async_copy(qkv.at[:, pl.ds(0, inner)], q_out, sems.at[1]),
    ]
    for copy in copies[-2:]:
        copy.start()
    for copy in copies:
        copy.wait()


def run(kernel, scalars, operands, outs, scratch, name, memory=pltpu.VMEM, limit=VMEM_BYTES):
    vmem, smem = pl.BlockSpec(memory_space=pltpu.VMEM), pl.BlockSpec(memory_space=pltpu.SMEM)
    if memory is pltpu.HBM:
        operands = [pltpu.with_memory_space_constraint(o, memory) for o in operands]
    return pl.pallas_call(
        kernel,
        out_shape=outs,
        in_specs=[smem] * len(scalars)
        + [smem if o.dtype == jnp.int32 and o.shape[-1] == 9 else pl.BlockSpec(memory_space=memory) for o in operands],
        out_specs=jax.tree.map(lambda _: vmem, outs),
        scratch_shapes=scratch,
        compiler_params=pltpu.CompilerParams(vmem_limit_bytes=limit),
        cost_estimate=pl.CostEstimate(flops=2**20, bytes_accessed=2**10, transcendentals=0),
        name=name,
    )(*scalars, *operands)


def arrays(*shapes):
    return tuple(jax.ShapeDtypeStruct(shape, dtype) for shape, dtype in shapes)


def exchange(value, partner):
    sizes = [lax.axis_size(axis) for axis in AXES]
    places = [(s, t, w) for s in range(sizes[0]) for t in range(sizes[1]) for w in range(sizes[2])]
    number = {place: index for index, place in enumerate(places)}
    links = [(number[p], number[partner(*p)]) for p in places if partner(*p) in number]
    return lax.ppermute(value, AXES, links)


def on_device(tokens, frame_order, tile_pattern, qkv_weight, out_weight, modulation):
    n_seg, n_th, n_tw = [lax.axis_size(axis) for axis in AXES]
    seg, row_tile, col_tile = [lax.axis_index(axis) for axis in AXES]
    frames, tile_h, tile_w, width = tokens.shape
    inner = out_weight.shape[1]
    patches = frames // FRAME_PATCH
    held_patches = patches // n_seg
    sides = 2 if n_tw % 2 == 0 and patches % 2 == 0 else 1
    rounds = patches // sides
    tile_rows = FRAME_PATCH * tile_h * tile_w
    edge_rows = FRAME_PATCH * tile_w
    strip_rows = sides * tile_rows

    lane = col_tile % sides
    bf16, f32 = jnp.bfloat16, jnp.float32

    def beside(w):
        return w + 1 - 2 * (w % 2)

    def patch_base(turn):
        return (rounds - 1 - turn) * sides

    def token_swap(s, t, w):
        if s == n_seg - 1:
            return (s, t, beside(w))
        return (s, t + 1 - 2 * (t % 2), w) if n_th % 2 == 0 else None

    place = jnp.stack([seg, row_tile, col_tile]).astype(jnp.int32)
    stored = tokens.transpose(0, 2, 1, 3).reshape(frames * tile_w, tile_h, width)
    tile_shape = ((edge_rows, tile_h, width), bf16)
    theirs, pattern = [], tile_pattern[0]
    patterns = [pattern]
    if sides == 2:
        (theirs0,) = run(
            functools.partial(gather_kernel, [(patch_base(0), 1)], sides),
            [place, frame_order],
            [stored],
            arrays(tile_shape),
            [pltpu.SemaphoreType.DMA((1, FRAME_PATCH))],
            "gather",
            pltpu.HBM,
            2**20,
        )
        theirs.append(exchange(theirs0, token_swap))
        patterns.append(exchange(pattern, lambda s, t, w: (s, t, beside(w))))
        theirs0, place, qkv_weight = lax.optimization_barrier((theirs0, place, qkv_weight))
    wanted = [(patch_base(turn), 0) for turn in range(rounds)]
    if sides == 2:
        wanted += [(patch_base(turn), 1) for turn in range(1, rounds)]
    kv_w, q_w, *tiles = run(
        functools.partial(load_kernel, wanted, sides),
        [place, frame_order],
        [stored, qkv_weight[0]],
        (pltpu.VMEM((width, 2 * inner), bf16), pltpu.VMEM((width, inner), bf16))
        + arrays(*[tile_shape] * len(wanted)),
        [pltpu.SemaphoreType.DMA((len(wanted), FRAME_PATCH)), pltpu.SemaphoreType.DMA((2,))],
        "load_weights",
        pltpu.HBM,
        2**20,
    )
    kv_w, q_w, out_w = [
        pltpu.with_memory_space_constraint(w, pltpu.VMEM) for w in (kv_w, q_w, out_weight[0])
    ]
    if sides == 2:
        theirs += [exchange(tile, token_swap) for tile in tiles[rounds:]]
    fresh = [[tiles[turn]] + ([theirs[turn]] if sides == 2 else []) for turn in range(rounds)]
    mod = modulation[0]

    side_halo = n_tw > sides
    grid = np.indices((sides, FRAME_PATCH, tile_w, tile_h)).reshape(4, -1)
    own_table = np.stack([grid[0], 0 * grid[0], grid[2], grid[3]])
    strip_edge = np.indices((sides, FRAME_PATCH, tile_w)).reshape(3, -1)
    extra = [
        np.stack([strip_edge[0], 0 * strip_edge[0] + kind, strip_edge[2], 0 * strip_edge[0]])
        for kind in (1, 2)
    ]
    if side_halo:
        tall = np.tile(np.arange(-HALO, tile_h + HALO), FRAME_PATCH)
        extra += [np.stack([0 * tall, 0 * tall + kind, 0 * tall, tall]) for kind in (3, 4)]
    tables = [jnp.asarray(t, jnp.int32) for t in (own_table, np.concatenate(extra, axis=1))]

    first = {n_seg - 1: 0}
    for s in range(n_seg - 1, 0, -1):
        first[s - 1] = first[s] + (1 if s % 2 else 2)
    steps = first[0] + rounds
    spec = (sides, tile_h, tile_w, n_th, n_tw)
    paired_rows, paired_segs = n_th % 2 == 0, n_seg % 2 == 0

    def running(step):
        return [s for s in range(n_seg) if 0 <= step - first[s] < rounds]

    def sources_of(step):
        live = running(step)
        found = []
        if n_seg - 1 in live:
            found.append(("fresh", [n_seg - 1]))
        near_to = [s for s in live if s % 2 == 0 and s != n_seg - 1]
        far_to = [s for s in live if s % 2 == 1 and s != n_seg - 1]
        return found + [("near", near_to)] * bool(near_to) + [("far", far_to)] * bool(far_to)

    def spare(live, s, t, w):
        if paired_segs and s ^ 1 not in live:
            return (s ^ 1, t, w)
        return (s, t, beside(w)) if n_tw % 2 == 0 else None

    def rows_a(live):
        def partner(s, t, w):
            if not paired_rows:
                return (s, t + 1, w)
            return (s, t + 1 - 2 * (t % 2), w) if s in live else spare(live, s, t, w)

        return partner

    def rows_b(live):
        def partner(s, t, w):
            other = t - 1 + 2 * (t % 2) if paired_rows else t - 1
            if paired_rows and not 0 <= other < n_th:
                return (s ^ 1, t, w) if paired_segs else None
            return (s, other, w) if s in live or not paired_rows else spare(live, s, t, w)

        return partner

    def near_hop(s, t, w):
        return (s ^ 1, t, w) if paired_segs else (s - 1, t, w) if s % 2 else None

    def far_hop(s, t, w):
        return (s - 1, t, w) if s % 2 == 0 and s > 0 else None

    def edge_column(kv, above, below, which):
        body = kv.reshape(sides, FRAME_PATCH, tile_w, tile_h, 2 * inner)
        ends = [part.reshape(sides, FRAME_PATCH, tile_w, 1, 2 * inner) for part in (above, below)]
        tall = jnp.concatenate([ends[0], body, ends[1]], axis=3)
        if which == 0:
            column = jnp.where(lane == 0, tall[0, :, 0], tall[sides - 1, :, 0])
        else:
            column = jnp.where(lane == 0, tall[sides - 1, :, -1], tall[0, :, -1])
        return column.reshape(-1, 2 * inner)

    masks = []

    def layer(step, live, sources):
        operands = [part for _, source in sources for part in source]
        counts = [(holders, len(source)) for holders, source in sources]
        strip = strip_rows
        outs = [
            ((strip, width), bf16),
            ((strip, width), bf16),
            ((strip, 2 * inner), bf16),
            ((sides * edge_rows, 2 * inner), bf16),
            ((sides * edge_rows, 2 * inner), bf16),
        ]
        operands += [mod, kv_w]
        if step == 0:
            operands += patterns + tables
            outs += [((sides, table.shape[1]), f32) for table in tables]
        x, modded, kv, send_a, send_b, *made = run(
            functools.partial(key_value_kernel, live, spec, counts, step == 0),
            [place],
            operands,
            arrays(*outs),
            [pltpu.VMEM((4, strip, HEAD), f32)],
            "key_value",
        )
        masks.extend(made)
        own_mask, extra_mask = masks
        extra_a = exchange(send_a, rows_a(live))
        extra_b = exchange(send_b, rows_b(live))
        queries, top, bottom = run(
            functools.partial(query_kernel, live, spec),
            [place],
            [modded, q_w, kv, own_mask],
            arrays(((strip, inner), bf16), ((strip, inner), f32), ((strip, inner), f32)),
            [],
            "query",
        )
        extras = [extra_a, extra_b]
        if side_halo:
            flip = (row_tile % 2 == 1) if paired_rows else jnp.array(True)
            above = jnp.where(flip, extra_a, extra_b)
            below = jnp.where(flip, extra_b, extra_a)
            above = jnp.where(row_tile > 0, above, jnp.zeros_like(above))
            below = jnp.where(row_tile < n_th - 1, below, jnp.zeros_like(below))
            left = edge_column(kv, above, below, 0)
            right = edge_column(kv, above, below, 1)
            from_left = exchange(right, lambda s, t, w: (s, t, w + sides))
            from_right = exchange(left, lambda s, t, w: (s, t, w - sides))
            extras.append(jnp.concatenate([from_left, from_right], axis=0))
        last = 0 in live
        out_shapes = [((tile_rows, width), bf16)] * sides if last else [((strip_rows, width), bf16)]
        return run(
            functools.partial(output_kernel, live, spec, len(extras)),
            [place],
            extras + [queries, top, bottom, extra_mask, x, mod, out_w],
            arrays(*out_shapes),
            [pltpu.VMEM((strip_rows, inner), bf16)],
            "output",
        )

    def owner_of(turn, w):
        return (patch_base(turn) + w % sides) // held_patches

    near = far = far_next = None
    finished = {}
    for step in range(steps):
        live = running(step)
        options = {"near": near, "far": [far]}
        if step < rounds:
            options["fresh"] = fresh[step]
        y = layer(step, live, [(holders, options[kind]) for kind, holders in sources_of(step)])
        near, far, far_next = None, far_next, None
        if any(s % 2 == 1 for s in live):
            near = [exchange(part, near_hop) for part in y]
        if any(s % 2 == 0 and s > 0 for s in live):
            far_next = exchange(y[0], far_hop)
        if 0 in live:
            turn = step - first[0]
            finished[turn] = [
                exchange(
                    part,
                    lambda s, t, w: (owner_of(turn, w), t, beside(w) if side else w)
                    if s == 0
                    else None,
                )
                for side, part in enumerate(y)
            ]
    wanted = []
    for held in range(held_patches):
        options = []
        for owner in range(n_seg):
            patch = owner * held_patches + held
            turn, member = rounds - 1 - patch // sides, patch % sides
            for w in range(sides):
                options.append((owner, w, sides, turn * sides + (0 if w == member else 1)))
        wanted.append(options)
    (chosen,) = run(
        functools.partial(choose_kernel, wanted),
        [place],
        [piece for turn in range(rounds) for piece in finished[turn]],
        arrays(((held_patches * edge_rows, tile_h, width), bf16)),
        [],
        "choose",
    )
    shaped = chosen.reshape(held_patches * FRAME_PATCH, tile_w, tile_h, width)
    return shaped.transpose(0, 2, 1, 3)


def solution(mesh):
    in_specs = (
        P(None, "th", "tw", None),
        P(),
        P("th", "tw", None),
        P("segment", None, None),
        P("segment", None, None),
        P("segment", None, None),
    )
    out_specs = P("segment", "th", "tw", None)
    return jax.shard_map(
        on_device, mesh=mesh, in_specs=in_specs, out_specs=out_specs, check_vma=False
    )
```

```python
import functools
import math

import jax
import jax.numpy as jnp
import numpy as np
from jax import lax
from jax.experimental import pallas as pl
from jax.experimental.pallas import tpu as pltpu
from jax.sharding import PartitionSpec as P

HEAD = 128
HALO = 1
FRAME_PATCH = 4
CHUNK = 512
VMEM_BYTES = 10 * 2**20
AXES = ("segment", "th", "tw")
SEG, ROW, COL = range(3)


def head_norm(values):
    mean_square = jnp.mean(values * values, axis=-1, keepdims=True)
    return values * lax.rsqrt(mean_square + 1e-06)


def is_active(place, live):
    return functools.reduce(jnp.logical_or, [place[SEG] == s for s in live])


def neighbour_rows(place, n_th, tile_h):
    below_first = place[ROW] % 2 == 0 if n_th % 2 == 0 else place[ROW] < 0
    row_a = jnp.where(below_first, tile_h, -1)
    row_b = jnp.where(below_first, -1, tile_h)
    valid = []
    for row in (row_a, row_b):
        tile = place[ROW] + jnp.where(row < 0, -1, 1)
        valid.append((tile >= 0) & (tile < n_th))
    return row_a, row_b, valid


def write_masks(spec, place, patterns, tables, outs):
    sides, tile_h, tile_w, n_th, n_tw = spec
    row_a, row_b, _ = neighbour_rows(place, n_th, tile_h)
    lane = place[COL] % sides
    for table, out in zip(tables, outs):
        side, kind = table[0:1, :], table[1:2, :]
        col, row = table[2:3, :], table[3:4, :]
        row = jnp.where(kind == 1, row_a, jnp.where(kind == 2, row_b, row))
        for query_side in range(sides):
            spot = lane if query_side == 0 else 1 - lane
            tile_col = place[COL] - lane + spot
            cols = (side - query_side) * (1 - 2 * lane) * tile_w + col
            cols = jnp.where(kind == 3, -1 - spot * tile_w, cols)
            cols = jnp.where(kind == 4, (sides - spot) * tile_w, cols)
            block = (
                ((row >= 0).astype(jnp.int32) + (row >= tile_h).astype(jnp.int32)) * 3
                + (cols >= 0).astype(jnp.int32)
                + (cols >= tile_w).astype(jnp.int32)
            )
            flag = jnp.zeros(block.shape, jnp.int32)
            for index in range(9):
                flag = jnp.where(block == index, patterns[query_side][0, index], flag)
            grid_row, grid_col = row + place[ROW] * tile_h, cols + tile_col * tile_w
            inside = (grid_row >= 0) & (grid_row < n_th * tile_h)
            inside &= (grid_col >= 0) & (grid_col < n_tw * tile_w)
            inside &= (cols >= -HALO) & (cols < tile_w + HALO)
            out[query_side : query_side + 1, :] = jnp.where(inside, flag, 0).astype(jnp.float32)


def key_value_kernel(live, spec, sources, masks, place, *refs):
    sides, tile_h, _, n_th, _ = spec
    count = sum(pieces for _, pieces in sources)
    parts, (mod, weight), refs = refs[:count], refs[count : count + 2], refs[count + 2 :]
    if masks:
        patterns, tables, refs = refs[:sides], refs[sides : sides + 2], refs[sides + 2 :]
        write_masks(spec, place, patterns, tables, refs[5:7])
    x_out, modded, kv, send_a, send_b = refs[:5]
    wide = refs[-1]
    inner = kv.shape[1] // 2
    tile_rows = kv.shape[0] // sides
    edges = kv.shape[0] // tile_h

    @pl.when(is_active(place, live))
    def _():
        for side in range(sides):
            rows = pl.ds(side * tile_rows, tile_rows)
            value, first = None, 0
            for holders, pieces in sources:
                part = parts[first + side][...] if pieces == sides else parts[first][rows, :]
                part = part.astype(jnp.float32).reshape(tile_rows, part.shape[-1])
                value = part if value is None else jnp.where(is_active(place, holders), part, value)
                first += pieces
            x_out[rows, :] = value.astype(jnp.bfloat16)
            centred = value - jnp.mean(value, axis=-1, keepdims=True)
            variance = jnp.mean(centred * centred, axis=-1, keepdims=True)
            normed = centred * lax.rsqrt(variance + 1e-06)
            modded[rows, :] = (normed * (1.0 + mod[1:2, :]) + mod[0:1, :]).astype(jnp.bfloat16)
        row_a, row_b, _ = neighbour_rows(place, n_th, tile_h)
        offset_a = jnp.where(row_a < 0, 0, tile_h - 1)
        offset_b = jnp.where(row_b < 0, 0, tile_h - 1)
        if n_th % 2:
            offset_a, offset_b = offset_b, offset_a
        for start in range(0, 2 * inner, CHUNK):
            projected = jnp.dot(
                modded[...], weight[:, start : start + CHUNK], preferred_element_type=jnp.float32
            )
            for low in range(0, CHUNK, HEAD):
                columns = pl.ds(start + low, HEAD)
                head = projected[:, low : low + HEAD]
                if start < inner:
                    head = head_norm(head)
                kv[:, columns] = head.astype(jnp.bfloat16)
                slot = wide.at[(start + low) // HEAD % wide.shape[0]]
                slot[...] = head
                send_a[:, columns] = slot[pl.ds(offset_a, edges, stride=tile_h), :].astype(
                    jnp.bfloat16
                )
                send_b[:, columns] = slot[pl.ds(offset_b, edges, stride=tile_h), :].astype(
                    jnp.bfloat16
                )


def masked(mask_ref, sides, tile_rows):
    keys = mask_ref.shape[1]
    return jnp.concatenate(
        [jnp.broadcast_to(mask_ref[s : s + 1, :], (tile_rows, keys)) for s in range(sides)], axis=0
    )


def weigh(queries, keys, values, mask):
    scores = [
        lax.dot_general(query, key, (((1,), (1,)), ((), ())), preferred_element_type=jnp.float32)
        for query, key in zip(queries, keys)
    ]
    weights = [
        (jnp.exp(score * (1.0 / math.sqrt(HEAD))) * mask).astype(jnp.bfloat16) for score in scores
    ]
    ones = jnp.ones((values[0].shape[0], HEAD), jnp.bfloat16)
    both = [
        jnp.dot(w, jnp.concatenate([v, ones], axis=1), preferred_element_type=jnp.float32)
        for w, v in zip(weights, values)
    ]
    return [b[:, :HEAD] for b in both], [b[:, HEAD:] for b in both]


def query_kernel(live, spec, place, modded, weight, kv, mask_ref, queries, top, bottom):
    sides = spec[0]
    tile_rows, inner = queries.shape[0] // sides, queries.shape[1]

    @pl.when(is_active(place, live))
    def _():
        mask = masked(mask_ref, sides, tile_rows)
        for start in range(0, inner, CHUNK):
            projected = jnp.dot(
                modded[...], weight[:, start : start + CHUNK], preferred_element_type=jnp.float32
            )
            heads = [pl.ds(start + low, HEAD) for low in range(0, CHUNK, HEAD)]
            found = []
            for index, columns in enumerate(heads):
                head = projected[:, index * HEAD : (index + 1) * HEAD]
                found.append(head_norm(head).astype(jnp.bfloat16))
                queries[:, columns] = found[-1]
            above, below = weigh(
                found,
                [kv[:, columns] for columns in heads],
                [kv[:, pl.ds(inner + columns.start, HEAD)] for columns in heads],
                mask,
            )
            for index, columns in enumerate(heads):
                top[:, columns] = above[index]
                bottom[:, columns] = below[index]


def output_kernel(live, spec, extra_count, place, *refs):
    extras, refs = refs[:extra_count], refs[extra_count:]
    (queries, top, bottom, mask_ref, x, mod, weight), outs = refs[:7], refs[7:-1]
    attended = refs[-1]
    sides, tile_h, _, n_th, _ = spec
    inner, width = weight.shape
    tile_rows = queries.shape[0] // sides

    @pl.when(is_active(place, live))
    def _():
        mask = masked(mask_ref, sides, tile_rows)
        valid = neighbour_rows(place, n_th, tile_h)[2]

        def received(columns):
            pieces = []
            for index, extra in enumerate(extras):
                piece = extra[:, columns]
                if index < 2:
                    piece = jnp.where(valid[index], piece, jnp.zeros_like(piece))
                pieces.append(piece)
            return jnp.concatenate(pieces, axis=0)

        for start in range(0, inner, CHUNK):
            heads = [pl.ds(start + low, HEAD) for low in range(0, CHUNK, HEAD)]
            above, below = weigh(
                [queries[:, columns] for columns in heads],
                [received(columns) for columns in heads],
                [received(pl.ds(inner + columns.start, HEAD)) for columns in heads],
                mask,
            )
            for index, columns in enumerate(heads):
                total = (top[:, columns] + above[index]) / (bottom[:, columns] + below[index])
                attended[:, columns] = total.astype(jnp.bfloat16)
        for start in range(0, width, CHUNK):
            columns = pl.ds(start, CHUNK)
            projected = jnp.dot(
                attended[...], weight[:, start : start + CHUNK], preferred_element_type=jnp.float32
            )
            updated = x[:, columns].astype(jnp.float32) + mod[2:3, start : start + CHUNK] * projected
            updated = updated.astype(jnp.bfloat16)
            for index, y in enumerate(outs):
                y[:, columns] = updated[index * y.shape[0] : (index + 1) * y.shape[0]]


def choose_kernel(wanted, place, *refs):
    pieces, out = refs[:-1], refs[-1]
    rows = out.shape[0] // len(wanted)
    for index, options in enumerate(wanted):
        for segment, lane, sides, source in options:

            @pl.when((place[SEG] == segment) & (place[COL] % sides == lane))
            def _(index=index, source=source):
                value = pieces[source][...].astype(jnp.float32).reshape(rows, *out.shape[1:])
                out[index * rows : (index + 1) * rows] = value.astype(jnp.bfloat16)


def gather_copies(place, order, tokens, outs, wanted, sides, sems):
    copies = []
    for slot, (out, (base, other)) in enumerate(zip(outs, wanted)):
        patch = base + (place[COL] + other) % sides
        rows = out.shape[0] // FRAME_PATCH
        for frame in range(FRAME_PATCH):
            source = order[patch * FRAME_PATCH + frame]
            copies.append(
                pltpu.make_async_copy(
                    tokens.at[pl.ds(source * rows, rows)],
                    out.at[pl.ds(frame * rows, rows)],
                    sems.at[slot, frame],
                )
            )
    for copy in copies:
        copy.start()
    return copies


def gather_kernel(wanted, sides, place, order, tokens, *refs):
    for copy in gather_copies(place, order, tokens, refs[:-1], wanted, sides, refs[-1]):
        copy.wait()


def load_kernel(wanted, sides, place, order, tokens, qkv, kv_out, q_out, *refs):
    outs, frame_sems, sems = refs[:-2], refs[-2], refs[-1]
    inner = q_out.shape[1]
    copies = gather_copies(place, order, tokens, outs, wanted, sides, frame_sems)
    copies += [
        pltpu.make_async_copy(qkv.at[:, pl.ds(inner, 2 * inner)], kv_out, sems.at[0]),
        pltpu.make_async_copy(qkv.at[:, pl.ds(0, inner)], q_out, sems.at[1]),
    ]
    for copy in copies[-2:]:
        copy.start()
    for copy in copies:
        copy.wait()


def run(
    kernel, scalars, operands, outs, scratch, name, memory=pltpu.VMEM, limit=VMEM_BYTES, after=()
):
    vmem, smem = pl.BlockSpec(memory_space=pltpu.VMEM), pl.BlockSpec(memory_space=pltpu.SMEM)
    if memory is pltpu.HBM:
        operands = [pltpu.with_memory_space_constraint(o, memory) for o in operands]
    skipped = len(after)
    in_specs = [pl.BlockSpec(memory_space=pl.ANY)] * skipped + [smem] * len(scalars)
    for operand in operands:
        small = operand.dtype == jnp.int32 and operand.shape[-1] == 9
        in_specs.append(smem if small else pl.BlockSpec(memory_space=memory))
    return pl.pallas_call(
        lambda *refs: kernel(*refs[skipped:]),
        out_shape=outs,
        in_specs=in_specs,
        out_specs=jax.tree.map(lambda _: vmem, outs),
        scratch_shapes=scratch,
        compiler_params=pltpu.CompilerParams(vmem_limit_bytes=limit),
        cost_estimate=pl.CostEstimate(flops=2**20, bytes_accessed=2**10, transcendentals=0),
        name=name,
    )(*after, *scalars, *operands)


def arrays(*shapes):
    return tuple(jax.ShapeDtypeStruct(shape, dtype) for shape, dtype in shapes)


def exchange(value, partner):
    sizes = [lax.axis_size(axis) for axis in AXES]
    places = [(s, t, w) for s in range(sizes[0]) for t in range(sizes[1]) for w in range(sizes[2])]
    number = {place: index for index, place in enumerate(places)}
    links = [(number[p], number[partner(*p)]) for p in places if partner(*p) in number]
    return lax.ppermute(value, AXES, links)


def on_device(tokens, frame_order, tile_pattern, qkv_weight, out_weight, modulation):
    n_seg, n_th, n_tw = [lax.axis_size(axis) for axis in AXES]
    seg, row_tile, col_tile = [lax.axis_index(axis) for axis in AXES]
    frames, tile_h, tile_w, width = tokens.shape
    inner = out_weight.shape[1]
    patches = frames // FRAME_PATCH
    held_patches = patches // n_seg
    sides = 2 if n_tw % 2 == 0 and patches % 2 == 0 else 1
    rounds = patches // sides
    tile_rows = FRAME_PATCH * tile_h * tile_w
    edge_rows = FRAME_PATCH * tile_w
    strip_rows = sides * tile_rows

    lane = col_tile % sides
    bf16, f32 = jnp.bfloat16, jnp.float32

    def beside(w):
        return w + 1 - 2 * (w % 2)

    def patch_base(turn):
        return (rounds - 1 - turn) * sides

    def token_swap(s, t, w):
        if s == n_seg - 1:
            return (s, t, beside(w))
        return (s, t + 1 - 2 * (t % 2), w) if n_th % 2 == 0 else None

    place = jnp.stack([seg, row_tile, col_tile]).astype(jnp.int32)
    stored = tokens.transpose(0, 2, 1, 3).reshape(frames * tile_w, tile_h, width)
    tile_shape = ((edge_rows, tile_h, width), bf16)
    theirs, pattern = [], tile_pattern[0]
    patterns = [pattern]
    if sides == 2:
        messages = run(
            functools.partial(gather_kernel, [(patch_base(turn), 1) for turn in range(rounds)], sides),
            [place, frame_order],
            [stored],
            arrays(*[tile_shape] * rounds),
            [pltpu.SemaphoreType.DMA((rounds, FRAME_PATCH))],
            "gather",
            pltpu.HBM,
            2**20,
        )
        theirs = [exchange(message, token_swap) for message in messages]
        patterns.append(exchange(pattern, lambda s, t, w: (s, t, beside(w))))
        messages, place, qkv_weight = lax.optimization_barrier((messages, place, qkv_weight))
    wanted = [(patch_base(turn), 0) for turn in range(rounds)]
    kv_w, q_w, *tiles = run(
        functools.partial(load_kernel, wanted, sides),
        [place, frame_order],
        [stored, qkv_weight[0]],
        (pltpu.VMEM((width, 2 * inner), bf16), pltpu.VMEM((width, inner), bf16))
        + arrays(*[tile_shape] * rounds),
        [pltpu.SemaphoreType.DMA((rounds, FRAME_PATCH)), pltpu.SemaphoreType.DMA((2,))],
        "load_weights",
        pltpu.HBM,
        2**20,
    )
    kv_w, q_w, out_w = [
        pltpu.with_memory_space_constraint(w, pltpu.VMEM) for w in (kv_w, q_w, out_weight[0])
    ]
    fresh = [[tiles[turn]] + ([theirs[turn]] if sides == 2 else []) for turn in range(rounds)]
    mod = modulation[0]

    side_halo = n_tw > sides
    grid = np.indices((sides, FRAME_PATCH, tile_w, tile_h)).reshape(4, -1)
    own_table = np.stack([grid[0], 0 * grid[0], grid[2], grid[3]])
    strip_edge = np.indices((sides, FRAME_PATCH, tile_w)).reshape(3, -1)
    extra = [
        np.stack([strip_edge[0], 0 * strip_edge[0] + kind, strip_edge[2], 0 * strip_edge[0]])
        for kind in (1, 2)
    ]
    if side_halo:
        tall = np.tile(np.arange(-HALO, tile_h + HALO), FRAME_PATCH)
        extra += [np.stack([0 * tall, 0 * tall + kind, 0 * tall, tall]) for kind in (3, 4)]
    tables = [jnp.asarray(t, jnp.int32) for t in (own_table, np.concatenate(extra, axis=1))]

    first = {n_seg - 1: 0}
    for s in range(n_seg - 1, 0, -1):
        first[s - 1] = first[s] + (1 if s % 2 else 2)
    steps = first[0] + rounds
    spec = (sides, tile_h, tile_w, n_th, n_tw)
    paired_rows, paired_segs = n_th % 2 == 0, n_seg % 2 == 0

    def running(step):
        return [s for s in range(n_seg) if 0 <= step - first[s] < rounds]

    def sources_of(step):
        live = running(step)
        found = []
        if n_seg - 1 in live:
            found.append(("fresh", [n_seg - 1]))
        near_to = [s for s in live if s % 2 == 0 and s != n_seg - 1]
        far_to = [s for s in live if s % 2 == 1 and s != n_seg - 1]
        return found + [("near", near_to)] * bool(near_to) + [("far", far_to)] * bool(far_to)

    def spare(live, s, t, w):
        if paired_segs and s ^ 1 not in live:
            return (s ^ 1, t, w)
        return (s, t, beside(w)) if n_tw % 2 == 0 else None

    def rows_a(live):
        def partner(s, t, w):
            if not paired_rows:
                return (s, t + 1, w)
            return (s, t + 1 - 2 * (t % 2), w) if s in live else spare(live, s, t, w)

        return partner

    def rows_b(live):
        def partner(s, t, w):
            other = t - 1 + 2 * (t % 2) if paired_rows else t - 1
            if paired_rows and not 0 <= other < n_th:
                return (s ^ 1, t, w) if paired_segs else None
            return (s, other, w) if s in live or not paired_rows else spare(live, s, t, w)

        return partner

    def near_hop(s, t, w):
        return (s ^ 1, t, w) if paired_segs else (s - 1, t, w) if s % 2 else None

    def far_hop(s, t, w):
        return (s - 1, t, w) if s % 2 == 0 and s > 0 else None

    def edge_column(kv, above, below, which):
        body = kv.reshape(sides, FRAME_PATCH, tile_w, tile_h, 2 * inner)
        ends = [part.reshape(sides, FRAME_PATCH, tile_w, 1, 2 * inner) for part in (above, below)]
        tall = jnp.concatenate([ends[0], body, ends[1]], axis=3)
        if which == 0:
            column = jnp.where(lane == 0, tall[0, :, 0], tall[sides - 1, :, 0])
        else:
            column = jnp.where(lane == 0, tall[sides - 1, :, -1], tall[0, :, -1])
        return column.reshape(-1, 2 * inner)

    masks = []

    def layer(step, live, sources, before):
        operands = [part for _, source in sources for part in source]
        counts = [(holders, len(source)) for holders, source in sources]
        strip = strip_rows
        outs = [
            ((strip, width), bf16),
            ((strip, width), bf16),
            ((strip, 2 * inner), bf16),
            ((sides * edge_rows, 2 * inner), bf16),
            ((sides * edge_rows, 2 * inner), bf16),
        ]
        operands += [mod, kv_w]
        if step == 0:
            operands += patterns + tables
            outs += [((sides, table.shape[1]), f32) for table in tables]
        x, modded, kv, send_a, send_b, *made = run(
            functools.partial(key_value_kernel, live, spec, counts, step == 0),
            [place],
            operands,
            arrays(*outs),
            [pltpu.VMEM((4, strip, HEAD), f32)],
            "key_value",
            after=before,
        )
        masks.extend(made)
        own_mask, extra_mask = masks
        extra_a = exchange(send_a, rows_a(live))
        extra_b = exchange(send_b, rows_b(live))
        queries, top, bottom = run(
            functools.partial(query_kernel, live, spec),
            [place],
            [modded, q_w, kv, own_mask],
            arrays(((strip, inner), bf16), ((strip, inner), f32), ((strip, inner), f32)),
            [],
            "query",
        )
        extras = [extra_a, extra_b]
        if side_halo:
            flip = (row_tile % 2 == 1) if paired_rows else jnp.array(True)
            above = jnp.where(flip, extra_a, extra_b)
            below = jnp.where(flip, extra_b, extra_a)
            above = jnp.where(row_tile > 0, above, jnp.zeros_like(above))
            below = jnp.where(row_tile < n_th - 1, below, jnp.zeros_like(below))
            left = edge_column(kv, above, below, 0)
            right = edge_column(kv, above, below, 1)
            from_left = exchange(right, lambda s, t, w: (s, t, w + sides))
            from_right = exchange(left, lambda s, t, w: (s, t, w - sides))
            extras.append(jnp.concatenate([from_left, from_right], axis=0))
        last = 0 in live
        out_shapes = [((tile_rows, width), bf16)] * sides if last else [((strip_rows, width), bf16)]
        return run(
            functools.partial(output_kernel, live, spec, len(extras)),
            [place],
            extras + [queries, top, bottom, extra_mask, x, mod, out_w],
            arrays(*out_shapes),
            [pltpu.VMEM((strip_rows, inner), bf16)],
            "output",
            after=[turn[-1] for turn in fresh[1:]] if step == 0 and sides == 2 else (),
        )

    def owner_of(turn, w):
        return (patch_base(turn) + w % sides) // held_patches

    near = far = far_next = None
    finished = {}
    y = ()
    for step in range(steps):
        live = running(step)
        options = {"near": near, "far": [far]}
        if step < rounds:
            options["fresh"] = fresh[step]
        found = [(holders, options[kind]) for kind, holders in sources_of(step)]
        y = layer(step, live, found, y)
        near, far, far_next = None, far_next, None
        if any(s % 2 == 1 for s in live):
            near = [exchange(part, near_hop) for part in y]
        if any(s % 2 == 0 and s > 0 for s in live):
            far_next = exchange(y[0], far_hop)
        if 0 in live:
            turn = step - first[0]
            finished[turn] = [
                exchange(
                    part,
                    lambda s, t, w: (owner_of(turn, w), t, beside(w) if side else w)
                    if s == 0
                    else None,
                )
                for side, part in enumerate(y)
            ]
    wanted = []
    for held in range(held_patches):
        options = []
        for owner in range(n_seg):
            patch = owner * held_patches + held
            turn, member = rounds - 1 - patch // sides, patch % sides
            for w in range(sides):
                options.append((owner, w, sides, turn * sides + (0 if w == member else 1)))
        wanted.append(options)
    (chosen,) = run(
        functools.partial(choose_kernel, wanted),
        [place],
        [piece for turn in range(rounds) for piece in finished[turn]],
        arrays(((held_patches * edge_rows, tile_h, width), bf16)),
        [],
        "choose",
    )
    shaped = chosen.reshape(held_patches * FRAME_PATCH, tile_w, tile_h, width)
    return shaped.transpose(0, 2, 1, 3)


def solution(mesh):
    in_specs = (
        P(None, "th", "tw", None),
        P(),
        P("th", "tw", None),
        P("segment", None, None),
        P("segment", None, None),
        P("segment", None, None),
    )
    out_specs = P("segment", "th", "tw", None)
    return jax.shard_map(
        on_device, mesh=mesh, in_specs=in_specs, out_specs=out_specs, check_vma=False
    )
```

```python
import functools
import math

import jax
import jax.numpy as jnp
import numpy as np
from jax import lax
from jax.experimental import pallas as pl
from jax.experimental.pallas import tpu as pltpu
from jax.sharding import PartitionSpec as P

HEAD = 128
HALO = 1
FRAME_PATCH = 4
CHUNK = 512
BLOCK = 16
GROUP = 12
VMEM_BYTES = 10 * 2**20
AXES = ("segment", "th", "tw")
SEG, ROW, COL = range(3)


def head_norm(values):
    mean_square = jnp.mean(values * values, axis=-1, keepdims=True)
    return values * lax.rsqrt(mean_square + 1e-06)


def is_active(place, live):
    return functools.reduce(jnp.logical_or, [place[SEG] == s for s in live])


def neighbour_rows(place, n_th, tile_h):
    below_first = place[ROW] % 2 == 0 if n_th % 2 == 0 else place[ROW] < 0
    row_a = jnp.where(below_first, tile_h, -1)
    row_b = jnp.where(below_first, -1, tile_h)
    valid = []
    for row in (row_a, row_b):
        tile = place[ROW] + jnp.where(row < 0, -1, 1)
        valid.append((tile >= 0) & (tile < n_th))
    return row_a, row_b, valid


def write_masks(spec, place, patterns, tables, outs):
    sides, tile_h, tile_w, n_th, n_tw = spec
    row_a, row_b, _ = neighbour_rows(place, n_th, tile_h)
    lane = place[COL] % sides
    for table, out in zip(tables, outs):
        side, kind = table[0:1, :], table[1:2, :]
        col, row = table[2:3, :], table[3:4, :]
        row = jnp.where(kind == 1, row_a, jnp.where(kind == 2, row_b, row))
        for query_side in range(sides):
            spot = lane if query_side == 0 else 1 - lane
            tile_col = place[COL] - lane + spot
            cols = (side - query_side) * (1 - 2 * lane) * tile_w + col
            cols = jnp.where(kind == 3, -1 - spot * tile_w, cols)
            cols = jnp.where(kind == 4, (sides - spot) * tile_w, cols)
            block = (
                ((row >= 0).astype(jnp.int32) + (row >= tile_h).astype(jnp.int32)) * 3
                + (cols >= 0).astype(jnp.int32)
                + (cols >= tile_w).astype(jnp.int32)
            )
            flag = jnp.zeros(block.shape, jnp.float32)
            for index in range(9):
                pattern = patterns[query_side]
                if len(pattern.shape) == 3:
                    last = pattern.shape[0] - 1
                    value = pattern[last, 0:1, index : index + 1].astype(jnp.float32)
                else:
                    value = pattern[0, index].astype(jnp.float32)
                flag = jnp.where(block == index, value, flag)
            grid_row, grid_col = row + place[ROW] * tile_h, cols + tile_col * tile_w
            inside = (grid_row >= 0) & (grid_row < n_th * tile_h)
            inside &= (grid_col >= 0) & (grid_col < n_tw * tile_w)
            inside &= (cols >= -HALO) & (cols < tile_w + HALO)
            out[query_side : query_side + 1, :] = jnp.where(inside, flag, 0.0)


def key_value_kernel(live, spec, sources, place, *refs):
    sides, tile_h, _, n_th, _ = spec
    count = sum(pieces for _, pieces in sources)
    parts, (mod, weight), refs = refs[:count], refs[count : count + 2], refs[count + 2 :]
    x_out, modded, kv, send_a, send_b = refs[:5]
    wide = refs[-1]
    inner = kv.shape[1] // 2
    tile_rows = kv.shape[0] // sides
    edges = kv.shape[0] // tile_h

    @pl.when(is_active(place, live))
    def _():
        gain, shift = 1.0 + mod[1:2, :], mod[0:1, :]
        for start in range(0, sides * tile_rows, BLOCK):
            rows = slice(start, start + BLOCK)
            side, within = start // tile_rows, start % tile_rows
            value, first = None, 0
            for holders, pieces in sources:
                if pieces < sides:
                    part = parts[first][rows, :]
                elif len(parts[first].shape) == 3:
                    part = parts[first + side][within // tile_h : (within + BLOCK) // tile_h]
                else:
                    part = parts[first + side][within : within + BLOCK, :]
                part = part.astype(jnp.float32).reshape(BLOCK, part.shape[-1])
                value = part if value is None else jnp.where(is_active(place, holders), part, value)
                first += pieces
            x_out[rows, :] = value.astype(jnp.bfloat16)
            centred = value - jnp.mean(value, axis=-1, keepdims=True)
            variance = jnp.mean(centred * centred, axis=-1, keepdims=True)
            normed = centred * lax.rsqrt(variance + 1e-06)
            modded[rows, :] = (normed * gain + shift).astype(jnp.bfloat16)
        row_a, row_b, _ = neighbour_rows(place, n_th, tile_h)
        offset_a = jnp.where(row_a < 0, 0, tile_h - 1)
        offset_b = jnp.where(row_b < 0, 0, tile_h - 1)
        if n_th % 2:
            offset_a, offset_b = offset_b, offset_a
        for start in range(0, 2 * inner, CHUNK):
            projected = jnp.dot(
                modded[...], weight[:, start : start + CHUNK], preferred_element_type=jnp.float32
            )
            for low in range(0, CHUNK, HEAD):
                columns = pl.ds(start + low, HEAD)
                head = projected[:, low : low + HEAD]
                if start < inner:
                    head = head_norm(head)
                kv[:, columns] = head.astype(jnp.bfloat16)
                slot = wide.at[(start + low) // HEAD % wide.shape[0]]
                slot[...] = head
                send_a[:, columns] = slot[pl.ds(offset_a, edges, stride=tile_h), :].astype(
                    jnp.bfloat16
                )
                send_b[:, columns] = slot[pl.ds(offset_b, edges, stride=tile_h), :].astype(
                    jnp.bfloat16
                )


def masked(mask_ref, chosen, tile_rows):
    keys = mask_ref.shape[1]
    return jnp.concatenate(
        [jnp.broadcast_to(mask_ref[s : s + 1, :], (tile_rows, keys)) for s in chosen], axis=0
    )


def weigh(queries, keys, values, mask):
    scores = [
        lax.dot_general(query, key, (((1,), (1,)), ((), ())), preferred_element_type=jnp.float32)
        for query, key in zip(queries, keys)
    ]
    weights = [
        (jnp.exp2(score * (1.0 / (math.sqrt(HEAD) * math.log(2.0)))) * mask).astype(jnp.bfloat16) for score in scores
    ]
    ones = jnp.ones((values[0].shape[0], HEAD), jnp.bfloat16)
    both = [
        jnp.dot(w, jnp.concatenate([v, ones], axis=1), preferred_element_type=jnp.float32)
        for w, v in zip(weights, values)
    ]
    return [b[:, :HEAD] for b in both], [b[:, HEAD:] for b in both]


def groups(inner):
    heads = [pl.ds(low, HEAD) for low in range(0, inner, HEAD)]
    return [heads[low : low + GROUP] for low in range(0, len(heads), GROUP)]


def first_key_value_kernel(live, spec, sources, place, qkv, *refs):
    loaded, wide, sem = refs[-3:]
    width = loaded.shape[1]
    copy = pltpu.make_async_copy(qkv.at[:, pl.ds(0, width)], loaded, sem.at[0])
    copy.start()
    key_value_kernel(live, spec, sources, place, *refs[:-3], wide)
    copy.wait()


def first_query_kernel(live, spec, place, modded, weight, kv, *refs):
    sides = spec[0]
    patterns, tables, out_weight = refs[:sides], refs[sides : sides + 2], refs[sides + 2]
    queries, top, bottom, own_mask, extra_mask, loaded, sem = refs[sides + 3 :]
    copy = pltpu.make_async_copy(out_weight, loaded, sem.at[0])
    copy.start()
    write_masks(spec, place, patterns, tables, (own_mask, extra_mask))
    query_kernel(live, spec, place, modded, weight, kv, own_mask, queries, top, bottom)
    copy.wait()


def second_query_kernel(live, spec, place, modded, weight, kv, *refs):
    sides = spec[0]
    patterns, tables, refs = refs[:sides], refs[sides : sides + 2], refs[sides + 2 :]
    queries, top, bottom, own_mask, extra_mask = refs
    write_masks(spec, place, patterns, tables, (own_mask, extra_mask))
    query_kernel(live, spec, place, modded, weight, kv, own_mask, queries, top, bottom)


def query_kernel(live, spec, place, modded, weight, kv, mask_ref, queries, top, bottom):
    sides = spec[0]
    tile_rows, inner = queries.shape[0] // sides, queries.shape[1]

    @pl.when(is_active(place, live))
    def _():
        mask = masked(mask_ref, range(sides), tile_rows)
        found = []
        for start in range(0, inner, CHUNK):
            projected = jnp.dot(
                modded[...], weight[:, start : start + CHUNK], preferred_element_type=jnp.float32
            )
            for low in range(0, CHUNK, HEAD):
                query = head_norm(projected[:, low : low + HEAD]).astype(jnp.bfloat16)
                found.append(query)
                queries[:, start + low : start + low + HEAD] = query
        for group in groups(inner):
            above, below = weigh(
                [found[columns.start // HEAD] for columns in group],
                [kv[:, columns] for columns in group],
                [kv[:, pl.ds(inner + columns.start, HEAD)] for columns in group],
                mask,
            )
            for index, columns in enumerate(group):
                top[:, columns] = above[index]
                bottom[:, columns] = below[index]


def output_kernel(live, spec, extra_count, chosen, place, *refs):
    extras, refs = refs[:extra_count], refs[extra_count:]
    (queries, top, bottom, mask_ref, x, mod, weight), outs = refs[:7], refs[7:-1]
    attended = refs[-1]
    sides, tile_h, _, n_th, _ = spec
    inner, width = weight.shape
    tile_rows = queries.shape[0] // sides
    rows = slice(chosen[0] * tile_rows, (chosen[-1] + 1) * tile_rows)

    @pl.when(is_active(place, live))
    def _():
        mask = masked(mask_ref, chosen, tile_rows)
        valid = neighbour_rows(place, n_th, tile_h)[2]

        def received(columns):
            pieces = []
            for index, extra in enumerate(extras):
                piece = extra[:, columns]
                if index < 2:
                    piece = jnp.where(valid[index], piece, jnp.zeros_like(piece))
                pieces.append(piece)
            return jnp.concatenate(pieces, axis=0)

        for heads in groups(inner):
            above, below = weigh(
                [queries[rows, columns] for columns in heads],
                [received(columns) for columns in heads],
                [received(pl.ds(inner + columns.start, HEAD)) for columns in heads],
                mask,
            )
            for index, columns in enumerate(heads):
                total = (top[rows, columns] + above[index]) / (bottom[rows, columns] + below[index])
                attended[:, columns] = total.astype(jnp.bfloat16)
        for start in range(0, width, CHUNK):
            columns = pl.ds(start, CHUNK)
            projected = jnp.dot(
                attended[...], weight[:, start : start + CHUNK], preferred_element_type=jnp.float32
            )
            updated = x[rows, columns].astype(jnp.float32)
            updated += mod[2:3, start : start + CHUNK] * projected
            if len(outs[0].shape) == 2:
                outs[0][:, columns] = updated.astype(jnp.bfloat16)
                continue
            for index, y in enumerate(outs):
                tile = updated[index * tile_rows : (index + 1) * tile_rows]
                y[:, :, columns] = tile.reshape(*y.shape[:2], CHUNK).astype(jnp.bfloat16)


def choose_kernel(wanted, place, *refs):
    pieces, out, sem = refs[:-2], refs[-2], refs[-1]
    rows = out.shape[0] // len(wanted)
    for index, options in enumerate(wanted):
        for segment, lane, sides, source in options:

            @pl.when((place[SEG] == segment) & (place[COL] % sides == lane))
            def _(index=index, source=source):
                copy = pltpu.make_async_copy(
                    pieces[source], out.at[pl.ds(index * rows, rows)], sem.at[0]
                )
                copy.start()
                copy.wait()


def gather_copies(place, order, tokens, outs, wanted, sides, sems):
    copies = []
    for slot, (out, (base, other)) in enumerate(zip(outs, wanted)):
        patch = base + (place[COL] + other) % sides
        rows = out.shape[0] // FRAME_PATCH
        for frame in range(FRAME_PATCH):
            source = order[patch * FRAME_PATCH + frame]
            copies.append(
                pltpu.make_async_copy(
                    tokens.at[pl.ds(source * rows, rows)],
                    out.at[pl.ds(frame * rows, rows)],
                    sems.at[slot, frame],
                )
            )
    for copy in copies:
        copy.start()
    return copies


def gather_kernel(wanted, sides, place, order, tokens, pattern, *refs):
    outs = refs[:-1]
    copies = gather_copies(place, order, tokens, outs, wanted, sides, refs[-1])
    shape = (1,) + outs[0].shape[1:]
    lanes = lax.broadcasted_iota(jnp.int32, shape, 2)
    block = jnp.zeros(shape, jnp.float32)
    for index in range(9):
        block = jnp.where(lanes == index, pattern[0, index].astype(jnp.float32), block)
    for out in outs:
        out[out.shape[0] - 1 :] = block.astype(jnp.bfloat16)
    for copy in copies:
        copy.wait()


def load_kernel(wanted, sides, place, order, tokens, qkv, loaded, *refs):
    outs, frame_sems, sem = refs[:-2], refs[-2], refs[-1]
    columns = loaded.shape[1]
    copy = pltpu.make_async_copy(qkv.at[:, pl.ds(columns // 2, columns)], loaded, sem.at[0])
    copy.start()
    for frame in gather_copies(place, order, tokens, outs, wanted, sides, frame_sems):
        frame.wait()
    copy.wait()


def run(
    kernel,
    scalars,
    operands,
    outs,
    scratch,
    name,
    memory=pltpu.VMEM,
    limit=VMEM_BYTES,
    after=(),
    out_memory=pltpu.VMEM,
    fixed=None,
):
    result, smem = pl.BlockSpec(memory_space=out_memory), pl.BlockSpec(memory_space=pltpu.SMEM)
    if memory is pltpu.HBM:
        operands = [
            o if o.dtype == jnp.int32 else pltpu.with_memory_space_constraint(o, memory)
            for o in operands
        ]
    skipped = len(after)
    in_specs = [pl.BlockSpec(memory_space=pl.ANY)] * skipped + [smem] * len(scalars)
    for operand in operands:
        small = operand.dtype == jnp.int32 and operand.shape[-1] == 9
        large = operand is fixed
        spec = pl.BlockSpec(memory_space=pltpu.HBM if large else memory)
        in_specs.append(smem if small else spec)
    return pl.pallas_call(
        lambda *refs: kernel(tuple(lax.axis_index(a) for a in AXES), *refs[skipped:]),
        out_shape=outs,
        in_specs=in_specs,
        out_specs=jax.tree.map(lambda _: result, outs),
        scratch_shapes=scratch,
        compiler_params=pltpu.CompilerParams(vmem_limit_bytes=limit),
        cost_estimate=pl.CostEstimate(flops=2**20, bytes_accessed=2**10, transcendentals=0),
        name=name,
    )(*after, *scalars, *operands)


def arrays(*shapes):
    return tuple(jax.ShapeDtypeStruct(shape, dtype) for shape, dtype in shapes)


def exchange(value, partner):
    sizes = [lax.axis_size(axis) for axis in AXES]
    places = [(s, t, w) for s in range(sizes[0]) for t in range(sizes[1]) for w in range(sizes[2])]
    number = {place: index for index, place in enumerate(places)}
    links = [(number[p], number[partner(*p)]) for p in places if partner(*p) in number]
    return lax.ppermute(value, AXES, links)


def on_device(tokens, frame_order, tile_pattern, qkv_weight, out_weight, modulation):
    n_seg, n_th, n_tw = [lax.axis_size(axis) for axis in AXES]
    seg, row_tile, col_tile = [lax.axis_index(axis) for axis in AXES]
    frames, tile_h, tile_w, width = tokens.shape
    inner = out_weight.shape[1]
    patches = frames // FRAME_PATCH
    held_patches = patches // n_seg
    sides = 2 if n_tw % 2 == 0 and patches % 2 == 0 else 1
    rounds = patches // sides
    tile_rows = FRAME_PATCH * tile_h * tile_w
    edge_rows = FRAME_PATCH * tile_w
    strip_rows = sides * tile_rows

    lane = col_tile % sides
    bf16, f32 = jnp.bfloat16, jnp.float32

    def beside(w):
        return w + 1 - 2 * (w % 2)

    def patch_base(turn):
        return (rounds - 1 - turn) * sides

    def token_swap(s, t, w):
        if s == n_seg - 1:
            return (s, t, beside(w))
        return (s, t + 1 - 2 * (t % 2), w) if n_th % 2 == 0 else None

    stored = tokens.transpose(0, 2, 1, 3).reshape(frames * tile_w, tile_h, width)
    tile_shape = ((edge_rows, tile_h, width), bf16)
    theirs, pattern = [], tile_pattern[0]
    patterns = [pattern]
    if sides == 2:
        messages = run(
            functools.partial(gather_kernel, [(patch_base(turn), 1) for turn in range(rounds)], sides),
            [frame_order],
            [stored, pattern],
            arrays(*[((edge_rows + 1, tile_h, width), bf16)] * rounds),
            [pltpu.SemaphoreType.DMA((rounds, FRAME_PATCH))],
            "gather",
            pltpu.HBM,
            2**20,
        )
        theirs = [exchange(message, token_swap) for message in messages]
        patterns.append(exchange(pattern, lambda s, t, w: (s, t, beside(w))))
        messages, qkv_weight = lax.optimization_barrier((messages, qkv_weight))
    wanted = [(patch_base(turn), 0) for turn in range(rounds)]
    kv_w, *tiles = run(
        functools.partial(load_kernel, wanted, sides),
        [frame_order],
        [stored, qkv_weight[0]],
        (pltpu.VMEM((width, 2 * inner), bf16),)
        + arrays(*[tile_shape] * rounds),
        [pltpu.SemaphoreType.DMA((rounds, FRAME_PATCH)), pltpu.SemaphoreType.DMA((1,))],
        "load_weights",
        pltpu.HBM,
        2**20,
    )
    kv_w = pltpu.with_memory_space_constraint(kv_w, pltpu.VMEM)
    fresh = [[tiles[turn]] + ([theirs[turn]] if sides == 2 else []) for turn in range(rounds)]
    stored_qkv, stored_out = [
        pltpu.with_memory_space_constraint(w[0], pltpu.HBM) for w in (qkv_weight, out_weight)
    ]
    mod = modulation[0]

    side_halo = n_tw > sides
    grid = np.indices((sides, FRAME_PATCH, tile_w, tile_h)).reshape(4, -1)
    own_table = np.stack([grid[0], 0 * grid[0], grid[2], grid[3]])
    strip_edge = np.indices((sides, FRAME_PATCH, tile_w)).reshape(3, -1)
    extra = [
        np.stack([strip_edge[0], 0 * strip_edge[0] + kind, strip_edge[2], 0 * strip_edge[0]])
        for kind in (1, 2)
    ]
    if side_halo:
        tall = np.tile(np.arange(-HALO, tile_h + HALO), FRAME_PATCH)
        extra += [np.stack([0 * tall, 0 * tall + kind, 0 * tall, tall]) for kind in (3, 4)]
    tables = [jnp.asarray(t, jnp.int32) for t in (own_table, np.concatenate(extra, axis=1))]

    first = {n_seg - 1: 0}
    for s in range(n_seg - 1, 0, -1):
        first[s - 1] = first[s] + (1 if s % 2 else 2)
    steps = first[0] + rounds
    spec = (sides, tile_h, tile_w, n_th, n_tw)
    paired_rows, paired_segs = n_th % 2 == 0, n_seg % 2 == 0

    def running(step):
        return [s for s in range(n_seg) if 0 <= step - first[s] < rounds]

    def sources_of(step):
        live = running(step)
        found = []
        if n_seg - 1 in live:
            found.append(("fresh", [n_seg - 1]))
        near_to = [s for s in live if s % 2 == 0 and s != n_seg - 1]
        far_to = [s for s in live if s % 2 == 1 and s != n_seg - 1]
        return found + [("near", near_to)] * bool(near_to) + [("far", far_to)] * bool(far_to)

    def spare(live, s, t, w):
        if paired_segs and s ^ 1 not in live:
            return (s ^ 1, t, w)
        return (s, t, beside(w)) if n_tw % 2 == 0 else None

    def rows_a(live):
        def partner(s, t, w):
            if not paired_rows:
                return (s, t + 1, w)
            return (s, t + 1 - 2 * (t % 2), w) if s in live else spare(live, s, t, w)

        return partner

    def rows_b(live):
        def partner(s, t, w):
            other = t - 1 + 2 * (t % 2) if paired_rows else t - 1
            if paired_rows and not 0 <= other < n_th:
                return (s ^ 1, t, w) if paired_segs else None
            if s in live or not paired_rows:
                return (s, other, w)
            if live == [n_seg - 1] and n_seg == 4:
                return (3 - s, t, w) if s in (1, 2) else (s, t, beside(w))
            return spare(live, s, t, w)

        return partner

    def near_hop(s, t, w):
        return (s ^ 1, t, w) if paired_segs else (s - 1, t, w) if s % 2 else None

    def far_hop(s, t, w):
        return (s - 1, t, w) if s % 2 == 0 and s > 0 else None

    def edge_column(kv, above, below, which):
        body = kv.reshape(sides, FRAME_PATCH, tile_w, tile_h, 2 * inner)
        ends = [part.reshape(sides, FRAME_PATCH, tile_w, 1, 2 * inner) for part in (above, below)]
        tall = jnp.concatenate([ends[0], body, ends[1]], axis=3)
        if which == 0:
            column = jnp.where(lane == 0, tall[0, :, 0], tall[sides - 1, :, 0])
        else:
            column = jnp.where(lane == 0, tall[sides - 1, :, -1], tall[0, :, -1])
        return column.reshape(-1, 2 * inner)

    kept = []

    def layer(step, live, sources, before):
        operands = [part for _, source in sources for part in source]
        counts = [(holders, len(source)) for holders, source in sources]
        strip = strip_rows
        outs = [
            ((strip, width), bf16),
            ((strip, width), bf16),
            ((strip, 2 * inner), bf16),
            ((sides * edge_rows, 2 * inner), bf16),
            ((sides * edge_rows, 2 * inner), bf16),
        ]
        operands += [mod, kv_w]
        wide = pltpu.VMEM((4, strip, HEAD), f32)
        if step == 0:
            x, modded, kv, send_a, send_b, q_w = run(
                functools.partial(first_key_value_kernel, live, spec, counts),
                [],
                [stored_qkv] + operands,
                arrays(*outs) + (pltpu.VMEM((width, inner), bf16),),
                [wide, pltpu.SemaphoreType.DMA((1,))],
                "key_value",
                fixed=stored_qkv,
            )
            kept.append(pltpu.with_memory_space_constraint(q_w, pltpu.VMEM))
        else:
            x, modded, kv, send_a, send_b = run(
                functools.partial(key_value_kernel, live, spec, counts),
                [],
                operands,
                arrays(*outs),
                [wide],
                "key_value",
                after=before,
            )
        extra_a = exchange(send_a, rows_a(live))
        extra_b = exchange(send_b, rows_b(live))
        outs = arrays(((strip, inner), bf16), ((strip, inner), f32), ((strip, inner), f32))
        if step == 0:
            made = arrays(*[((sides, table.shape[1]), f32) for table in tables])
            queries, top, bottom, own_mask, extra_mask, out_w = run(
                functools.partial(first_query_kernel, live, spec),
                [],
                [modded, kept[0], kv, pattern] + fresh[0][1:] + tables + [stored_out],
                outs + made + (pltpu.VMEM((inner, width), bf16),),
                [pltpu.SemaphoreType.DMA((1,))],
                "query",
                fixed=stored_out,
            )
            out_w = pltpu.with_memory_space_constraint(out_w, pltpu.VMEM)
            kept.extend([own_mask, extra_mask, out_w])
        elif step == 1:
            made = arrays(*[((sides, table.shape[1]), f32) for table in tables])
            queries, top, bottom, *kept[1:3] = run(
                functools.partial(second_query_kernel, live, spec),
                [],
                [modded, kept[0], kv] + patterns + tables,
                outs + made,
                [],
                "query",
            )
        else:
            queries, top, bottom = run(
                functools.partial(query_kernel, live, spec),
                [],
                [modded, kept[0], kv, kept[1]],
                outs,
                [],
                "query",
            )
        extra_mask, out_w = kept[2:]
        extras = [extra_a, extra_b]
        if side_halo:
            flip = (row_tile % 2 == 1) if paired_rows else jnp.array(True)
            above = jnp.where(flip, extra_a, extra_b)
            below = jnp.where(flip, extra_b, extra_a)
            above = jnp.where(row_tile > 0, above, jnp.zeros_like(above))
            below = jnp.where(row_tile < n_th - 1, below, jnp.zeros_like(below))
            left = edge_column(kv, above, below, 0)
            right = edge_column(kv, above, below, 1)
            from_left = exchange(right, lambda s, t, w: (s, t, w + sides))
            from_right = exchange(left, lambda s, t, w: (s, t, w - sides))
            extras.append(jnp.concatenate([from_left, from_right], axis=0))
        def finish(chosen, shapes):
            return run(
                functools.partial(output_kernel, live, spec, len(extras), chosen),
                [],
                extras + [queries, top, bottom, extra_mask, x, mod, out_w],
                arrays(*shapes),
                [pltpu.VMEM((len(chosen) * tile_rows, inner), bf16)],
                "output",
                after=[turn[-1] for turn in fresh[1:]] if step == 0 and sides == 2 else (),
            )

        last = 0 in live
        return finish(range(sides), [tile_shape] * sides if last else [((strip, width), bf16)])

    def owner_of(turn, w):
        return (patch_base(turn) + w % sides) // held_patches

    near = far = far_next = None
    finished = {}
    y = ()
    for step in range(steps):
        live = running(step)
        options = {"near": near, "far": [far]}
        if step < rounds:
            options["fresh"] = fresh[step]
        found = [(holders, options[kind]) for kind, holders in sources_of(step)]
        y = layer(step, live, found, y)
        near, far, far_next = None, far_next, None
        if any(s % 2 == 1 for s in live):
            near = [exchange(part, near_hop) for part in y]
        if any(s % 2 == 0 and s > 0 for s in live):
            far_next = exchange(y[0], far_hop)
        if 0 in live:
            turn = step - first[0]
            finished[turn] = [None] * sides
            for side in reversed(range(sides)):
                finished[turn][side] = exchange(
                    y[side],
                    lambda s, t, w: (owner_of(turn, w), t, beside(w) if side else w)
                    if s == 0
                    else None,
                )
    wanted = []
    for held in range(held_patches):
        options = []
        for owner in range(n_seg):
            patch = owner * held_patches + held
            turn, member = rounds - 1 - patch // sides, patch % sides
            for w in range(sides):
                options.append((owner, w, sides, turn * sides + (0 if w == member else 1)))
        wanted.append(options)
    (chosen,) = run(
        functools.partial(choose_kernel, wanted),
        [],
        [piece for turn in range(rounds) for piece in finished[turn]],
        arrays(((held_patches * edge_rows, tile_h, width), bf16)),
        [pltpu.SemaphoreType.DMA((1,))],
        "choose",
        pl.ANY,
        out_memory=pl.ANY,
    )
    shaped = chosen.reshape(held_patches * FRAME_PATCH, tile_w, tile_h, width)
    return shaped.transpose(0, 2, 1, 3)


def solution(mesh):
    in_specs = (
        P(None, "th", "tw", None),
        P(),
        P("th", "tw", None),
        P("segment", None, None),
        P("segment", None, None),
        P("segment", None, None),
    )
    out_specs = P("segment", "th", "tw", None)
    return jax.shard_map(
        on_device, mesh=mesh, in_specs=in_specs, out_specs=out_specs, check_vma=False
    )
```

```python
import functools
import math

import jax
import jax.numpy as jnp
import numpy as np
from jax import lax
from jax.experimental import pallas as pl
from jax.experimental.pallas import tpu as pltpu
from jax.sharding import PartitionSpec as P

HEAD = 128
HALO = 1
FRAME_PATCH = 4
CHUNK = 512
BLOCK = 16
GROUP = 12
VMEM_BYTES = 10 * 2**20
AXES = ("segment", "th", "tw")
SEG, ROW, COL = range(3)


def head_norm(values):
    mean_square = jnp.mean(values * values, axis=-1, keepdims=True)
    return values * lax.rsqrt(mean_square + 1e-06)


def is_active(place, live):
    return functools.reduce(jnp.logical_or, [place[SEG] == s for s in live])


def neighbour_rows(place, n_th, tile_h):
    below_first = place[ROW] % 2 == 0 if n_th % 2 == 0 else place[ROW] < 0
    row_a = jnp.where(below_first, tile_h, -1)
    row_b = jnp.where(below_first, -1, tile_h)
    valid = []
    for row in (row_a, row_b):
        tile = place[ROW] + jnp.where(row < 0, -1, 1)
        valid.append((tile >= 0) & (tile < n_th))
    return row_a, row_b, valid


def write_masks(spec, place, patterns, tables, outs):
    sides, tile_h, tile_w, n_th, n_tw = spec
    row_a, row_b, _ = neighbour_rows(place, n_th, tile_h)
    lane = place[COL] % sides
    for table, out in zip(tables, outs):
        side, kind = table[0:1, :], table[1:2, :]
        col, row = table[2:3, :], table[3:4, :]
        row = jnp.where(kind == 1, row_a, jnp.where(kind == 2, row_b, row))
        for query_side in range(sides):
            spot = lane if query_side == 0 else 1 - lane
            tile_col = place[COL] - lane + spot
            cols = (side - query_side) * (1 - 2 * lane) * tile_w + col
            cols = jnp.where(kind == 3, -1 - spot * tile_w, cols)
            cols = jnp.where(kind == 4, (sides - spot) * tile_w, cols)
            block = (
                ((row >= 0).astype(jnp.int32) + (row >= tile_h).astype(jnp.int32)) * 3
                + (cols >= 0).astype(jnp.int32)
                + (cols >= tile_w).astype(jnp.int32)
            )
            flag = jnp.zeros(block.shape, jnp.float32)
            for index in range(9):
                pattern = patterns[query_side]
                if len(pattern.shape) == 3:
                    last = pattern.shape[0] - 1
                    value = pattern[last, 0:1, index : index + 1].astype(jnp.float32)
                else:
                    value = pattern[0, index].astype(jnp.float32)
                flag = jnp.where(block == index, value, flag)
            grid_row, grid_col = row + place[ROW] * tile_h, cols + tile_col * tile_w
            inside = (grid_row >= 0) & (grid_row < n_th * tile_h)
            inside &= (grid_col >= 0) & (grid_col < n_tw * tile_w)
            inside &= (cols >= -HALO) & (cols < tile_w + HALO)
            out[query_side : query_side + 1, :] = jnp.where(inside, flag, 0.0)


def row_order(tile_h):
    return [0, tile_h - 1] + list(range(1, tile_h - 1))


def key_value_kernel(live, spec, sources, chosen, place, *refs):
    sides, tile_h, _, n_th, _ = spec
    count = sum(pieces for _, pieces in sources)
    parts, (mod, weight), refs = refs[:count], refs[count : count + 2], refs[count + 2 :]
    x_out, modded, kv = refs[:3]
    inner = kv.shape[1] // 2
    order = row_order(tile_h)
    strip_row = kv.shape[0] // len(chosen)
    base = order.index(chosen[0]) * strip_row

    @pl.when(is_active(place, live))
    def _():
        first = 0
        for holders, pieces in sources:
            if len(parts[first].shape) == 3:
                tile, turned = refs[-2:]

                @pl.when(is_active(place, holders))
                def _(first=first):
                    edge = strip_row // sides
                    for side in range(sides):
                        frames = parts[first + side][: edge].astype(jnp.float32)
                        frames = frames.reshape(tile.shape[1], turned.shape[1])
                        for low in range(0, turned.shape[1], HEAD):
                            lanes = tile.at[low // HEAD]
                            lanes[...] = frames[:, low : low + HEAD]
                            for index, row in enumerate(chosen):
                                start = index * strip_row + side * edge
                                turned[start : start + edge, low : low + HEAD] = lanes[
                                    pl.ds(row, edge, stride=tile_h), :
                                ]

            first += pieces
        gain, shift = 1.0 + mod[1:2, :], mod[0:1, :]
        for start in range(0, kv.shape[0], BLOCK):
            rows = slice(start, start + BLOCK)
            value, first = None, 0
            for holders, pieces in sources:
                if len(parts[first].shape) == 3:
                    part = turned[rows, :]
                else:
                    part = parts[first][base + start : base + start + BLOCK, :].astype(jnp.float32)
                value = part if value is None else jnp.where(is_active(place, holders), part, value)
                first += pieces
            x_out[rows, :] = value.astype(jnp.bfloat16)
            centred = value - jnp.mean(value, axis=-1, keepdims=True)
            variance = jnp.mean(centred * centred, axis=-1, keepdims=True)
            normed = centred * lax.rsqrt(variance + 1e-06)
            modded[rows, :] = (normed * gain + shift).astype(jnp.bfloat16)
        row_a, row_b, _ = neighbour_rows(place, n_th, tile_h)
        low_a, low_b = row_a > 0, row_b > 0
        if n_th % 2:
            low_a, low_b = low_b, low_a
        for start in range(0, 2 * inner, CHUNK):
            projected = jnp.dot(
                modded[...], weight[:, start : start + CHUNK], preferred_element_type=jnp.float32
            )
            for low in range(0, CHUNK, HEAD):
                columns = pl.ds(start + low, HEAD)
                head = projected[:, low : low + HEAD]
                if start < inner:
                    head = head_norm(head)
                head = head.astype(jnp.bfloat16)
                kv[:, columns] = head
                if base == 0:
                    send_a, send_b = refs[3:5]
                    top, bottom = head[:strip_row], head[strip_row : 2 * strip_row]
                    send_a[:, columns] = jnp.where(low_a, bottom, top)
                    send_b[:, columns] = jnp.where(low_b, bottom, top)


def together(parts, columns):
    if len(parts) == 1:
        return parts[0][:, columns]
    return jnp.concatenate([part[:, columns] for part in parts], axis=0)


def masked(mask_ref, tile_h, edge):
    sides, keys = mask_ref.shape
    rows = [jnp.broadcast_to(mask_ref[s : s + 1, :], (edge, keys)) for s in range(sides)]
    return jnp.concatenate(rows * tile_h, axis=0)


def weigh(queries, keys, values, mask):
    scores = [
        lax.dot_general(query, key, (((1,), (1,)), ((), ())), preferred_element_type=jnp.float32)
        for query, key in zip(queries, keys)
    ]
    weights = [
        (jnp.exp2(score * (1.0 / (math.sqrt(HEAD) * math.log(2.0)))) * mask).astype(jnp.bfloat16) for score in scores
    ]
    ones = jnp.ones((values[0].shape[0], HEAD), jnp.bfloat16)
    both = [
        jnp.dot(w, jnp.concatenate([v, ones], axis=1), preferred_element_type=jnp.float32)
        for w, v in zip(weights, values)
    ]
    return [b[:, :HEAD] for b in both], [b[:, HEAD:] for b in both]


def groups(inner):
    heads = [pl.ds(low, HEAD) for low in range(0, inner, HEAD)]
    return [heads[low : low + GROUP] for low in range(0, len(heads), GROUP)]


def first_key_value_kernel(live, spec, sources, chosen, place, qkv, *refs):
    loaded, scratch, sem = refs[-4], refs[-3:-1], refs[-1]
    width = loaded.shape[1]
    copy = pltpu.make_async_copy(qkv.at[:, pl.ds(0, width)], loaded, sem.at[0])
    copy.start()
    key_value_kernel(live, spec, sources, chosen, place, *refs[:-4], *scratch)
    copy.wait()


def first_query_kernel(live, spec, passes, place, *refs):
    tokens = 2 * passes + 1
    sides, tokens, refs = spec[0], refs[:tokens], refs[tokens:]
    patterns, tables, out_weight = refs[:sides], refs[sides : sides + 2], refs[sides + 2]
    queries, top, bottom, own_mask, extra_mask, loaded, sem = refs[sides + 3 :]
    copy = pltpu.make_async_copy(out_weight, loaded, sem.at[0])
    copy.start()
    write_masks(spec, place, patterns, tables, (own_mask, extra_mask))
    query_kernel(live, spec, passes, place, *tokens, own_mask, queries, top, bottom)
    copy.wait()


def second_query_kernel(live, spec, passes, place, *refs):
    tokens = 2 * passes + 1
    sides, tokens, refs = spec[0], refs[:tokens], refs[tokens:]
    patterns, tables, refs = refs[:sides], refs[sides : sides + 2], refs[sides + 2 :]
    queries, top, bottom, own_mask, extra_mask = refs
    write_masks(spec, place, patterns, tables, (own_mask, extra_mask))
    query_kernel(live, spec, passes, place, *tokens, own_mask, queries, top, bottom)


def query_kernel(live, spec, passes, place, *refs):
    modded, kv, refs = refs[:passes], refs[passes : 2 * passes], refs[2 * passes :]
    weight, mask_ref, queries, top, bottom = refs
    sides, tile_h = spec[:2]
    rows, inner = queries.shape

    @pl.when(is_active(place, live))
    def _():
        mask = masked(mask_ref, tile_h, rows // (sides * tile_h))
        tokens = together(modded, slice(None))
        found = []
        for start in range(0, inner, CHUNK):
            projected = jnp.dot(
                tokens, weight[:, start : start + CHUNK], preferred_element_type=jnp.float32
            )
            for low in range(0, CHUNK, HEAD):
                query = head_norm(projected[:, low : low + HEAD]).astype(jnp.bfloat16)
                found.append(query)
                queries[:, start + low : start + low + HEAD] = query
        for group in groups(inner):
            above, below = weigh(
                [found[columns.start // HEAD] for columns in group],
                [together(kv, columns) for columns in group],
                [together(kv, pl.ds(inner + columns.start, HEAD)) for columns in group],
                mask,
            )
            for index, columns in enumerate(group):
                top[:, columns] = above[index]
                bottom[:, columns] = below[index]


def output_kernel(live, spec, extra_count, passes, place, *refs):
    extras, refs = refs[:extra_count], refs[extra_count:]
    (queries, top, bottom, mask_ref), refs = refs[:4], refs[4:]
    x, (mod, weight), refs = refs[:passes], refs[passes : passes + 2], refs[passes + 2 :]
    outs, (attended, turned) = refs[:-2], refs[-2:]
    sides, tile_h, _, n_th, _ = spec
    inner, width = weight.shape
    edge = queries.shape[0] // (sides * tile_h)

    @pl.when(is_active(place, live))
    def _():
        mask = masked(mask_ref, tile_h, edge)
        valid = neighbour_rows(place, n_th, tile_h)[2]

        def received(columns):
            pieces = []
            for index, extra in enumerate(extras):
                piece = extra[:, columns]
                if index < 2:
                    piece = jnp.where(valid[index], piece, jnp.zeros_like(piece))
                pieces.append(piece)
            return jnp.concatenate(pieces, axis=0)

        for heads in groups(inner):
            above, below = weigh(
                [queries[:, columns] for columns in heads],
                [received(columns) for columns in heads],
                [received(pl.ds(inner + columns.start, HEAD)) for columns in heads],
                mask,
            )
            for index, columns in enumerate(heads):
                total = (top[:, columns] + above[index]) / (bottom[:, columns] + below[index])
                attended[:, columns] = total.astype(jnp.bfloat16)
        for start in range(0, width, CHUNK):
            columns = pl.ds(start, CHUNK)
            projected = jnp.dot(
                attended[...], weight[:, start : start + CHUNK], preferred_element_type=jnp.float32
            )
            updated = together(x, columns).astype(jnp.float32)
            updated += mod[2:3, start : start + CHUNK] * projected
            tiles = outs
            if len(outs[0].shape) == 2:
                outs[0][:, columns] = updated.astype(jnp.bfloat16)
                tiles = outs[1:]
            for side, y in enumerate(tiles):
                for low in range(0, CHUNK, HEAD):
                    lanes = turned.at[(side * CHUNK + low) // HEAD]
                    for index, row in enumerate(row_order(tile_h)):
                        first = (index * sides + side) * edge
                        lanes[pl.ds(row, edge, stride=tile_h), :] = updated[
                            first : first + edge, low : low + HEAD
                        ]
                    tile = lanes[...].reshape(*y.shape[:2], HEAD).astype(jnp.bfloat16)
                    y[:, :, pl.ds(start + low, HEAD)] = tile


def choose_kernel(wanted, place, *refs):
    pieces, out, sem = refs[:-2], refs[-2], refs[-1]
    rows = out.shape[0] // len(wanted)
    for index, options in enumerate(wanted):
        for segment, lane, sides, source in options:

            @pl.when((place[SEG] == segment) & (place[COL] % sides == lane))
            def _(index=index, source=source):
                copy = pltpu.make_async_copy(
                    pieces[source], out.at[pl.ds(index * rows, rows)], sem.at[0]
                )
                copy.start()
                copy.wait()


def gather_copies(place, order, tokens, outs, wanted, sides, sems):
    copies = []
    for slot, (out, (base, other)) in enumerate(zip(outs, wanted)):
        patch = base + (place[COL] + other) % sides
        rows = out.shape[0] // FRAME_PATCH
        for frame in range(FRAME_PATCH):
            source = order[patch * FRAME_PATCH + frame]
            copies.append(
                pltpu.make_async_copy(
                    tokens.at[pl.ds(source * rows, rows)],
                    out.at[pl.ds(frame * rows, rows)],
                    sems.at[slot, frame],
                )
            )
    for copy in copies:
        copy.start()
    return copies


def gather_kernel(wanted, sides, place, order, tokens, pattern, *refs):
    outs = refs[:-1]
    copies = gather_copies(place, order, tokens, outs, wanted, sides, refs[-1])
    shape = (1,) + outs[0].shape[1:]
    lanes = lax.broadcasted_iota(jnp.int32, shape, 2)
    block = jnp.zeros(shape, jnp.float32)
    for index in range(9):
        block = jnp.where(lanes == index, pattern[0, index].astype(jnp.float32), block)
    for out in outs:
        out[out.shape[0] - 1 :] = block.astype(jnp.bfloat16)
    for copy in copies:
        copy.wait()


def load_kernel(wanted, sides, place, order, tokens, qkv, loaded, *refs):
    outs, frame_sems, sem = refs[:-2], refs[-2], refs[-1]
    columns = loaded.shape[1]
    copy = pltpu.make_async_copy(qkv.at[:, pl.ds(columns // 2, columns)], loaded, sem.at[0])
    copy.start()
    for frame in gather_copies(place, order, tokens, outs, wanted, sides, frame_sems):
        frame.wait()
    copy.wait()


def run(
    kernel,
    scalars,
    operands,
    outs,
    scratch,
    name,
    memory=pltpu.VMEM,
    limit=VMEM_BYTES,
    after=(),
    out_memory=pltpu.VMEM,
    fixed=None,
):
    result, smem = pl.BlockSpec(memory_space=out_memory), pl.BlockSpec(memory_space=pltpu.SMEM)
    if memory is pltpu.HBM:
        operands = [
            o if o.dtype == jnp.int32 else pltpu.with_memory_space_constraint(o, memory)
            for o in operands
        ]
    skipped = len(after)
    in_specs = [pl.BlockSpec(memory_space=pl.ANY)] * skipped + [smem] * len(scalars)
    for operand in operands:
        small = operand.dtype == jnp.int32 and operand.shape[-1] == 9
        large = operand is fixed
        spec = pl.BlockSpec(memory_space=pltpu.HBM if large else memory)
        in_specs.append(smem if small else spec)
    return pl.pallas_call(
        lambda *refs: kernel(tuple(lax.axis_index(a) for a in AXES), *refs[skipped:]),
        out_shape=outs,
        in_specs=in_specs,
        out_specs=jax.tree.map(lambda _: result, outs),
        scratch_shapes=scratch,
        compiler_params=pltpu.CompilerParams(vmem_limit_bytes=limit),
        cost_estimate=pl.CostEstimate(flops=2**20, bytes_accessed=2**10, transcendentals=0),
        name=name,
    )(*after, *scalars, *operands)


def arrays(*shapes):
    return tuple(jax.ShapeDtypeStruct(shape, dtype) for shape, dtype in shapes)


def exchange(value, partner):
    sizes = [lax.axis_size(axis) for axis in AXES]
    places = [(s, t, w) for s in range(sizes[0]) for t in range(sizes[1]) for w in range(sizes[2])]
    number = {place: index for index, place in enumerate(places)}
    links = [(number[p], number[partner(*p)]) for p in places if partner(*p) in number]
    return lax.ppermute(value, AXES, links)


def on_device(tokens, frame_order, tile_pattern, qkv_weight, out_weight, modulation):
    n_seg, n_th, n_tw = [lax.axis_size(axis) for axis in AXES]
    seg, row_tile, col_tile = [lax.axis_index(axis) for axis in AXES]
    frames, tile_h, tile_w, width = tokens.shape
    inner = out_weight.shape[1]
    patches = frames // FRAME_PATCH
    held_patches = patches // n_seg
    sides = 2 if n_tw % 2 == 0 and patches % 2 == 0 else 1
    rounds = patches // sides
    tile_rows = FRAME_PATCH * tile_h * tile_w
    edge_rows = FRAME_PATCH * tile_w
    strip_rows = sides * tile_rows

    lane = col_tile % sides
    bf16, f32 = jnp.bfloat16, jnp.float32

    def beside(w):
        return w + 1 - 2 * (w % 2)

    def patch_base(turn):
        return (rounds - 1 - turn) * sides

    def token_swap(s, t, w):
        if s == n_seg - 1:
            return (s, t, beside(w))
        return (s, t + 1 - 2 * (t % 2), w) if n_th % 2 == 0 else None

    stored = tokens.transpose(0, 2, 1, 3).reshape(frames * tile_w, tile_h, width)
    tile_shape = ((edge_rows, tile_h, width), bf16)
    theirs, pattern = [], tile_pattern[0]
    patterns = [pattern]
    if sides == 2:
        messages = run(
            functools.partial(gather_kernel, [(patch_base(turn), 1) for turn in range(rounds)], sides),
            [frame_order],
            [stored, pattern],
            arrays(*[((edge_rows + 1, tile_h, width), bf16)] * rounds),
            [pltpu.SemaphoreType.DMA((rounds, FRAME_PATCH))],
            "gather",
            pltpu.HBM,
            2**20,
        )
        theirs = [exchange(message, token_swap) for message in messages]
        patterns.append(exchange(pattern, lambda s, t, w: (s, t, beside(w))))
        messages, qkv_weight = lax.optimization_barrier((messages, qkv_weight))
    wanted = [(patch_base(turn), 0) for turn in range(rounds)]
    kv_w, *tiles = run(
        functools.partial(load_kernel, wanted, sides),
        [frame_order],
        [stored, qkv_weight[0]],
        (pltpu.VMEM((width, 2 * inner), bf16),)
        + arrays(*[tile_shape] * rounds),
        [pltpu.SemaphoreType.DMA((rounds, FRAME_PATCH)), pltpu.SemaphoreType.DMA((1,))],
        "load_weights",
        pltpu.HBM,
        2**20,
    )
    kv_w = pltpu.with_memory_space_constraint(kv_w, pltpu.VMEM)
    fresh = [[tiles[turn]] + ([theirs[turn]] if sides == 2 else []) for turn in range(rounds)]
    stored_qkv, stored_out = [
        pltpu.with_memory_space_constraint(w[0], pltpu.HBM) for w in (qkv_weight, out_weight)
    ]
    mod = modulation[0]

    side_halo = n_tw > sides
    order = row_order(tile_h)
    grid = np.indices((tile_h, sides, FRAME_PATCH, tile_w)).reshape(4, -1)
    own_table = np.stack([grid[1], 0 * grid[1], grid[3], np.asarray(order)[grid[0]]])
    strip_edge = np.indices((sides, FRAME_PATCH, tile_w)).reshape(3, -1)
    extra = [
        np.stack([strip_edge[0], 0 * strip_edge[0] + kind, strip_edge[2], 0 * strip_edge[0]])
        for kind in (1, 2)
    ]
    if side_halo:
        tall = np.repeat(np.arange(-HALO, tile_h + HALO), FRAME_PATCH)
        extra += [np.stack([0 * tall, 0 * tall + kind, 0 * tall, tall]) for kind in (3, 4)]
    tables = [jnp.asarray(t, jnp.int32) for t in (own_table, np.concatenate(extra, axis=1))]

    first = {n_seg - 1: 0}
    for s in range(n_seg - 1, 0, -1):
        first[s - 1] = first[s] + (1 if s % 2 else 2)
    steps = first[0] + rounds
    spec = (sides, tile_h, tile_w, n_th, n_tw)
    paired_rows, paired_segs = n_th % 2 == 0, n_seg % 2 == 0

    def running(step):
        return [s for s in range(n_seg) if 0 <= step - first[s] < rounds]

    def sources_of(step):
        live = running(step)
        found = []
        if n_seg - 1 in live:
            found.append(("fresh", [n_seg - 1]))
        near_to = [s for s in live if s % 2 == 0 and s != n_seg - 1]
        far_to = [s for s in live if s % 2 == 1 and s != n_seg - 1]
        return found + [("near", near_to)] * bool(near_to) + [("far", far_to)] * bool(far_to)

    def spare(live, s, t, w):
        if paired_segs and s ^ 1 not in live:
            return (s ^ 1, t, w)
        return (s, t, beside(w)) if n_tw % 2 == 0 else None

    def rows_a(live):
        def partner(s, t, w):
            if not paired_rows:
                return (s, t + 1, w)
            return (s, t + 1 - 2 * (t % 2), w) if s in live else spare(live, s, t, w)

        return partner

    def rows_b(live):
        def partner(s, t, w):
            other = t - 1 + 2 * (t % 2) if paired_rows else t - 1
            if paired_rows and not 0 <= other < n_th:
                return (s ^ 1, t, w) if paired_segs else None
            if s in live or not paired_rows:
                return (s, other, w)
            if live == [n_seg - 1] and n_seg == 4:
                return (3 - s, t, w) if s in (1, 2) else (s, t, beside(w))
            return spare(live, s, t, w)

        return partner

    def near_hop(s, t, w):
        return (s ^ 1, t, w) if paired_segs else (s - 1, t, w) if s % 2 else None

    def far_hop(s, t, w):
        return (s - 1, t, w) if s % 2 == 0 and s > 0 else None

    def edge_column(kv, above, below, which):
        shape = (-1, sides, FRAME_PATCH, tile_w, 2 * inner)
        rows = jnp.concatenate(kv, axis=0).reshape(shape)
        edge, middle = rows[:2], rows[2:]
        ends = [part.reshape(shape) for part in (above, below)]
        tall = jnp.concatenate([ends[0], edge[:1], middle, edge[1:], ends[1]], axis=0)
        if which == 0:
            column = jnp.where(lane == 0, tall[:, 0, :, 0], tall[:, sides - 1, :, 0])
        else:
            column = jnp.where(lane == 0, tall[:, sides - 1, :, -1], tall[:, 0, :, -1])
        return column.reshape(-1, 2 * inner)

    kept = []

    def layer(step, live, sources, before):
        operands = [part for _, source in sources for part in source]
        counts = [(holders, len(source)) for holders, source in sources]
        strip, edges = strip_rows, sides * edge_rows
        operands += [mod, kv_w]

        def key_value(chosen, sends, **rest):
            rows = len(chosen) * edges
            outs = [((rows, width), bf16), ((rows, width), bf16), ((rows, 2 * inner), bf16)]
            native = any(part.ndim == 3 for part in operands)
            turn = [((width // HEAD, tile_rows, HEAD), f32), ((rows, width), f32)] * native
            return run(
                functools.partial(rest.pop("kernel"), live, spec, counts, chosen),
                [],
                rest.pop("first", []) + operands,
                arrays(*outs, *[((edges, 2 * inner), bf16)] * sends) + rest.pop("more", ()),
                [pltpu.VMEM(shape, kind) for shape, kind in turn] + rest.pop("scratch", []),
                "key_value",
                **rest,
            )

        passes = [order[:2], order[2:]] if 0 < step <= rounds + 1 else [order]
        x, modded, kv = [], [], []
        if step == 0:
            *found, send_a, send_b, q_w = key_value(
                order,
                2,
                kernel=first_key_value_kernel,
                first=[stored_qkv],
                more=(pltpu.VMEM((width, inner), bf16),),
                scratch=[pltpu.SemaphoreType.DMA((1,))],
                fixed=stored_qkv,
            )
            kept.append(pltpu.with_memory_space_constraint(q_w, pltpu.VMEM))
            for held, part in zip((x, modded, kv), found):
                held.append(part)
        else:
            for index, chosen in enumerate(passes):
                found = key_value(
                    chosen,
                    0 if index else 2,
                    kernel=key_value_kernel,
                    after=[send_a] if index else before,
                )
                for held, part in zip((x, modded, kv), found):
                    held.append(part)
                if not index:
                    send_a, send_b = found[3:]
        tokens = modded + kv
        count = len(passes)
        extra_a = exchange(send_a, rows_a(live))
        extra_b = exchange(send_b, rows_b(live))
        outs = arrays(((strip, inner), bf16), ((strip, inner), f32), ((strip, inner), f32))
        if step == 0:
            made = arrays(*[((sides, table.shape[1]), f32) for table in tables])
            queries, top, bottom, own_mask, extra_mask, out_w = run(
                functools.partial(first_query_kernel, live, spec, count),
                [],
                tokens + [kept[0], pattern] + fresh[0][1:] + tables + [stored_out],
                outs + made + (pltpu.VMEM((inner, width), bf16),),
                [pltpu.SemaphoreType.DMA((1,))],
                "query",
                fixed=stored_out,
            )
            out_w = pltpu.with_memory_space_constraint(out_w, pltpu.VMEM)
            kept.extend([own_mask, extra_mask, out_w])
        elif step == 1:
            made = arrays(*[((sides, table.shape[1]), f32) for table in tables])
            queries, top, bottom, *kept[1:3] = run(
                functools.partial(second_query_kernel, live, spec, count),
                [],
                tokens + [kept[0]] + patterns + tables,
                outs + made,
                [],
                "query",
            )
        else:
            queries, top, bottom = run(
                functools.partial(query_kernel, live, spec, count),
                [],
                tokens + kept[:2],
                outs,
                [],
                "query",
            )
        extra_mask, out_w = kept[2:]
        extras = [extra_a, extra_b]
        if side_halo:
            flip = (row_tile % 2 == 1) if paired_rows else jnp.array(True)
            above = jnp.where(flip, extra_a, extra_b)
            below = jnp.where(flip, extra_b, extra_a)
            above = jnp.where(row_tile > 0, above, jnp.zeros_like(above))
            below = jnp.where(row_tile < n_th - 1, below, jnp.zeros_like(below))
            left = edge_column(kv, above, below, 0)
            right = edge_column(kv, above, below, 1)
            from_left = exchange(right, lambda s, t, w: (s, t, w + sides))
            from_right = exchange(left, lambda s, t, w: (s, t, w - sides))
            extras.append(jnp.concatenate([from_left, from_right], axis=0))
        shapes = [((strip, width), bf16)] * (live != [0]) + [tile_shape] * (sides * (0 in live))
        found = run(
            functools.partial(output_kernel, live, spec, len(extras), count),
            [],
            extras + [queries, top, bottom, extra_mask] + x + [mod, out_w],
            arrays(*shapes),
            [pltpu.VMEM((strip, inner), bf16), pltpu.VMEM((sides * CHUNK // HEAD, tile_rows, HEAD), f32)],
            "output",
            after=[turn[-1] for turn in fresh[1:]] if step == 0 and sides == 2 else (),
        )
        return (found[:1], found[1:]) if live != [0] else ((), found)

    def owner_of(turn, w):
        return (patch_base(turn) + w % sides) // held_patches

    near = far = far_next = None
    finished = {}
    y = ()
    for step in range(steps):
        live = running(step)
        options = {"near": near, "far": [far]}
        if step < rounds:
            options["fresh"] = fresh[step]
        found = [(holders, options[kind]) for kind, holders in sources_of(step)]
        y, finals = layer(step, live, found, y)
        near, far, far_next = None, far_next, None
        if any(s % 2 == 1 for s in live):
            near = [exchange(part, near_hop) for part in y]
        if any(s % 2 == 0 and s > 0 for s in live):
            far_next = exchange(y[0], far_hop)
        if 0 in live:
            turn = step - first[0]
            finished[turn] = [None] * sides
            for side in reversed(range(sides)):
                finished[turn][side] = exchange(
                    finals[side],
                    lambda s, t, w: (owner_of(turn, w), t, beside(w) if side else w)
                    if s == 0
                    else None,
                )
    wanted = []
    for held in range(held_patches):
        options = []
        for owner in range(n_seg):
            patch = owner * held_patches + held
            turn, member = rounds - 1 - patch // sides, patch % sides
            for w in range(sides):
                options.append((owner, w, sides, turn * sides + (0 if w == member else 1)))
        wanted.append(options)
    (chosen,) = run(
        functools.partial(choose_kernel, wanted),
        [],
        [piece for turn in range(rounds) for piece in finished[turn]],
        arrays(((held_patches * edge_rows, tile_h, width), bf16)),
        [pltpu.SemaphoreType.DMA((1,))],
        "choose",
        pl.ANY,
        out_memory=pl.ANY,
    )
    shaped = chosen.reshape(held_patches * FRAME_PATCH, tile_w, tile_h, width)
    return shaped.transpose(0, 2, 1, 3)


def solution(mesh):
    in_specs = (
        P(None, "th", "tw", None),
        P(),
        P("th", "tw", None),
        P("segment", None, None),
        P("segment", None, None),
        P("segment", None, None),
    )
    out_specs = P("segment", "th", "tw", None)
    return jax.shard_map(
        on_device, mesh=mesh, in_specs=in_specs, out_specs=out_specs, check_vma=False
    )
```

```python
import functools
import math

import jax
import jax.numpy as jnp
import numpy as np
from jax import lax
from jax.experimental import pallas as pl
from jax.experimental.pallas import tpu as pltpu
from jax.sharding import PartitionSpec as P

HEAD = 128
HALO = 1
FRAME_PATCH = 4
CHUNK = 512
BLOCK = 16
GROUP = 12
VMEM_BYTES = 10 * 2**20
AXES = ("segment", "th", "tw")
SEG, ROW, COL = range(3)


def head_norm(values):
    mean_square = jnp.mean(values * values, axis=-1, keepdims=True)
    return values * lax.rsqrt(mean_square + 1e-06)


def is_active(place, live):
    return functools.reduce(jnp.logical_or, [place[SEG] == s for s in live])


def neighbour_rows(place, n_th, tile_h):
    below_first = place[ROW] % 2 == 0 if n_th % 2 == 0 else place[ROW] < 0
    row_a = jnp.where(below_first, tile_h, -1)
    row_b = jnp.where(below_first, -1, tile_h)
    valid = []
    for row in (row_a, row_b):
        tile = place[ROW] + jnp.where(row < 0, -1, 1)
        valid.append((tile >= 0) & (tile < n_th))
    return row_a, row_b, valid


def write_masks(spec, place, patterns, tables, outs):
    sides, tile_h, tile_w, n_th, n_tw = spec
    row_a, row_b, _ = neighbour_rows(place, n_th, tile_h)
    lane = place[COL] % sides
    for table, out in zip(tables, outs):
        side, kind = table[0:1, :], table[1:2, :]
        col, row = table[2:3, :], table[3:4, :]
        row = jnp.where(kind == 1, row_a, jnp.where(kind == 2, row_b, row))
        for query_side in range(sides):
            spot = lane if query_side == 0 else 1 - lane
            tile_col = place[COL] - lane + spot
            cols = (side - query_side) * (1 - 2 * lane) * tile_w + col
            cols = jnp.where(kind == 3, -1 - spot * tile_w, cols)
            cols = jnp.where(kind == 4, (sides - spot) * tile_w, cols)
            block = (
                ((row >= 0).astype(jnp.int32) + (row >= tile_h).astype(jnp.int32)) * 3
                + (cols >= 0).astype(jnp.int32)
                + (cols >= tile_w).astype(jnp.int32)
            )
            flag = jnp.zeros(block.shape, jnp.float32)
            for index in range(9):
                pattern = patterns[query_side]
                if len(pattern.shape) == 3:
                    last = pattern.shape[0] - 1
                    value = pattern[last, 0:1, index : index + 1].astype(jnp.float32)
                else:
                    value = pattern[0, index].astype(jnp.float32)
                flag = jnp.where(block == index, value, flag)
            grid_row, grid_col = row + place[ROW] * tile_h, cols + tile_col * tile_w
            inside = (grid_row >= 0) & (grid_row < n_th * tile_h)
            inside &= (grid_col >= 0) & (grid_col < n_tw * tile_w)
            inside &= (cols >= -HALO) & (cols < tile_w + HALO)
            out[query_side : query_side + 1, :] = jnp.where(inside, flag, 0.0)


def row_order(tile_h):
    return [0, tile_h - 1] + list(range(1, tile_h - 1))


def key_value_kernel(live, spec, sources, chosen, place, *refs):
    sides, tile_h, _, n_th, _ = spec
    count = sum(pieces for _, pieces in sources)
    parts, (mod, weight), refs = refs[:count], refs[count : count + 2], refs[count + 2 :]
    x_out, modded, kv = refs[:3]
    inner = kv.shape[1] // 2
    order = row_order(tile_h)
    strip_row = kv.shape[0] // len(chosen)
    base = order.index(chosen[0]) * strip_row

    @pl.when(is_active(place, live))
    def _():
        first = 0
        for holders, pieces in sources:
            if len(parts[first].shape) == 3:
                tile, turned = refs[-2:]

                @pl.when(is_active(place, holders))
                def _(first=first):
                    edge = strip_row // sides
                    for side in range(sides):
                        frames = parts[first + side][: edge].astype(jnp.float32)
                        frames = frames.reshape(tile.shape[1], turned.shape[1])
                        for low in range(0, turned.shape[1], HEAD):
                            lanes = tile.at[low // HEAD]
                            lanes[...] = frames[:, low : low + HEAD]
                            for index, row in enumerate(chosen):
                                start = index * strip_row + side * edge
                                turned[start : start + edge, low : low + HEAD] = lanes[
                                    pl.ds(row, edge, stride=tile_h), :
                                ]

            first += pieces
        gain, shift = 1.0 + mod[1:2, :], mod[0:1, :]
        for start in range(0, kv.shape[0], BLOCK):
            rows = slice(start, start + BLOCK)
            value, first = None, 0
            for holders, pieces in sources:
                if len(parts[first].shape) == 3:
                    part = turned[rows, :]
                else:
                    index, within = divmod(start, parts[first].shape[0])
                    part = parts[first + index][within : within + BLOCK, :].astype(jnp.float32)
                value = part if value is None else jnp.where(is_active(place, holders), part, value)
                first += pieces
            x_out[rows, :] = value.astype(jnp.bfloat16)
            centred = value - jnp.mean(value, axis=-1, keepdims=True)
            variance = jnp.mean(centred * centred, axis=-1, keepdims=True)
            normed = centred * lax.rsqrt(variance + 1e-06)
            modded[rows, :] = (normed * gain + shift).astype(jnp.bfloat16)
        row_a, row_b, _ = neighbour_rows(place, n_th, tile_h)
        low_a, low_b = row_a > 0, row_b > 0
        if n_th % 2:
            low_a, low_b = low_b, low_a
        for start in range(0, 2 * inner, CHUNK):
            projected = jnp.dot(
                modded[...], weight[:, start : start + CHUNK], preferred_element_type=jnp.float32
            )
            for low in range(0, CHUNK, HEAD):
                columns = pl.ds(start + low, HEAD)
                head = projected[:, low : low + HEAD]
                if start < inner:
                    head = head_norm(head)
                head = head.astype(jnp.bfloat16)
                kv[:, columns] = head
                if base == 0:
                    send_a, send_b = refs[3:5]
                    top, bottom = head[:strip_row], head[strip_row : 2 * strip_row]
                    send_a[:, columns] = jnp.where(low_a, bottom, top)
                    send_b[:, columns] = jnp.where(low_b, bottom, top)


def together(parts, columns):
    if len(parts) == 1:
        return parts[0][:, columns]
    return jnp.concatenate([part[:, columns] for part in parts], axis=0)


def masked(mask_ref, tile_h, edge):
    sides, keys = mask_ref.shape
    rows = [jnp.broadcast_to(mask_ref[s : s + 1, :], (edge, keys)) for s in range(sides)]
    return jnp.concatenate(rows * tile_h, axis=0)


def weigh(queries, keys, values, mask):
    scores = [
        lax.dot_general(query, key, (((1,), (1,)), ((), ())), preferred_element_type=jnp.float32)
        for query, key in zip(queries, keys)
    ]
    weights = [
        (jnp.exp2(score * (1.0 / (math.sqrt(HEAD) * math.log(2.0)))) * mask).astype(jnp.bfloat16) for score in scores
    ]
    ones = jnp.ones((values[0].shape[0], HEAD), jnp.bfloat16)
    both = [
        jnp.dot(w, jnp.concatenate([v, ones], axis=1), preferred_element_type=jnp.float32)
        for w, v in zip(weights, values)
    ]
    return [b[:, :HEAD] for b in both], [b[:, HEAD:] for b in both]


def groups(inner):
    heads = [pl.ds(low, HEAD) for low in range(0, inner, HEAD)]
    return [heads[low : low + GROUP] for low in range(0, len(heads), GROUP)]


def first_key_value_kernel(live, spec, sources, chosen, place, qkv, *refs):
    loaded, scratch, sem = refs[-4], refs[-3:-1], refs[-1]
    width = loaded.shape[1]
    copy = pltpu.make_async_copy(qkv.at[:, pl.ds(0, width)], loaded, sem.at[0])
    copy.start()
    key_value_kernel(live, spec, sources, chosen, place, *refs[:-4], *scratch)
    copy.wait()


def first_query_kernel(live, spec, passes, place, *refs):
    tokens = 2 * passes + 1
    sides, tokens, refs = spec[0], refs[:tokens], refs[tokens:]
    patterns, tables, out_weight = refs[:sides], refs[sides : sides + 2], refs[sides + 2]
    queries, top, bottom, own_mask, extra_mask, loaded, sem = refs[sides + 3 :]
    copy = pltpu.make_async_copy(out_weight, loaded, sem.at[0])
    copy.start()
    write_masks(spec, place, patterns, tables, (own_mask, extra_mask))
    query_kernel(live, spec, passes, place, *tokens, own_mask, queries, top, bottom)
    copy.wait()


def second_query_kernel(live, spec, passes, place, *refs):
    tokens = 2 * passes + 1
    sides, tokens, refs = spec[0], refs[:tokens], refs[tokens:]
    patterns, tables, refs = refs[:sides], refs[sides : sides + 2], refs[sides + 2 :]
    queries, top, bottom, own_mask, extra_mask = refs
    write_masks(spec, place, patterns, tables, (own_mask, extra_mask))
    query_kernel(live, spec, passes, place, *tokens, own_mask, queries, top, bottom)


def query_kernel(live, spec, passes, place, *refs):
    modded, kv, refs = refs[:passes], refs[passes : 2 * passes], refs[2 * passes :]
    weight, mask_ref, queries, top, bottom = refs
    sides, tile_h = spec[:2]
    rows, inner = queries.shape

    @pl.when(is_active(place, live))
    def _():
        mask = masked(mask_ref, tile_h, rows // (sides * tile_h))
        tokens = together(modded, slice(None))
        found = []
        for start in range(0, inner, CHUNK):
            projected = jnp.dot(
                tokens, weight[:, start : start + CHUNK], preferred_element_type=jnp.float32
            )
            for low in range(0, CHUNK, HEAD):
                query = head_norm(projected[:, low : low + HEAD]).astype(jnp.bfloat16)
                found.append(query)
                queries[:, start + low : start + low + HEAD] = query
        for group in groups(inner):
            above, below = weigh(
                [found[columns.start // HEAD] for columns in group],
                [together(kv, columns) for columns in group],
                [together(kv, pl.ds(inner + columns.start, HEAD)) for columns in group],
                mask,
            )
            for index, columns in enumerate(group):
                top[:, columns] = above[index]
                bottom[:, columns] = below[index]


def output_kernel(live, spec, extra_count, passes, place, *refs):
    extras, refs = refs[:extra_count], refs[extra_count:]
    (queries, top, bottom, mask_ref), refs = refs[:4], refs[4:]
    x, (mod, weight), refs = refs[:passes], refs[passes : passes + 2], refs[passes + 2 :]
    outs, (attended, turned) = refs[:-2], refs[-2:]
    sides, tile_h, _, n_th, _ = spec
    inner, width = weight.shape
    edge = queries.shape[0] // (sides * tile_h)

    @pl.when(is_active(place, live))
    def _():
        mask = masked(mask_ref, tile_h, edge)
        valid = neighbour_rows(place, n_th, tile_h)[2]

        def received(columns):
            pieces = []
            for index, extra in enumerate(extras):
                piece = extra[:, columns]
                if index < 2:
                    piece = jnp.where(valid[index], piece, jnp.zeros_like(piece))
                pieces.append(piece)
            return jnp.concatenate(pieces, axis=0)

        for heads in groups(inner):
            above, below = weigh(
                [queries[:, columns] for columns in heads],
                [received(columns) for columns in heads],
                [received(pl.ds(inner + columns.start, HEAD)) for columns in heads],
                mask,
            )
            for index, columns in enumerate(heads):
                total = (top[:, columns] + above[index]) / (bottom[:, columns] + below[index])
                attended[:, columns] = total.astype(jnp.bfloat16)
        for start in range(0, width, CHUNK):
            columns = pl.ds(start, CHUNK)
            projected = jnp.dot(
                attended[...], weight[:, start : start + CHUNK], preferred_element_type=jnp.float32
            )
            updated = together(x, columns).astype(jnp.float32)
            updated += mod[2:3, start : start + CHUNK] * projected
            first = 0
            for y in outs:
                if len(y.shape) == 2:
                    y[:, columns] = updated[first : first + y.shape[0]].astype(jnp.bfloat16)
                    first += y.shape[0]
            for side, y in enumerate([y for y in outs if len(y.shape) == 3]):
                for low in range(0, CHUNK, HEAD):
                    lanes = turned.at[(side * CHUNK + low) // HEAD]
                    for index, row in enumerate(row_order(tile_h)):
                        first = (index * sides + side) * edge
                        lanes[pl.ds(row, edge, stride=tile_h), :] = updated[
                            first : first + edge, low : low + HEAD
                        ]
                    tile = lanes[...].reshape(*y.shape[:2], HEAD).astype(jnp.bfloat16)
                    y[:, :, pl.ds(start + low, HEAD)] = tile


def choose_kernel(wanted, place, *refs):
    pieces, out, sem = refs[:-2], refs[-2], refs[-1]
    rows = out.shape[0] // len(wanted)
    for index, options in enumerate(wanted):
        for segment, lane, sides, source in options:

            @pl.when((place[SEG] == segment) & (place[COL] % sides == lane))
            def _(index=index, source=source):
                copy = pltpu.make_async_copy(
                    pieces[source], out.at[pl.ds(index * rows, rows)], sem.at[0]
                )
                copy.start()
                copy.wait()


def gather_copies(place, order, tokens, outs, wanted, sides, sems):
    copies = []
    for slot, (out, (base, other)) in enumerate(zip(outs, wanted)):
        patch = base + (place[COL] + other) % sides
        rows = out.shape[0] // FRAME_PATCH
        for frame in range(FRAME_PATCH):
            source = order[patch * FRAME_PATCH + frame]
            copies.append(
                pltpu.make_async_copy(
                    tokens.at[pl.ds(source * rows, rows)],
                    out.at[pl.ds(frame * rows, rows)],
                    sems.at[slot, frame],
                )
            )
    for copy in copies:
        copy.start()
    return copies


def gather_kernel(wanted, sides, place, order, tokens, pattern, *refs):
    outs = refs[:-1]
    copies = gather_copies(place, order, tokens, outs, wanted, sides, refs[-1])
    shape = (1,) + outs[0].shape[1:]
    lanes = lax.broadcasted_iota(jnp.int32, shape, 2)
    block = jnp.zeros(shape, jnp.float32)
    for index in range(9):
        block = jnp.where(lanes == index, pattern[0, index].astype(jnp.float32), block)
    for out in outs:
        out[out.shape[0] - 1 :] = block.astype(jnp.bfloat16)
    for copy in copies:
        copy.wait()


def load_kernel(wanted, sides, place, order, tokens, qkv, loaded, *refs):
    outs, frame_sems, sem = refs[:-2], refs[-2], refs[-1]
    columns = loaded.shape[1]
    copy = pltpu.make_async_copy(qkv.at[:, pl.ds(columns // 2, columns)], loaded, sem.at[0])
    copy.start()
    for frame in gather_copies(place, order, tokens, outs, wanted, sides, frame_sems):
        frame.wait()
    copy.wait()


def run(
    kernel,
    scalars,
    operands,
    outs,
    scratch,
    name,
    memory=pltpu.VMEM,
    limit=VMEM_BYTES,
    after=(),
    out_memory=pltpu.VMEM,
    fixed=None,
):
    result, smem = pl.BlockSpec(memory_space=out_memory), pl.BlockSpec(memory_space=pltpu.SMEM)
    if memory is pltpu.HBM:
        operands = [
            o if o.dtype == jnp.int32 else pltpu.with_memory_space_constraint(o, memory)
            for o in operands
        ]
    skipped = len(after)
    in_specs = [pl.BlockSpec(memory_space=pl.ANY)] * skipped + [smem] * len(scalars)
    for operand in operands:
        small = operand.dtype == jnp.int32 and operand.shape[-1] == 9
        large = operand is fixed
        spec = pl.BlockSpec(memory_space=pltpu.HBM if large else memory)
        in_specs.append(smem if small else spec)
    return pl.pallas_call(
        lambda *refs: kernel(tuple(lax.axis_index(a) for a in AXES), *refs[skipped:]),
        out_shape=outs,
        in_specs=in_specs,
        out_specs=jax.tree.map(lambda _: result, outs),
        scratch_shapes=scratch,
        compiler_params=pltpu.CompilerParams(vmem_limit_bytes=limit),
        cost_estimate=pl.CostEstimate(flops=2**20, bytes_accessed=2**10, transcendentals=0),
        name=name,
    )(*after, *scalars, *operands)


def arrays(*shapes):
    return tuple(jax.ShapeDtypeStruct(shape, dtype) for shape, dtype in shapes)


def exchange(value, partner):
    sizes = [lax.axis_size(axis) for axis in AXES]
    places = [(s, t, w) for s in range(sizes[0]) for t in range(sizes[1]) for w in range(sizes[2])]
    number = {place: index for index, place in enumerate(places)}
    links = [(number[p], number[partner(*p)]) for p in places if partner(*p) in number]
    return lax.ppermute(value, AXES, links)


def on_device(tokens, frame_order, tile_pattern, qkv_weight, out_weight, modulation):
    n_seg, n_th, n_tw = [lax.axis_size(axis) for axis in AXES]
    seg, row_tile, col_tile = [lax.axis_index(axis) for axis in AXES]
    frames, tile_h, tile_w, width = tokens.shape
    inner = out_weight.shape[1]
    patches = frames // FRAME_PATCH
    held_patches = patches // n_seg
    sides = 2 if n_tw % 2 == 0 and patches % 2 == 0 else 1
    rounds = patches // sides
    tile_rows = FRAME_PATCH * tile_h * tile_w
    edge_rows = FRAME_PATCH * tile_w
    strip_rows = sides * tile_rows

    lane = col_tile % sides
    bf16, f32 = jnp.bfloat16, jnp.float32

    def beside(w):
        return w + 1 - 2 * (w % 2)

    def patch_base(turn):
        return (rounds - 1 - turn) * sides

    def token_swap(s, t, w):
        if s == n_seg - 1:
            return (s, t, beside(w))
        return (s, t + 1 - 2 * (t % 2), w) if n_th % 2 == 0 else None

    stored = tokens.transpose(0, 2, 1, 3).reshape(frames * tile_w, tile_h, width)
    tile_shape = ((edge_rows, tile_h, width), bf16)
    theirs, pattern = [], tile_pattern[0]
    patterns = [pattern]
    if sides == 2:
        messages = run(
            functools.partial(gather_kernel, [(patch_base(turn), 1) for turn in range(rounds)], sides),
            [frame_order],
            [stored, pattern],
            arrays(*[((edge_rows + 1, tile_h, width), bf16)] * rounds),
            [pltpu.SemaphoreType.DMA((rounds, FRAME_PATCH))],
            "gather",
            pltpu.HBM,
            2**20,
        )
        theirs = [exchange(message, token_swap) for message in messages]
        patterns.append(exchange(pattern, lambda s, t, w: (s, t, beside(w))))
        messages, qkv_weight = lax.optimization_barrier((messages, qkv_weight))
    wanted = [(patch_base(turn), 0) for turn in range(rounds)]
    kv_w, *tiles = run(
        functools.partial(load_kernel, wanted, sides),
        [frame_order],
        [stored, qkv_weight[0]],
        (pltpu.VMEM((width, 2 * inner), bf16),)
        + arrays(*[tile_shape] * rounds),
        [pltpu.SemaphoreType.DMA((rounds, FRAME_PATCH)), pltpu.SemaphoreType.DMA((1,))],
        "load_weights",
        pltpu.HBM,
        2**20,
    )
    kv_w = pltpu.with_memory_space_constraint(kv_w, pltpu.VMEM)
    fresh = [[tiles[turn]] + ([theirs[turn]] if sides == 2 else []) for turn in range(rounds)]
    stored_qkv, stored_out = [
        pltpu.with_memory_space_constraint(w[0], pltpu.HBM) for w in (qkv_weight, out_weight)
    ]
    mod = modulation[0]

    side_halo = n_tw > sides
    order = row_order(tile_h)
    grid = np.indices((tile_h, sides, FRAME_PATCH, tile_w)).reshape(4, -1)
    own_table = np.stack([grid[1], 0 * grid[1], grid[3], np.asarray(order)[grid[0]]])
    strip_edge = np.indices((sides, FRAME_PATCH, tile_w)).reshape(3, -1)
    extra = [
        np.stack([strip_edge[0], 0 * strip_edge[0] + kind, strip_edge[2], 0 * strip_edge[0]])
        for kind in (1, 2)
    ]
    if side_halo:
        tall = np.repeat(np.arange(-HALO, tile_h + HALO), FRAME_PATCH)
        extra += [np.stack([0 * tall, 0 * tall + kind, 0 * tall, tall]) for kind in (3, 4)]
    tables = [jnp.asarray(t, jnp.int32) for t in (own_table, np.concatenate(extra, axis=1))]

    first = {n_seg - 1: 0}
    for s in range(n_seg - 1, 0, -1):
        first[s - 1] = first[s] + (1 if s % 2 else 2)
    steps = first[0] + rounds
    spec = (sides, tile_h, tile_w, n_th, n_tw)
    paired_rows, paired_segs = n_th % 2 == 0, n_seg % 2 == 0

    def running(step):
        return [s for s in range(n_seg) if 0 <= step - first[s] < rounds]

    def sources_of(step):
        live = running(step)
        found = []
        if n_seg - 1 in live:
            found.append(("fresh", [n_seg - 1]))
        near_to = [s for s in live if s % 2 == 0 and s != n_seg - 1]
        far_to = [s for s in live if s % 2 == 1 and s != n_seg - 1]
        return found + [("near", near_to)] * bool(near_to) + [("far", far_to)] * bool(far_to)

    def spare(live, s, t, w):
        if paired_segs and s ^ 1 not in live:
            return (s ^ 1, t, w)
        return (s, t, beside(w)) if n_tw % 2 == 0 else None

    def rows_a(live):
        def partner(s, t, w):
            if not paired_rows:
                return (s, t + 1, w)
            return (s, t + 1 - 2 * (t % 2), w) if s in live else spare(live, s, t, w)

        return partner

    def rows_b(live):
        def partner(s, t, w):
            other = t - 1 + 2 * (t % 2) if paired_rows else t - 1
            if paired_rows and not 0 <= other < n_th:
                return (s ^ 1, t, w) if paired_segs else None
            if s in live or not paired_rows:
                return (s, other, w)
            if live == [n_seg - 1] and n_seg == 4:
                return (3 - s, t, w) if s in (1, 2) else (s, t, beside(w))
            return spare(live, s, t, w)

        return partner

    def near_hop(s, t, w):
        return (s ^ 1, t, w) if paired_segs else (s - 1, t, w) if s % 2 else None

    def far_hop(s, t, w):
        return (s - 1, t, w) if s % 2 == 0 and s > 0 else None

    def far_swap(s, t, w):
        return (s + 1, t, w) if s % 2 and s < n_seg - 1 else far_hop(s, t, w)

    def edge_column(kv, above, below, which):
        shape = (-1, sides, FRAME_PATCH, tile_w, 2 * inner)
        rows = jnp.concatenate(kv, axis=0).reshape(shape)
        edge, middle = rows[:2], rows[2:]
        ends = [part.reshape(shape) for part in (above, below)]
        tall = jnp.concatenate([ends[0], edge[:1], middle, edge[1:], ends[1]], axis=0)
        if which == 0:
            column = jnp.where(lane == 0, tall[:, 0, :, 0], tall[:, sides - 1, :, 0])
        else:
            column = jnp.where(lane == 0, tall[:, sides - 1, :, -1], tall[:, 0, :, -1])
        return column.reshape(-1, 2 * inner)

    kept = []

    def layer(step, live, sources, before):
        strip, edges = strip_rows, sides * edge_rows

        def key_value(chosen, sends, **rest):
            rows = len(chosen) * edges
            operands, counts = [], []
            for holders, source in sources:
                if source[0].ndim == 2 and len(chosen) < tile_h:
                    source = source[:1] if chosen[0] == 0 else source[1:]
                operands += source
                counts.append((holders, len(source)))
            operands += [mod, kv_w]
            outs = [((rows, width), bf16), ((rows, width), bf16), ((rows, 2 * inner), bf16)]
            native = any(part.ndim == 3 for part in operands)
            turn = [((width // HEAD, tile_rows, HEAD), f32), ((rows, width), f32)] * native
            return run(
                functools.partial(rest.pop("kernel"), live, spec, counts, chosen),
                [],
                rest.pop("first", []) + operands,
                arrays(*outs, *[((edges, 2 * inner), bf16)] * sends) + rest.pop("more", ()),
                [pltpu.VMEM(shape, kind) for shape, kind in turn] + rest.pop("scratch", []),
                "key_value",
                **rest,
            )

        passes = [order[:2], order[2:]] if 0 < step < steps - 1 else [order]
        x, modded, kv = [], [], []
        if step == 0:
            *found, send_a, send_b, q_w = key_value(
                order,
                2,
                kernel=first_key_value_kernel,
                first=[stored_qkv],
                more=(pltpu.VMEM((width, inner), bf16),),
                scratch=[pltpu.SemaphoreType.DMA((1,))],
                fixed=stored_qkv,
            )
            kept.append(pltpu.with_memory_space_constraint(q_w, pltpu.VMEM))
            for held, part in zip((x, modded, kv), found):
                held.append(part)
        else:
            for index, chosen in enumerate(passes):
                found = key_value(
                    chosen,
                    0 if index else 2,
                    kernel=key_value_kernel,
                    after=[send_a] if index else before,
                )
                for held, part in zip((x, modded, kv), found):
                    held.append(part)
                if not index:
                    send_a, send_b = found[3:]
        tokens = modded + kv
        count = len(passes)
        extra_a = exchange(send_a, rows_a(live))
        extra_b = exchange(send_b, rows_b(live))
        outs = arrays(((strip, inner), bf16), ((strip, inner), f32), ((strip, inner), f32))
        if step == 0:
            made = arrays(*[((sides, table.shape[1]), f32) for table in tables])
            queries, top, bottom, own_mask, extra_mask, out_w = run(
                functools.partial(first_query_kernel, live, spec, count),
                [],
                tokens + [kept[0], pattern] + fresh[0][1:] + tables + [stored_out],
                outs + made + (pltpu.VMEM((inner, width), bf16),),
                [pltpu.SemaphoreType.DMA((1,))],
                "query",
                fixed=stored_out,
            )
            out_w = pltpu.with_memory_space_constraint(out_w, pltpu.VMEM)
            kept.extend([own_mask, extra_mask, out_w])
        elif step == 1:
            made = arrays(*[((sides, table.shape[1]), f32) for table in tables])
            queries, top, bottom, *kept[1:3] = run(
                functools.partial(second_query_kernel, live, spec, count),
                [],
                tokens + [kept[0]] + patterns + tables,
                outs + made,
                [],
                "query",
            )
        else:
            queries, top, bottom = run(
                functools.partial(query_kernel, live, spec, count),
                [],
                tokens + kept[:2],
                outs,
                [],
                "query",
            )
        extra_mask, out_w = kept[2:]
        extras = [extra_a, extra_b]
        if side_halo:
            flip = (row_tile % 2 == 1) if paired_rows else jnp.array(True)
            above = jnp.where(flip, extra_a, extra_b)
            below = jnp.where(flip, extra_b, extra_a)
            above = jnp.where(row_tile > 0, above, jnp.zeros_like(above))
            below = jnp.where(row_tile < n_th - 1, below, jnp.zeros_like(below))
            left = edge_column(kv, above, below, 0)
            right = edge_column(kv, above, below, 1)
            from_left = exchange(right, lambda s, t, w: (s, t, w + sides))
            from_right = exchange(left, lambda s, t, w: (s, t, w - sides))
            extras.append(jnp.concatenate([from_left, from_right], axis=0))
        shapes = [((2 * edges, width), bf16), ((strip - 2 * edges, width), bf16)]
        shapes = shapes * (live != [0]) + [tile_shape] * (sides * (0 in live))
        found = run(
            functools.partial(output_kernel, live, spec, len(extras), count),
            [],
            extras + [queries, top, bottom, extra_mask] + x + [mod, out_w],
            arrays(*shapes),
            [pltpu.VMEM((strip, inner), bf16), pltpu.VMEM((sides * CHUNK // HEAD, tile_rows, HEAD), f32)],
            "output",
            after=[turn[-1] for turn in fresh[1:]] if step == 0 and sides == 2 else (),
        )
        return (found[:2], found[2:]) if live != [0] else ((), found)

    def owner_of(turn, w):
        return (patch_base(turn) + w % sides) // held_patches

    near = far = far_next = None
    finished = {}
    y = ()
    for step in range(steps):
        live = running(step)
        options = {"near": near, "far": far}
        if step < rounds:
            options["fresh"] = fresh[step]
        found = [(holders, options[kind]) for kind, holders in sources_of(step)]
        y, finals = layer(step, live, found, y)
        near, far, far_next = None, far_next, None
        if any(s % 2 == 1 for s in live):
            near = [exchange(part, near_hop) for part in y]
        if any(s % 2 == 0 and s > 0 for s in live):
            far_next = [exchange(y[0], far_hop), exchange(y[1], far_swap)]
        if 0 in live:
            turn = step - first[0]
            finished[turn] = [None] * sides
            for side in reversed(range(sides)):
                finished[turn][side] = exchange(
                    finals[side],
                    lambda s, t, w: (owner_of(turn, w), t, beside(w) if side else w)
                    if s == 0
                    else None,
                )
    wanted = []
    for held in range(held_patches):
        options = []
        for owner in range(n_seg):
            patch = owner * held_patches + held
            turn, member = rounds - 1 - patch // sides, patch % sides
            for w in range(sides):
                options.append((owner, w, sides, turn * sides + (0 if w == member else 1)))
        wanted.append(options)
    (chosen,) = run(
        functools.partial(choose_kernel, wanted),
        [],
        [piece for turn in range(rounds) for piece in finished[turn]],
        arrays(((held_patches * edge_rows, tile_h, width), bf16)),
        [pltpu.SemaphoreType.DMA((1,))],
        "choose",
        pl.ANY,
        out_memory=pl.ANY,
    )
    shaped = chosen.reshape(held_patches * FRAME_PATCH, tile_w, tile_h, width)
    return shaped.transpose(0, 2, 1, 3)


def solution(mesh):
    in_specs = (
        P(None, "th", "tw", None),
        P(),
        P("th", "tw", None),
        P("segment", None, None),
        P("segment", None, None),
        P("segment", None, None),
    )
    out_specs = P("segment", "th", "tw", None)
    return jax.shard_map(
        on_device, mesh=mesh, in_specs=in_specs, out_specs=out_specs, check_vma=False
    )
```

```python
import functools
import math

import jax
import jax.numpy as jnp
import numpy as np
from jax import lax
from jax.experimental import pallas as pl
from jax.experimental.pallas import tpu as pltpu
from jax.sharding import PartitionSpec as P

HEAD = 128
HALO = 1
FRAME_PATCH = 4
CHUNK = 512
BLOCK = 16
GROUP = 12
VMEM_BYTES = 10 * 2**20
AXES = ("segment", "th", "tw")
SEG, ROW, COL = range(3)


def head_norm(values):
    mean_square = jnp.mean(values * values, axis=-1, keepdims=True)
    return values * lax.rsqrt(mean_square + 1e-06)


def is_active(place, live):
    return functools.reduce(jnp.logical_or, [place[SEG] == s for s in live])


def neighbour_rows(place, n_th, tile_h):
    below_first = place[ROW] % 2 == 0 if n_th % 2 == 0 else place[ROW] < 0
    row_a = jnp.where(below_first, tile_h, -1)
    row_b = jnp.where(below_first, -1, tile_h)
    valid = []
    for row in (row_a, row_b):
        tile = place[ROW] + jnp.where(row < 0, -1, 1)
        valid.append((tile >= 0) & (tile < n_th))
    return row_a, row_b, valid


def write_masks(spec, place, patterns, tables, outs):
    sides, tile_h, tile_w, n_th, n_tw = spec
    row_a, row_b, _ = neighbour_rows(place, n_th, tile_h)
    lane = place[COL] % sides
    for table, out in zip(tables, outs):
        side, kind = table[0:1, :], table[1:2, :]
        col, row = table[2:3, :], table[3:4, :]
        row = jnp.where(kind == 1, row_a, jnp.where(kind == 2, row_b, row))
        for query_side in range(sides):
            spot = lane if query_side == 0 else 1 - lane
            tile_col = place[COL] - lane + spot
            cols = (side - query_side) * (1 - 2 * lane) * tile_w + col
            cols = jnp.where(kind == 3, -1 - spot * tile_w, cols)
            cols = jnp.where(kind == 4, (sides - spot) * tile_w, cols)
            block = (
                ((row >= 0).astype(jnp.int32) + (row >= tile_h).astype(jnp.int32)) * 3
                + (cols >= 0).astype(jnp.int32)
                + (cols >= tile_w).astype(jnp.int32)
            )
            flag = jnp.zeros(block.shape, jnp.float32)
            for index in range(9):
                pattern = patterns[query_side]
                if len(pattern.shape) == 3:
                    last = pattern.shape[0] - 1
                    value = pattern[last, 0:1, index : index + 1].astype(jnp.float32)
                else:
                    value = pattern[0, index].astype(jnp.float32)
                flag = jnp.where(block == index, value, flag)
            grid_row, grid_col = row + place[ROW] * tile_h, cols + tile_col * tile_w
            inside = (grid_row >= 0) & (grid_row < n_th * tile_h)
            inside &= (grid_col >= 0) & (grid_col < n_tw * tile_w)
            inside &= (cols >= -HALO) & (cols < tile_w + HALO)
            out[query_side : query_side + 1, :] = jnp.where(inside, flag, 0.0)


def row_order(tile_h):
    return [0, tile_h - 1] + list(range(1, tile_h - 1))


def key_value_kernel(live, spec, sources, chosen, place, *refs):
    sides, tile_h, _, n_th, _ = spec
    count = sum(pieces for _, pieces in sources)
    parts, (mod, weight), refs = refs[:count], refs[count : count + 2], refs[count + 2 :]
    x_out, modded, kv = refs[:3]
    inner = kv.shape[1] // 2
    order = row_order(tile_h)
    strip_row = kv.shape[0] // len(chosen)
    base = order.index(chosen[0]) * strip_row

    @pl.when(is_active(place, live))
    def _():
        first = 0
        for holders, pieces in sources:
            if len(parts[first].shape) == 3:
                tile, turned = refs[-2:]

                @pl.when(is_active(place, holders))
                def _(first=first):
                    edge = strip_row // sides
                    for side in range(sides):
                        frames = parts[first + side][: edge].astype(jnp.float32)
                        frames = frames.reshape(tile.shape[1], turned.shape[1])
                        for low in range(0, turned.shape[1], HEAD):
                            lanes = tile.at[low // HEAD]
                            lanes[...] = frames[:, low : low + HEAD]
                            for index, row in enumerate(chosen):
                                start = index * strip_row + side * edge
                                turned[start : start + edge, low : low + HEAD] = lanes[
                                    pl.ds(row, edge, stride=tile_h), :
                                ]

            first += pieces
        gain, shift = 1.0 + mod[1:2, :], mod[0:1, :]
        for start in range(0, kv.shape[0], BLOCK):
            rows = slice(start, start + BLOCK)
            value, first = None, 0
            for holders, pieces in sources:
                if len(parts[first].shape) == 3:
                    part = turned[rows, :]
                else:
                    index, within = divmod(start, parts[first].shape[0])
                    part = parts[first + index][within : within + BLOCK, :].astype(jnp.float32)
                value = part if value is None else jnp.where(is_active(place, holders), part, value)
                first += pieces
            x_out[rows, :] = value.astype(jnp.bfloat16)
            centred = value - jnp.mean(value, axis=-1, keepdims=True)
            variance = jnp.mean(centred * centred, axis=-1, keepdims=True)
            normed = centred * lax.rsqrt(variance + 1e-06)
            modded[rows, :] = (normed * gain + shift).astype(jnp.bfloat16)
        row_a, row_b, _ = neighbour_rows(place, n_th, tile_h)
        low_a, low_b = row_a > 0, row_b > 0
        if n_th % 2:
            low_a, low_b = low_b, low_a
        for start in range(0, 2 * inner, CHUNK):
            projected = jnp.dot(
                modded[...], weight[:, start : start + CHUNK], preferred_element_type=jnp.float32
            )
            for low in range(0, CHUNK, HEAD):
                columns = pl.ds(start + low, HEAD)
                head = projected[:, low : low + HEAD]
                if start < inner:
                    head = head_norm(head)
                head = head.astype(jnp.bfloat16)
                kv[:, columns] = head
                if base == 0:
                    send_a, send_b = refs[3:5]
                    top, bottom = head[:strip_row], head[strip_row : 2 * strip_row]
                    send_a[:, columns] = jnp.where(low_a, bottom, top)
                    send_b[:, columns] = jnp.where(low_b, bottom, top)


def together(parts, columns):
    if len(parts) == 1:
        return parts[0][:, columns]
    return jnp.concatenate([part[:, columns] for part in parts], axis=0)


def masked(mask_ref, tile_h, edge):
    sides, keys = mask_ref.shape
    rows = [jnp.broadcast_to(mask_ref[s : s + 1, :], (edge, keys)) for s in range(sides)]
    return jnp.concatenate(rows * tile_h, axis=0)


def weigh(queries, keys, values, mask):
    scores = [
        lax.dot_general(query, key, (((1,), (1,)), ((), ())), preferred_element_type=jnp.float32)
        for query, key in zip(queries, keys)
    ]
    weights = [
        (jnp.exp2(score * (1.0 / (math.sqrt(HEAD) * math.log(2.0)))) * mask).astype(jnp.bfloat16) for score in scores
    ]
    ones = jnp.ones((values[0].shape[0], HEAD), jnp.bfloat16)
    both = [
        jnp.dot(w, jnp.concatenate([v, ones], axis=1), preferred_element_type=jnp.float32)
        for w, v in zip(weights, values)
    ]
    return [b[:, :HEAD] for b in both], [b[:, HEAD:] for b in both]


def groups(inner):
    heads = [pl.ds(low, HEAD) for low in range(0, inner, HEAD)]
    return [heads[low : low + GROUP] for low in range(0, len(heads), GROUP)]


def first_key_value_kernel(live, spec, sources, chosen, place, qkv, *refs):
    loaded, scratch, sem = refs[-4], refs[-3:-1], refs[-1]
    width = loaded.shape[1]
    copy = pltpu.make_async_copy(qkv.at[:, pl.ds(0, width)], loaded, sem.at[0])
    copy.start()
    key_value_kernel(live, spec, sources, chosen, place, *refs[:-4], *scratch)
    copy.wait()


def first_query_kernel(live, spec, passes, place, *refs):
    tokens = 2 * passes + 1
    sides, tokens, refs = spec[0], refs[:tokens], refs[tokens:]
    patterns, tables, out_weight = refs[:sides], refs[sides : sides + 2], refs[sides + 2]
    queries, top, bottom, own_mask, extra_mask, loaded, sem = refs[sides + 3 :]
    copy = pltpu.make_async_copy(out_weight, loaded, sem.at[0])
    copy.start()
    write_masks(spec, place, patterns, tables, (own_mask, extra_mask))
    query_kernel(live, spec, passes, place, *tokens, own_mask, queries, top, bottom)
    copy.wait()


def second_query_kernel(live, spec, passes, place, *refs):
    tokens = 2 * passes + 1
    sides, tokens, refs = spec[0], refs[:tokens], refs[tokens:]
    patterns, tables, refs = refs[:sides], refs[sides : sides + 2], refs[sides + 2 :]
    queries, top, bottom, own_mask, extra_mask = refs
    write_masks(spec, place, patterns, tables, (own_mask, extra_mask))
    query_kernel(live, spec, passes, place, *tokens, own_mask, queries, top, bottom)


def query_kernel(live, spec, passes, place, *refs):
    modded, kv, refs = refs[:passes], refs[passes : 2 * passes], refs[2 * passes :]
    weight, mask_ref, queries, top, bottom = refs
    sides, tile_h = spec[:2]
    rows, inner = queries.shape

    @pl.when(is_active(place, live))
    def _():
        mask = masked(mask_ref, tile_h, rows // (sides * tile_h))
        tokens = together(modded, slice(None))
        found = []
        for start in range(0, inner, CHUNK):
            projected = jnp.dot(
                tokens, weight[:, start : start + CHUNK], preferred_element_type=jnp.float32
            )
            for low in range(0, CHUNK, HEAD):
                query = head_norm(projected[:, low : low + HEAD]).astype(jnp.bfloat16)
                found.append(query)
                queries[:, start + low : start + low + HEAD] = query
        for group in groups(inner):
            above, below = weigh(
                [found[columns.start // HEAD] for columns in group],
                [together(kv, columns) for columns in group],
                [together(kv, pl.ds(inner + columns.start, HEAD)) for columns in group],
                mask,
            )
            for index, columns in enumerate(group):
                top[:, columns] = above[index]
                bottom[:, columns] = below[index]


def output_kernel(live, spec, extra_count, passes, place, *refs):
    extras, refs = refs[:extra_count], refs[extra_count:]
    (queries, top, bottom, mask_ref), refs = refs[:4], refs[4:]
    x, (mod, weight), refs = refs[:passes], refs[passes : passes + 2], refs[passes + 2 :]
    outs, (attended, turned) = refs[:-2], refs[-2:]
    sides, tile_h, _, n_th, _ = spec
    inner, width = weight.shape
    edge = queries.shape[0] // (sides * tile_h)

    @pl.when(is_active(place, live))
    def _():
        mask = masked(mask_ref, tile_h, edge)
        valid = neighbour_rows(place, n_th, tile_h)[2]

        def received(columns):
            pieces = []
            for index, extra in enumerate(extras):
                piece = extra[:, columns]
                if index < 2:
                    piece = jnp.where(valid[index], piece, jnp.zeros_like(piece))
                pieces.append(piece)
            return jnp.concatenate(pieces, axis=0)

        for heads in groups(inner):
            above, below = weigh(
                [queries[:, columns] for columns in heads],
                [received(columns) for columns in heads],
                [received(pl.ds(inner + columns.start, HEAD)) for columns in heads],
                mask,
            )
            for index, columns in enumerate(heads):
                total = (top[:, columns] + above[index]) / (bottom[:, columns] + below[index])
                attended[:, columns] = total.astype(jnp.bfloat16)
        for start in range(0, width, CHUNK):
            columns = pl.ds(start, CHUNK)
            projected = jnp.dot(
                attended[...], weight[:, start : start + CHUNK], preferred_element_type=jnp.float32
            )
            updated = together(x, columns).astype(jnp.float32)
            updated += mod[2:3, start : start + CHUNK] * projected
            first = 0
            for y in outs:
                if len(y.shape) == 2:
                    y[:, columns] = updated[first : first + y.shape[0]].astype(jnp.bfloat16)
                    first += y.shape[0]
            for side, y in enumerate([y for y in outs if len(y.shape) == 3]):
                for low in range(0, CHUNK, HEAD):
                    lanes = turned.at[(side * CHUNK + low) // HEAD]
                    for index, row in enumerate(row_order(tile_h)):
                        first = (index * sides + side) * edge
                        lanes[pl.ds(row, edge, stride=tile_h), :] = updated[
                            first : first + edge, low : low + HEAD
                        ]
                    tile = lanes[...].reshape(*y.shape[:2], HEAD).astype(jnp.bfloat16)
                    y[:, :, pl.ds(start + low, HEAD)] = tile


def choose_kernel(wanted, place, *refs):
    pieces, out, sem = refs[:-2], refs[-2], refs[-1]
    rows = out.shape[0] // len(wanted)
    for index, options in enumerate(wanted):
        for segment, lane, sides, source in options:

            @pl.when((place[SEG] == segment) & (place[COL] % sides == lane))
            def _(index=index, source=source):
                copy = pltpu.make_async_copy(
                    pieces[source], out.at[pl.ds(index * rows, rows)], sem.at[0]
                )
                copy.start()
                copy.wait()


def gather_copies(place, order, tokens, outs, wanted, sides, sems):
    copies = []
    for slot, (out, (base, other)) in enumerate(zip(outs, wanted)):
        patch = base + (place[COL] + other) % sides
        rows = out.shape[0] // FRAME_PATCH
        for frame in range(FRAME_PATCH):
            source = order[patch * FRAME_PATCH + frame]
            copies.append(
                pltpu.make_async_copy(
                    tokens.at[pl.ds(source * rows, rows)],
                    out.at[pl.ds(frame * rows, rows)],
                    sems.at[slot, frame],
                )
            )
    for copy in copies:
        copy.start()
    return copies


def gather_kernel(wanted, sides, place, order, tokens, pattern, *refs):
    outs = refs[:-1]
    copies = gather_copies(place, order, tokens, outs, wanted, sides, refs[-1])
    shape = (1,) + outs[0].shape[1:]
    lanes = lax.broadcasted_iota(jnp.int32, shape, 2)
    block = jnp.zeros(shape, jnp.float32)
    for index in range(9):
        block = jnp.where(lanes == index, pattern[0, index].astype(jnp.float32), block)
    for out in outs:
        out[out.shape[0] - 1 :] = block.astype(jnp.bfloat16)
    for copy in copies:
        copy.wait()


def load_kernel(wanted, sides, place, order, tokens, qkv, loaded, *refs):
    outs, frame_sems, sem = refs[:-2], refs[-2], refs[-1]
    columns = loaded.shape[1]
    copy = pltpu.make_async_copy(qkv.at[:, pl.ds(columns // 2, columns)], loaded, sem.at[0])
    copy.start()
    for frame in gather_copies(place, order, tokens, outs, wanted, sides, frame_sems):
        frame.wait()
    copy.wait()


def run(
    kernel,
    scalars,
    operands,
    outs,
    scratch,
    name,
    memory=pltpu.VMEM,
    limit=VMEM_BYTES,
    after=(),
    out_memory=pltpu.VMEM,
    fixed=None,
):
    result, smem = pl.BlockSpec(memory_space=out_memory), pl.BlockSpec(memory_space=pltpu.SMEM)
    if memory is pltpu.HBM:
        operands = [
            o if o.dtype == jnp.int32 else pltpu.with_memory_space_constraint(o, memory)
            for o in operands
        ]
    skipped = len(after)
    in_specs = [pl.BlockSpec(memory_space=pl.ANY)] * skipped + [smem] * len(scalars)
    for operand in operands:
        small = operand.dtype == jnp.int32 and operand.shape[-1] == 9
        large = operand is fixed
        spec = pl.BlockSpec(memory_space=pltpu.HBM if large else memory)
        in_specs.append(smem if small else spec)
    return pl.pallas_call(
        lambda *refs: kernel(tuple(lax.axis_index(a) for a in AXES), *refs[skipped:]),
        out_shape=outs,
        in_specs=in_specs,
        out_specs=jax.tree.map(lambda _: result, outs),
        scratch_shapes=scratch,
        compiler_params=pltpu.CompilerParams(vmem_limit_bytes=limit),
        cost_estimate=pl.CostEstimate(flops=2**31, bytes_accessed=2**20, transcendentals=0),
        name=name,
    )(*after, *scalars, *operands)


def arrays(*shapes):
    return tuple(jax.ShapeDtypeStruct(shape, dtype) for shape, dtype in shapes)


def exchange(value, partner):
    sizes = [lax.axis_size(axis) for axis in AXES]
    places = [(s, t, w) for s in range(sizes[0]) for t in range(sizes[1]) for w in range(sizes[2])]
    number = {place: index for index, place in enumerate(places)}
    links = [(number[p], number[partner(*p)]) for p in places if partner(*p) in number]
    return lax.ppermute(value, AXES, links)


def on_device(tokens, frame_order, tile_pattern, qkv_weight, out_weight, modulation):
    n_seg, n_th, n_tw = [lax.axis_size(axis) for axis in AXES]
    seg, row_tile, col_tile = [lax.axis_index(axis) for axis in AXES]
    frames, tile_h, tile_w, width = tokens.shape
    inner = out_weight.shape[1]
    patches = frames // FRAME_PATCH
    held_patches = patches // n_seg
    sides = 2 if n_tw % 2 == 0 and patches % 2 == 0 else 1
    rounds = patches // sides
    tile_rows = FRAME_PATCH * tile_h * tile_w
    edge_rows = FRAME_PATCH * tile_w
    strip_rows = sides * tile_rows

    lane = col_tile % sides
    bf16, f32 = jnp.bfloat16, jnp.float32

    def beside(w):
        return w + 1 - 2 * (w % 2)

    def patch_base(turn):
        return (rounds - 1 - turn) * sides

    def token_swap(s, t, w):
        if s == n_seg - 1:
            return (s, t, beside(w))
        return (s, t + 1 - 2 * (t % 2), w) if n_th % 2 == 0 else None

    stored = tokens.transpose(0, 2, 1, 3).reshape(frames * tile_w, tile_h, width)
    tile_shape = ((edge_rows, tile_h, width), bf16)
    theirs, pattern = [], tile_pattern[0]
    patterns = [pattern]
    if sides == 2:
        messages = run(
            functools.partial(gather_kernel, [(patch_base(turn), 1) for turn in range(rounds)], sides),
            [frame_order],
            [stored, pattern],
            arrays(*[((edge_rows + 1, tile_h, width), bf16)] * rounds),
            [pltpu.SemaphoreType.DMA((rounds, FRAME_PATCH))],
            "gather",
            pltpu.HBM,
            2**20,
        )
        theirs = [exchange(message, token_swap) for message in messages]
        patterns.append(exchange(pattern, lambda s, t, w: (s, t, beside(w))))
        messages, qkv_weight = lax.optimization_barrier((messages, qkv_weight))
    wanted = [(patch_base(turn), 0) for turn in range(rounds)]
    kv_w, *tiles = run(
        functools.partial(load_kernel, wanted, sides),
        [frame_order],
        [stored, qkv_weight[0]],
        (pltpu.VMEM((width, 2 * inner), bf16),)
        + arrays(*[tile_shape] * rounds),
        [pltpu.SemaphoreType.DMA((rounds, FRAME_PATCH)), pltpu.SemaphoreType.DMA((1,))],
        "load_weights",
        pltpu.HBM,
        2**20,
    )
    kv_w = pltpu.with_memory_space_constraint(kv_w, pltpu.VMEM)
    fresh = [[tiles[turn]] + ([theirs[turn]] if sides == 2 else []) for turn in range(rounds)]
    stored_qkv, stored_out = [
        pltpu.with_memory_space_constraint(w[0], pltpu.HBM) for w in (qkv_weight, out_weight)
    ]
    mod = modulation[0]

    side_halo = n_tw > sides
    order = row_order(tile_h)
    grid = np.indices((tile_h, sides, FRAME_PATCH, tile_w)).reshape(4, -1)
    own_table = np.stack([grid[1], 0 * grid[1], grid[3], np.asarray(order)[grid[0]]])
    strip_edge = np.indices((sides, FRAME_PATCH, tile_w)).reshape(3, -1)
    extra = [
        np.stack([strip_edge[0], 0 * strip_edge[0] + kind, strip_edge[2], 0 * strip_edge[0]])
        for kind in (1, 2)
    ]
    if side_halo:
        tall = np.repeat(np.arange(-HALO, tile_h + HALO), FRAME_PATCH)
        extra += [np.stack([0 * tall, 0 * tall + kind, 0 * tall, tall]) for kind in (3, 4)]
    tables = [jnp.asarray(t, jnp.int32) for t in (own_table, np.concatenate(extra, axis=1))]

    first = {n_seg - 1: 0}
    for s in range(n_seg - 1, 0, -1):
        first[s - 1] = first[s] + (1 if s % 2 else 2)
    steps = first[0] + rounds
    spec = (sides, tile_h, tile_w, n_th, n_tw)
    paired_rows, paired_segs = n_th % 2 == 0, n_seg % 2 == 0

    def running(step):
        return [s for s in range(n_seg) if 0 <= step - first[s] < rounds]

    def sources_of(step):
        live = running(step)
        found = []
        if n_seg - 1 in live:
            found.append(("fresh", [n_seg - 1]))
        near_to = [s for s in live if s % 2 == 0 and s != n_seg - 1]
        far_to = [s for s in live if s % 2 == 1 and s != n_seg - 1]
        return found + [("near", near_to)] * bool(near_to) + [("far", far_to)] * bool(far_to)

    def spare(live, s, t, w):
        if paired_segs and s ^ 1 not in live:
            return (s ^ 1, t, w)
        return (s, t, beside(w)) if n_tw % 2 == 0 else None

    def rows_a(live):
        def partner(s, t, w):
            if not paired_rows:
                return (s, t + 1, w)
            return (s, t + 1 - 2 * (t % 2), w) if s in live else spare(live, s, t, w)

        return partner

    def rows_b(live):
        def partner(s, t, w):
            other = t - 1 + 2 * (t % 2) if paired_rows else t - 1
            if paired_rows and not 0 <= other < n_th:
                return (s ^ 1, t, w) if paired_segs else None
            if s in live or not paired_rows:
                return (s, other, w)
            if live == [n_seg - 1] and n_seg == 4:
                return (3 - s, t, w) if s in (1, 2) else (s, t, beside(w))
            return spare(live, s, t, w)

        return partner

    def near_hop(s, t, w):
        return (s ^ 1, t, w) if paired_segs else (s - 1, t, w) if s % 2 else None

    def far_hop(s, t, w):
        return (s - 1, t, w) if s % 2 == 0 and s > 0 else None

    def far_swap(s, t, w):
        return (s + 1, t, w) if s % 2 and s < n_seg - 1 else far_hop(s, t, w)

    def edge_column(kv, above, below, which):
        shape = (-1, sides, FRAME_PATCH, tile_w, 2 * inner)
        rows = jnp.concatenate(kv, axis=0).reshape(shape)
        edge, middle = rows[:2], rows[2:]
        ends = [part.reshape(shape) for part in (above, below)]
        tall = jnp.concatenate([ends[0], edge[:1], middle, edge[1:], ends[1]], axis=0)
        if which == 0:
            column = jnp.where(lane == 0, tall[:, 0, :, 0], tall[:, sides - 1, :, 0])
        else:
            column = jnp.where(lane == 0, tall[:, sides - 1, :, -1], tall[:, 0, :, -1])
        return column.reshape(-1, 2 * inner)

    kept = []

    def layer(step, live, sources, before):
        strip, edges = strip_rows, sides * edge_rows

        def key_value(chosen, sends, **rest):
            rows = len(chosen) * edges
            operands, counts = [], []
            for holders, source in sources:
                if source[0].ndim == 2 and len(chosen) < tile_h:
                    source = source[:1] if chosen[0] == 0 else source[1:]
                operands += source
                counts.append((holders, len(source)))
            operands += [mod, kv_w]
            outs = [((rows, width), bf16), ((rows, width), bf16), ((rows, 2 * inner), bf16)]
            native = any(part.ndim == 3 for part in operands)
            turn = [((width // HEAD, tile_rows, HEAD), f32), ((rows, width), f32)] * native
            return run(
                functools.partial(rest.pop("kernel"), live, spec, counts, chosen),
                [],
                rest.pop("first", []) + operands,
                arrays(*outs, *[((edges, 2 * inner), bf16)] * sends) + rest.pop("more", ()),
                [pltpu.VMEM(shape, kind) for shape, kind in turn] + rest.pop("scratch", []),
                "key_value",
                **rest,
            )

        passes = [order[:2], order[2:]] if 0 < step < steps - 1 else [order]
        x, modded, kv = [], [], []
        if step == 0:
            *found, send_a, send_b, q_w = key_value(
                order,
                2,
                kernel=first_key_value_kernel,
                first=[stored_qkv],
                more=(pltpu.VMEM((width, inner), bf16),),
                scratch=[pltpu.SemaphoreType.DMA((1,))],
                fixed=stored_qkv,
            )
            kept.append(pltpu.with_memory_space_constraint(q_w, pltpu.VMEM))
            for held, part in zip((x, modded, kv), found):
                held.append(part)
        else:
            for index, chosen in enumerate(passes):
                found = key_value(
                    chosen,
                    0 if index else 2,
                    kernel=key_value_kernel,
                    after=[send_a] if index else before,
                )
                for held, part in zip((x, modded, kv), found):
                    held.append(part)
                if not index:
                    send_a, send_b = found[3:]
        tokens = modded + kv
        count = len(passes)
        extra_a = exchange(send_a, rows_a(live))
        extra_b = exchange(send_b, rows_b(live))
        outs = arrays(((strip, inner), bf16), ((strip, inner), f32), ((strip, inner), f32))
        if step == 0:
            made = arrays(*[((sides, table.shape[1]), f32) for table in tables])
            queries, top, bottom, own_mask, extra_mask, out_w = run(
                functools.partial(first_query_kernel, live, spec, count),
                [],
                tokens + [kept[0], pattern] + fresh[0][1:] + tables + [stored_out],
                outs + made + (pltpu.VMEM((inner, width), bf16),),
                [pltpu.SemaphoreType.DMA((1,))],
                "query",
                fixed=stored_out,
            )
            out_w = pltpu.with_memory_space_constraint(out_w, pltpu.VMEM)
            kept.extend([own_mask, extra_mask, out_w])
        elif step == 1:
            made = arrays(*[((sides, table.shape[1]), f32) for table in tables])
            queries, top, bottom, *kept[1:3] = run(
                functools.partial(second_query_kernel, live, spec, count),
                [],
                tokens + [kept[0]] + patterns + tables,
                outs + made,
                [],
                "query",
            )
        else:
            queries, top, bottom = run(
                functools.partial(query_kernel, live, spec, count),
                [],
                tokens + kept[:2],
                outs,
                [],
                "query",
            )
        extra_mask, out_w = kept[2:]
        extras = [extra_a, extra_b]
        if side_halo:
            flip = (row_tile % 2 == 1) if paired_rows else jnp.array(True)
            above = jnp.where(flip, extra_a, extra_b)
            below = jnp.where(flip, extra_b, extra_a)
            above = jnp.where(row_tile > 0, above, jnp.zeros_like(above))
            below = jnp.where(row_tile < n_th - 1, below, jnp.zeros_like(below))
            left = edge_column(kv, above, below, 0)
            right = edge_column(kv, above, below, 1)
            from_left = exchange(right, lambda s, t, w: (s, t, w + sides))
            from_right = exchange(left, lambda s, t, w: (s, t, w - sides))
            extras.append(jnp.concatenate([from_left, from_right], axis=0))
        shapes = [((2 * edges, width), bf16), ((strip - 2 * edges, width), bf16)]
        shapes = shapes * (live != [0]) + [tile_shape] * (sides * (0 in live))
        found = run(
            functools.partial(output_kernel, live, spec, len(extras), count),
            [],
            extras + [queries, top, bottom, extra_mask] + x + [mod, out_w],
            arrays(*shapes),
            [pltpu.VMEM((strip, inner), bf16), pltpu.VMEM((sides * CHUNK // HEAD, tile_rows, HEAD), f32)],
            "output",
            after=[turn[-1] for turn in fresh[1:]] if step == 0 and sides == 2 else (),
        )
        return (found[:2], found[2:]) if live != [0] else ((), found)

    def owner_of(turn, w):
        return (patch_base(turn) + w % sides) // held_patches

    near = far = far_next = None
    finished = {}
    y = ()
    for step in range(steps):
        live = running(step)
        options = {"near": near, "far": far}
        if step < rounds:
            options["fresh"] = fresh[step]
        found = [(holders, options[kind]) for kind, holders in sources_of(step)]
        y, finals = layer(step, live, found, y)
        near, far, far_next = None, far_next, None
        if any(s % 2 == 1 for s in live):
            near = [exchange(part, near_hop) for part in y]
        if any(s % 2 == 0 and s > 0 for s in live):
            far_next = [exchange(y[0], far_hop), exchange(y[1], far_swap)]
        if 0 in live:
            turn = step - first[0]
            finished[turn] = [None] * sides
            for side in reversed(range(sides)):
                finished[turn][side] = exchange(
                    finals[side],
                    lambda s, t, w: (owner_of(turn, w), t, beside(w) if side else w)
                    if s == 0
                    else None,
                )
    wanted = []
    for held in range(held_patches):
        options = []
        for owner in range(n_seg):
            patch = owner * held_patches + held
            turn, member = rounds - 1 - patch // sides, patch % sides
            for w in range(sides):
                options.append((owner, w, sides, turn * sides + (0 if w == member else 1)))
        wanted.append(options)
    (chosen,) = run(
        functools.partial(choose_kernel, wanted),
        [],
        [piece for turn in range(rounds) for piece in finished[turn]],
        arrays(((held_patches * edge_rows, tile_h, width), bf16)),
        [pltpu.SemaphoreType.DMA((1,))],
        "choose",
        pl.ANY,
        out_memory=pl.ANY,
    )
    shaped = chosen.reshape(held_patches * FRAME_PATCH, tile_w, tile_h, width)
    return shaped.transpose(0, 2, 1, 3)


def solution(mesh):
    in_specs = (
        P(None, "th", "tw", None),
        P(),
        P("th", "tw", None),
        P("segment", None, None),
        P("segment", None, None),
        P("segment", None, None),
    )
    out_specs = P("segment", "th", "tw", None)
    return jax.shard_map(
        on_device, mesh=mesh, in_specs=in_specs, out_specs=out_specs, check_vma=False
    )
```

```python
import functools
import math

import jax
import jax.numpy as jnp
import numpy as np
from jax import lax
from jax.experimental import pallas as pl
from jax.experimental.pallas import tpu as pltpu
from jax.sharding import PartitionSpec as P

HEAD = 128
HALO = 1
FRAME_PATCH = 4
CHUNK = 512
BLOCK = 16
GROUP = 12
VMEM_BYTES = 10 * 2**20
AXES = ("segment", "th", "tw")
SEG, ROW, COL = range(3)


def head_norm(values):
    mean_square = jnp.mean(values * values, axis=-1, keepdims=True)
    return values * lax.rsqrt(mean_square + 1e-06)


def is_active(place, live):
    return functools.reduce(jnp.logical_or, [place[SEG] == s for s in live])


def neighbour_rows(place, n_th, tile_h):
    below_first = place[ROW] % 2 == 0 if n_th % 2 == 0 else place[ROW] < 0
    row_a = jnp.where(below_first, tile_h, -1)
    row_b = jnp.where(below_first, -1, tile_h)
    valid = []
    for row in (row_a, row_b):
        tile = place[ROW] + jnp.where(row < 0, -1, 1)
        valid.append((tile >= 0) & (tile < n_th))
    return row_a, row_b, valid


def write_masks(spec, place, patterns, tables, outs):
    sides, tile_h, tile_w, n_th, n_tw = spec
    row_a, row_b, _ = neighbour_rows(place, n_th, tile_h)
    lane = place[COL] % sides
    for table, out in zip(tables, outs):
        side, kind = table[0:1, :], table[1:2, :]
        col, row = table[2:3, :], table[3:4, :]
        row = jnp.where(kind == 1, row_a, jnp.where(kind == 2, row_b, row))
        for query_side in range(sides):
            spot = lane if query_side == 0 else 1 - lane
            tile_col = place[COL] - lane + spot
            cols = (side - query_side) * (1 - 2 * lane) * tile_w + col
            cols = jnp.where(kind == 3, -1 - spot * tile_w, cols)
            cols = jnp.where(kind == 4, (sides - spot) * tile_w, cols)
            block = (
                ((row >= 0).astype(jnp.int32) + (row >= tile_h).astype(jnp.int32)) * 3
                + (cols >= 0).astype(jnp.int32)
                + (cols >= tile_w).astype(jnp.int32)
            )
            flag = jnp.zeros(block.shape, jnp.float32)
            for index in range(9):
                pattern = patterns[query_side]
                if len(pattern.shape) == 3:
                    last = pattern.shape[0] - 1
                    value = pattern[last, 0:1, index : index + 1].astype(jnp.float32)
                else:
                    value = pattern[0, index].astype(jnp.float32)
                flag = jnp.where(block == index, value, flag)
            grid_row, grid_col = row + place[ROW] * tile_h, cols + tile_col * tile_w
            inside = (grid_row >= 0) & (grid_row < n_th * tile_h)
            inside &= (grid_col >= 0) & (grid_col < n_tw * tile_w)
            inside &= (cols >= -HALO) & (cols < tile_w + HALO)
            out[query_side : query_side + 1, :] = jnp.where(inside, flag, 0.0)


def row_order(tile_h):
    return [0, tile_h - 1] + list(range(1, tile_h - 1))


def key_value_kernel(live, spec, sources, chosen, place, *refs):
    sides, tile_h, _, n_th, _ = spec
    count = sum(pieces for _, pieces in sources)
    parts, (mod, weight), refs = refs[:count], refs[count : count + 2], refs[count + 2 :]
    x_out, modded, kv = refs[:3]
    inner = kv.shape[1] // 2
    order = row_order(tile_h)
    strip_row = kv.shape[0] // len(chosen)
    base = order.index(chosen[0]) * strip_row

    @pl.when(is_active(place, live))
    def _():
        first = 0
        for holders, pieces in sources:
            if len(parts[first].shape) == 3:
                tile, turned = refs[-2:]

                @pl.when(is_active(place, holders))
                def _(first=first):
                    edge = strip_row // sides
                    for side in range(sides):
                        frames = parts[first + side][: edge].astype(jnp.float32)
                        frames = frames.reshape(tile.shape[1], turned.shape[1])
                        for low in range(0, turned.shape[1], HEAD):
                            lanes = tile.at[low // HEAD]
                            lanes[...] = frames[:, low : low + HEAD]
                            for index, row in enumerate(chosen):
                                start = index * strip_row + side * edge
                                turned[start : start + edge, low : low + HEAD] = lanes[
                                    pl.ds(row, edge, stride=tile_h), :
                                ]

            first += pieces
        gain, shift = 1.0 + mod[1:2, :], mod[0:1, :]
        for start in range(0, kv.shape[0], BLOCK):
            rows = slice(start, start + BLOCK)
            value, first = None, 0
            for holders, pieces in sources:
                if len(parts[first].shape) == 3:
                    part = turned[rows, :]
                else:
                    index, within = divmod(start, parts[first].shape[0])
                    part = parts[first + index][within : within + BLOCK, :].astype(jnp.float32)
                value = part if value is None else jnp.where(is_active(place, holders), part, value)
                first += pieces
            x_out[rows, :] = value.astype(jnp.bfloat16)
            centred = value - jnp.mean(value, axis=-1, keepdims=True)
            variance = jnp.mean(centred * centred, axis=-1, keepdims=True)
            normed = centred * lax.rsqrt(variance + 1e-06)
            modded[rows, :] = (normed * gain + shift).astype(jnp.bfloat16)
        row_a, row_b, _ = neighbour_rows(place, n_th, tile_h)
        low_a, low_b = row_a > 0, row_b > 0
        if n_th % 2:
            low_a, low_b = low_b, low_a
        for start in range(0, 2 * inner, CHUNK):
            projected = jnp.dot(
                modded[...], weight[:, start : start + CHUNK], preferred_element_type=jnp.float32
            )
            for low in range(0, CHUNK, HEAD):
                columns = pl.ds(start + low, HEAD)
                head = projected[:, low : low + HEAD]
                if start < inner:
                    head = head_norm(head)
                head = head.astype(jnp.bfloat16)
                kv[:, columns] = head
                if base == 0:
                    send_a, send_b = refs[3:5]
                    top, bottom = head[:strip_row], head[strip_row : 2 * strip_row]
                    send_a[:, columns] = jnp.where(low_a, bottom, top)
                    send_b[:, columns] = jnp.where(low_b, bottom, top)


def together(parts, columns):
    if len(parts) == 1:
        return parts[0][:, columns]
    return jnp.concatenate([part[:, columns] for part in parts], axis=0)


def masked(mask_ref, tile_h, edge):
    sides, keys = mask_ref.shape
    rows = [jnp.broadcast_to(mask_ref[s : s + 1, :], (edge, keys)) for s in range(sides)]
    return jnp.concatenate(rows * tile_h, axis=0)


def weigh(queries, keys, values, mask):
    scores = [
        lax.dot_general(query, key, (((1,), (1,)), ((), ())), preferred_element_type=jnp.float32)
        for query, key in zip(queries, keys)
    ]
    weights = [
        (jnp.exp2(score * (1.0 / (math.sqrt(HEAD) * math.log(2.0)))) * mask).astype(jnp.bfloat16) for score in scores
    ]
    ones = jnp.ones((values[0].shape[0], HEAD), jnp.bfloat16)
    both = [
        jnp.dot(w, jnp.concatenate([v, ones], axis=1), preferred_element_type=jnp.float32)
        for w, v in zip(weights, values)
    ]
    return [b[:, :HEAD] for b in both], [b[:, HEAD:] for b in both]


def groups(inner):
    heads = [pl.ds(low, HEAD) for low in range(0, inner, HEAD)]
    return [heads[low : low + GROUP] for low in range(0, len(heads), GROUP)]


def first_key_value_kernel(live, spec, sources, chosen, place, qkv, *refs):
    loaded, scratch, sem = refs[-4], refs[-3:-1], refs[-1]
    width = loaded.shape[1]
    copy = pltpu.make_async_copy(qkv.at[:, pl.ds(0, width)], loaded, sem.at[0])
    copy.start()
    key_value_kernel(live, spec, sources, chosen, place, *refs[:-4], *scratch)
    copy.wait()


def first_query_kernel(live, spec, passes, place, *refs):
    tokens = 2 * passes + 1
    sides, tokens, refs = spec[0], refs[:tokens], refs[tokens:]
    patterns, tables, out_weight = refs[:sides], refs[sides : sides + 2], refs[sides + 2]
    queries, top, bottom, own_mask, extra_mask, loaded, sem = refs[sides + 3 :]
    copy = pltpu.make_async_copy(out_weight, loaded, sem.at[0])
    copy.start()
    write_masks(spec, place, patterns, tables, (own_mask, extra_mask))
    query_kernel(live, spec, passes, place, *tokens, own_mask, queries, top, bottom)
    copy.wait()


def second_query_kernel(live, spec, passes, place, *refs):
    tokens = 2 * passes + 1
    sides, tokens, refs = spec[0], refs[:tokens], refs[tokens:]
    patterns, tables, refs = refs[:sides], refs[sides : sides + 2], refs[sides + 2 :]
    queries, top, bottom, own_mask, extra_mask = refs
    write_masks(spec, place, patterns, tables, (own_mask, extra_mask))
    query_kernel(live, spec, passes, place, *tokens, own_mask, queries, top, bottom)


def query_kernel(live, spec, passes, place, *refs):
    modded, kv, refs = refs[:passes], refs[passes : 2 * passes], refs[2 * passes :]
    weight, mask_ref, queries, top, bottom = refs
    sides, tile_h = spec[:2]
    rows, inner = queries.shape

    @pl.when(is_active(place, live))
    def _():
        mask = masked(mask_ref, tile_h, rows // (sides * tile_h))
        tokens = together(modded, slice(None))
        found = []
        for start in range(0, inner, CHUNK):
            projected = jnp.dot(
                tokens, weight[:, start : start + CHUNK], preferred_element_type=jnp.float32
            )
            for low in range(0, CHUNK, HEAD):
                query = head_norm(projected[:, low : low + HEAD]).astype(jnp.bfloat16)
                found.append(query)
                queries[:, start + low : start + low + HEAD] = query
        for group in groups(inner):
            above, below = weigh(
                [found[columns.start // HEAD] for columns in group],
                [together(kv, columns) for columns in group],
                [together(kv, pl.ds(inner + columns.start, HEAD)) for columns in group],
                mask,
            )
            for index, columns in enumerate(group):
                top[:, columns] = above[index]
                bottom[:, columns] = below[index]


def output_kernel(live, spec, extra_count, passes, place, *refs):
    extras, refs = refs[:extra_count], refs[extra_count:]
    (queries, top, bottom, mask_ref), refs = refs[:4], refs[4:]
    x, (mod, weight), refs = refs[:passes], refs[passes : passes + 2], refs[passes + 2 :]
    outs, (attended, turned) = refs[:-2], refs[-2:]
    sides, tile_h, _, n_th, _ = spec
    inner, width = weight.shape
    edge = queries.shape[0] // (sides * tile_h)

    @pl.when(is_active(place, live))
    def _():
        mask = masked(mask_ref, tile_h, edge)
        valid = neighbour_rows(place, n_th, tile_h)[2]

        def received(columns):
            pieces = []
            for index, extra in enumerate(extras):
                piece = extra[:, columns]
                if index < 2:
                    piece = jnp.where(valid[index], piece, jnp.zeros_like(piece))
                pieces.append(piece)
            return jnp.concatenate(pieces, axis=0)

        for heads in groups(inner):
            above, below = weigh(
                [queries[:, columns] for columns in heads],
                [received(columns) for columns in heads],
                [received(pl.ds(inner + columns.start, HEAD)) for columns in heads],
                mask,
            )
            for index, columns in enumerate(heads):
                total = (top[:, columns] + above[index]) / (bottom[:, columns] + below[index])
                attended[:, columns] = total.astype(jnp.bfloat16)
        for start in range(0, width, CHUNK):
            columns = pl.ds(start, CHUNK)
            projected = jnp.dot(
                attended[...], weight[:, start : start + CHUNK], preferred_element_type=jnp.float32
            )
            updated = together(x, columns).astype(jnp.float32)
            updated += mod[2:3, start : start + CHUNK] * projected
            first = 0
            for y in outs:
                if len(y.shape) == 2:
                    y[:, columns] = updated[first : first + y.shape[0]].astype(jnp.bfloat16)
                    first += y.shape[0]
            for side, y in enumerate([y for y in outs if len(y.shape) == 3]):
                for low in range(0, CHUNK, HEAD):
                    lanes = turned.at[(side * CHUNK + low) // HEAD]
                    for index, row in enumerate(row_order(tile_h)):
                        first = (index * sides + side) * edge
                        lanes[pl.ds(row, edge, stride=tile_h), :] = updated[
                            first : first + edge, low : low + HEAD
                        ]
                    tile = lanes[...].reshape(*y.shape[:2], HEAD).astype(jnp.bfloat16)
                    y[:, :, pl.ds(start + low, HEAD)] = tile


def choose_kernel(wanted, place, *refs):
    pieces, out, sem = refs[:-2], refs[-2], refs[-1]
    rows = out.shape[0] // len(wanted)
    for index, options in enumerate(wanted):
        for segment, lane, sides, source in options:

            @pl.when((place[SEG] == segment) & (place[COL] % sides == lane))
            def _(index=index, source=source):
                copy = pltpu.make_async_copy(
                    pieces[source], out.at[pl.ds(index * rows, rows)], sem.at[0]
                )
                copy.start()
                copy.wait()


def gather_copies(place, order, tokens, outs, wanted, sides, sems):
    copies = []
    for slot, (out, (base, other)) in enumerate(zip(outs, wanted)):
        patch = base + (place[COL] + other) % sides
        rows = out.shape[0] // FRAME_PATCH
        for frame in range(FRAME_PATCH):
            source = order[patch * FRAME_PATCH + frame]
            copies.append(
                pltpu.make_async_copy(
                    tokens.at[pl.ds(source * rows, rows)],
                    out.at[pl.ds(frame * rows, rows)],
                    sems.at[slot, frame],
                )
            )
    for copy in copies:
        copy.start()
    return copies


def gather_kernel(wanted, sides, place, tokens, stored_order, stored_pattern, *refs):
    outs, (order, pattern, small, sems) = refs[:-4], refs[-4:]
    fetches = [
        pltpu.make_async_copy(stored_order, order, small.at[0]),
        pltpu.make_async_copy(stored_pattern, pattern, small.at[1]),
    ]
    for fetch in fetches:
        fetch.start()
    for fetch in fetches:
        fetch.wait()
    copies = gather_copies(place, order, tokens, outs, wanted, sides, sems)
    shape = (1,) + outs[0].shape[1:]
    lanes = lax.broadcasted_iota(jnp.int32, shape, 2)
    block = jnp.zeros(shape, jnp.float32)
    for index in range(9):
        block = jnp.where(lanes == index, pattern[0, index].astype(jnp.float32), block)
    for out in outs:
        out[out.shape[0] - 1 :] = block.astype(jnp.bfloat16)
    for copy in copies:
        copy.wait()


def load_kernel(wanted, sides, place, order, tokens, qkv, loaded, *refs):
    outs, frame_sems, sem = refs[:-2], refs[-2], refs[-1]
    columns = loaded.shape[1]
    copy = pltpu.make_async_copy(qkv.at[:, pl.ds(columns // 2, columns)], loaded, sem.at[0])
    copy.start()
    for frame in gather_copies(place, order, tokens, outs, wanted, sides, frame_sems):
        frame.wait()
    copy.wait()


def run(
    kernel,
    scalars,
    operands,
    outs,
    scratch,
    name,
    memory=pltpu.VMEM,
    limit=VMEM_BYTES,
    after=(),
    out_memory=pltpu.VMEM,
    fixed=None,
):
    result, smem = pl.BlockSpec(memory_space=out_memory), pl.BlockSpec(memory_space=pltpu.SMEM)
    if memory is pltpu.HBM:
        operands = [pltpu.with_memory_space_constraint(o, memory) for o in operands]
    skipped = len(after)
    in_specs = [pl.BlockSpec(memory_space=pl.ANY)] * skipped + [smem] * len(scalars)
    for operand in operands:
        small = operand.dtype == jnp.int32 and operand.shape[-1] == 9 and memory is not pltpu.HBM
        large = operand is fixed
        spec = pl.BlockSpec(memory_space=pltpu.HBM if large else memory)
        in_specs.append(smem if small else spec)
    return pl.pallas_call(
        lambda *refs: kernel(tuple(lax.axis_index(a) for a in AXES), *refs[skipped:]),
        out_shape=outs,
        in_specs=in_specs,
        out_specs=jax.tree.map(lambda _: result, outs),
        scratch_shapes=scratch,
        compiler_params=pltpu.CompilerParams(vmem_limit_bytes=limit),
        cost_estimate=pl.CostEstimate(flops=2**31, bytes_accessed=2**20, transcendentals=0),
        name=name,
    )(*after, *scalars, *operands)


def arrays(*shapes):
    return tuple(jax.ShapeDtypeStruct(shape, dtype) for shape, dtype in shapes)


def exchange(value, partner):
    sizes = [lax.axis_size(axis) for axis in AXES]
    places = [(s, t, w) for s in range(sizes[0]) for t in range(sizes[1]) for w in range(sizes[2])]
    number = {place: index for index, place in enumerate(places)}
    links = [(number[p], number[partner(*p)]) for p in places if partner(*p) in number]
    return lax.ppermute(value, AXES, links)


def on_device(tokens, frame_order, tile_pattern, qkv_weight, out_weight, modulation):
    n_seg, n_th, n_tw = [lax.axis_size(axis) for axis in AXES]
    seg, row_tile, col_tile = [lax.axis_index(axis) for axis in AXES]
    frames, tile_h, tile_w, width = tokens.shape
    inner = out_weight.shape[1]
    patches = frames // FRAME_PATCH
    held_patches = patches // n_seg
    sides = 2 if n_tw % 2 == 0 and patches % 2 == 0 else 1
    rounds = patches // sides
    tile_rows = FRAME_PATCH * tile_h * tile_w
    edge_rows = FRAME_PATCH * tile_w
    strip_rows = sides * tile_rows

    lane = col_tile % sides
    bf16, f32 = jnp.bfloat16, jnp.float32

    def beside(w):
        return w + 1 - 2 * (w % 2)

    def patch_base(turn):
        return (rounds - 1 - turn) * sides

    def token_swap(s, t, w):
        if s == n_seg - 1:
            return (s, t, beside(w))
        return (s, t + 1 - 2 * (t % 2), w) if n_th % 2 == 0 else None

    stored = tokens.transpose(0, 2, 1, 3).reshape(frames * tile_w, tile_h, width)
    tile_shape = ((edge_rows, tile_h, width), bf16)
    theirs, pattern = [], tile_pattern[0]
    patterns = [pattern]
    if sides == 2:
        messages = run(
            functools.partial(gather_kernel, [(patch_base(turn), 1) for turn in range(rounds)], sides),
            [],
            [stored, frame_order, pattern],
            arrays(*[((edge_rows + 1, tile_h, width), bf16)] * rounds),
            [
                pltpu.SMEM(frame_order.shape, jnp.int32),
                pltpu.SMEM(pattern.shape, jnp.int32),
                pltpu.SemaphoreType.DMA((2,)),
                pltpu.SemaphoreType.DMA((rounds, FRAME_PATCH)),
            ],
            "gather",
            pltpu.HBM,
            2**20,
        )
        theirs = [exchange(message, token_swap) for message in messages]
        patterns.append(exchange(pattern, lambda s, t, w: (s, t, beside(w))))
        messages, qkv_weight = lax.optimization_barrier((messages, qkv_weight))
    wanted = [(patch_base(turn), 0) for turn in range(rounds)]
    kv_w, *tiles = run(
        functools.partial(load_kernel, wanted, sides),
        [frame_order],
        [stored, qkv_weight[0]],
        (pltpu.VMEM((width, 2 * inner), bf16),)
        + arrays(*[tile_shape] * rounds),
        [pltpu.SemaphoreType.DMA((rounds, FRAME_PATCH)), pltpu.SemaphoreType.DMA((1,))],
        "load_weights",
        pltpu.HBM,
        2**20,
    )
    kv_w = pltpu.with_memory_space_constraint(kv_w, pltpu.VMEM)
    fresh = [[tiles[turn]] + ([theirs[turn]] if sides == 2 else []) for turn in range(rounds)]
    stored_qkv, stored_out = [
        pltpu.with_memory_space_constraint(w[0], pltpu.HBM) for w in (qkv_weight, out_weight)
    ]
    mod = modulation[0]

    side_halo = n_tw > sides
    order = row_order(tile_h)
    grid = np.indices((tile_h, sides, FRAME_PATCH, tile_w)).reshape(4, -1)
    own_table = np.stack([grid[1], 0 * grid[1], grid[3], np.asarray(order)[grid[0]]])
    strip_edge = np.indices((sides, FRAME_PATCH, tile_w)).reshape(3, -1)
    extra = [
        np.stack([strip_edge[0], 0 * strip_edge[0] + kind, strip_edge[2], 0 * strip_edge[0]])
        for kind in (1, 2)
    ]
    if side_halo:
        tall = np.repeat(np.arange(-HALO, tile_h + HALO), FRAME_PATCH)
        extra += [np.stack([0 * tall, 0 * tall + kind, 0 * tall, tall]) for kind in (3, 4)]
    tables = [jnp.asarray(t, jnp.int32) for t in (own_table, np.concatenate(extra, axis=1))]

    first = {n_seg - 1: 0}
    for s in range(n_seg - 1, 0, -1):
        first[s - 1] = first[s] + (1 if s % 2 else 2)
    steps = first[0] + rounds
    spec = (sides, tile_h, tile_w, n_th, n_tw)
    paired_rows, paired_segs = n_th % 2 == 0, n_seg % 2 == 0

    def running(step):
        return [s for s in range(n_seg) if 0 <= step - first[s] < rounds]

    def sources_of(step):
        live = running(step)
        found = []
        if n_seg - 1 in live:
            found.append(("fresh", [n_seg - 1]))
        near_to = [s for s in live if s % 2 == 0 and s != n_seg - 1]
        far_to = [s for s in live if s % 2 == 1 and s != n_seg - 1]
        return found + [("near", near_to)] * bool(near_to) + [("far", far_to)] * bool(far_to)

    def spare(live, s, t, w):
        if paired_segs and s ^ 1 not in live:
            return (s ^ 1, t, w)
        return (s, t, beside(w)) if n_tw % 2 == 0 else None

    def rows_a(live):
        def partner(s, t, w):
            if not paired_rows:
                return (s, t + 1, w)
            return (s, t + 1 - 2 * (t % 2), w) if s in live else spare(live, s, t, w)

        return partner

    def rows_b(live):
        def partner(s, t, w):
            other = t - 1 + 2 * (t % 2) if paired_rows else t - 1
            if paired_rows and not 0 <= other < n_th:
                return (s ^ 1, t, w) if paired_segs else None
            if s in live or not paired_rows:
                return (s, other, w)
            if live == [n_seg - 1] and n_seg == 4:
                return (3 - s, t, w) if s in (1, 2) else (s, t, beside(w))
            return spare(live, s, t, w)

        return partner

    def near_hop(s, t, w):
        return (s ^ 1, t, w) if paired_segs else (s - 1, t, w) if s % 2 else None

    def far_hop(s, t, w):
        return (s - 1, t, w) if s % 2 == 0 and s > 0 else None

    def far_swap(s, t, w):
        return (s + 1, t, w) if s % 2 and s < n_seg - 1 else far_hop(s, t, w)

    def edge_column(kv, above, below, which):
        shape = (-1, sides, FRAME_PATCH, tile_w, 2 * inner)
        rows = jnp.concatenate(kv, axis=0).reshape(shape)
        edge, middle = rows[:2], rows[2:]
        ends = [part.reshape(shape) for part in (above, below)]
        tall = jnp.concatenate([ends[0], edge[:1], middle, edge[1:], ends[1]], axis=0)
        if which == 0:
            column = jnp.where(lane == 0, tall[:, 0, :, 0], tall[:, sides - 1, :, 0])
        else:
            column = jnp.where(lane == 0, tall[:, sides - 1, :, -1], tall[:, 0, :, -1])
        return column.reshape(-1, 2 * inner)

    kept = []

    def layer(step, live, sources, before):
        strip, edges = strip_rows, sides * edge_rows

        def key_value(chosen, sends, **rest):
            rows = len(chosen) * edges
            operands, counts = [], []
            for holders, source in sources:
                if source[0].ndim == 2 and len(chosen) < tile_h:
                    source = source[:1] if chosen[0] == 0 else source[1:]
                operands += source
                counts.append((holders, len(source)))
            operands += [mod, kv_w]
            outs = [((rows, width), bf16), ((rows, width), bf16), ((rows, 2 * inner), bf16)]
            native = any(part.ndim == 3 for part in operands)
            turn = [((width // HEAD, tile_rows, HEAD), f32), ((rows, width), f32)] * native
            return run(
                functools.partial(rest.pop("kernel"), live, spec, counts, chosen),
                [],
                rest.pop("first", []) + operands,
                arrays(*outs, *[((edges, 2 * inner), bf16)] * sends) + rest.pop("more", ()),
                [pltpu.VMEM(shape, kind) for shape, kind in turn] + rest.pop("scratch", []),
                "key_value",
                **rest,
            )

        passes = [order[:2], order[2:]] if 0 < step < steps - 1 else [order]
        x, modded, kv = [], [], []
        if step == 0:
            *found, send_a, send_b, q_w = key_value(
                order,
                2,
                kernel=first_key_value_kernel,
                first=[stored_qkv],
                more=(pltpu.VMEM((width, inner), bf16),),
                scratch=[pltpu.SemaphoreType.DMA((1,))],
                fixed=stored_qkv,
            )
            kept.append(pltpu.with_memory_space_constraint(q_w, pltpu.VMEM))
            for held, part in zip((x, modded, kv), found):
                held.append(part)
        else:
            for index, chosen in enumerate(passes):
                found = key_value(
                    chosen,
                    0 if index else 2,
                    kernel=key_value_kernel,
                    after=[send_a] if index else before,
                )
                for held, part in zip((x, modded, kv), found):
                    held.append(part)
                if not index:
                    send_a, send_b = found[3:]
        tokens = modded + kv
        count = len(passes)
        extra_a = exchange(send_a, rows_a(live))
        extra_b = exchange(send_b, rows_b(live))
        outs = arrays(((strip, inner), bf16), ((strip, inner), f32), ((strip, inner), f32))
        if step == 0:
            made = arrays(*[((sides, table.shape[1]), f32) for table in tables])
            queries, top, bottom, own_mask, extra_mask, out_w = run(
                functools.partial(first_query_kernel, live, spec, count),
                [],
                tokens + [kept[0], pattern] + fresh[0][1:] + tables + [stored_out],
                outs + made + (pltpu.VMEM((inner, width), bf16),),
                [pltpu.SemaphoreType.DMA((1,))],
                "query",
                fixed=stored_out,
            )
            out_w = pltpu.with_memory_space_constraint(out_w, pltpu.VMEM)
            kept.extend([own_mask, extra_mask, out_w])
        elif step == 1:
            made = arrays(*[((sides, table.shape[1]), f32) for table in tables])
            queries, top, bottom, *kept[1:3] = run(
                functools.partial(second_query_kernel, live, spec, count),
                [],
                tokens + [kept[0]] + patterns + tables,
                outs + made,
                [],
                "query",
            )
        else:
            queries, top, bottom = run(
                functools.partial(query_kernel, live, spec, count),
                [],
                tokens + kept[:2],
                outs,
                [],
                "query",
            )
        extra_mask, out_w = kept[2:]
        extras = [extra_a, extra_b]
        if side_halo:
            flip = (row_tile % 2 == 1) if paired_rows else jnp.array(True)
            above = jnp.where(flip, extra_a, extra_b)
            below = jnp.where(flip, extra_b, extra_a)
            above = jnp.where(row_tile > 0, above, jnp.zeros_like(above))
            below = jnp.where(row_tile < n_th - 1, below, jnp.zeros_like(below))
            left = edge_column(kv, above, below, 0)
            right = edge_column(kv, above, below, 1)
            from_left = exchange(right, lambda s, t, w: (s, t, w + sides))
            from_right = exchange(left, lambda s, t, w: (s, t, w - sides))
            extras.append(jnp.concatenate([from_left, from_right], axis=0))
        shapes = [((2 * edges, width), bf16), ((strip - 2 * edges, width), bf16)]
        shapes = shapes * (live != [0]) + [tile_shape] * (sides * (0 in live))
        found = run(
            functools.partial(output_kernel, live, spec, len(extras), count),
            [],
            extras + [queries, top, bottom, extra_mask] + x + [mod, out_w],
            arrays(*shapes),
            [pltpu.VMEM((strip, inner), bf16), pltpu.VMEM((sides * CHUNK // HEAD, tile_rows, HEAD), f32)],
            "output",
            after=[turn[-1] for turn in fresh[1:]] if step == 0 and sides == 2 else (),
        )
        return (found[:2], found[2:]) if live != [0] else ((), found)

    def owner_of(turn, w):
        return (patch_base(turn) + w % sides) // held_patches

    near = far = far_next = None
    finished = {}
    y = ()
    for step in range(steps):
        live = running(step)
        options = {"near": near, "far": far}
        if step < rounds:
            options["fresh"] = fresh[step]
        found = [(holders, options[kind]) for kind, holders in sources_of(step)]
        y, finals = layer(step, live, found, y)
        near, far, far_next = None, far_next, None
        if any(s % 2 == 1 for s in live):
            near = [exchange(part, near_hop) for part in y]
        if any(s % 2 == 0 and s > 0 for s in live):
            far_next = [exchange(y[0], far_hop), exchange(y[1], far_swap)]
        if 0 in live:
            turn = step - first[0]
            finished[turn] = [None] * sides
            for side in reversed(range(sides)):
                finished[turn][side] = exchange(
                    finals[side],
                    lambda s, t, w: (owner_of(turn, w), t, beside(w) if side else w)
                    if s == 0
                    else None,
                )
    wanted = []
    for held in range(held_patches):
        options = []
        for owner in range(n_seg):
            patch = owner * held_patches + held
            turn, member = rounds - 1 - patch // sides, patch % sides
            for w in range(sides):
                options.append((owner, w, sides, turn * sides + (0 if w == member else 1)))
        wanted.append(options)
    (chosen,) = run(
        functools.partial(choose_kernel, wanted),
        [],
        [piece for turn in range(rounds) for piece in finished[turn]],
        arrays(((held_patches * edge_rows, tile_h, width), bf16)),
        [pltpu.SemaphoreType.DMA((1,))],
        "choose",
        pl.ANY,
        out_memory=pl.ANY,
    )
    shaped = chosen.reshape(held_patches * FRAME_PATCH, tile_w, tile_h, width)
    return shaped.transpose(0, 2, 1, 3)


def solution(mesh):
    in_specs = (
        P(None, "th", "tw", None),
        P(),
        P("th", "tw", None),
        P("segment", None, None),
        P("segment", None, None),
        P("segment", None, None),
    )
    out_specs = P("segment", "th", "tw", None)
    return jax.shard_map(
        on_device, mesh=mesh, in_specs=in_specs, out_specs=out_specs, check_vma=False
    )
```

```python
import functools
import math

import jax
import jax.numpy as jnp
import numpy as np
from jax import lax
from jax.experimental import pallas as pl
from jax.experimental.pallas import tpu as pltpu
from jax.sharding import PartitionSpec as P

HEAD = 128
HALO = 1
FRAME_PATCH = 4
CHUNK = 512
BLOCK = 16
GROUP = 12
VMEM_BYTES = 10 * 2**20
AXES = ("segment", "th", "tw")
SEG, ROW, COL = range(3)


def head_norm(values):
    mean_square = jnp.mean(values * values, axis=-1, keepdims=True)
    return values * lax.rsqrt(mean_square + 1e-06)


def is_active(place, live):
    return functools.reduce(jnp.logical_or, [place[SEG] == s for s in live])


def neighbour_rows(place, n_th, tile_h):
    below_first = place[ROW] % 2 == 0 if n_th % 2 == 0 else place[ROW] < 0
    row_a = jnp.where(below_first, tile_h, -1)
    row_b = jnp.where(below_first, -1, tile_h)
    valid = []
    for row in (row_a, row_b):
        tile = place[ROW] + jnp.where(row < 0, -1, 1)
        valid.append((tile >= 0) & (tile < n_th))
    return row_a, row_b, valid


def write_masks(spec, place, patterns, tables, outs):
    sides, tile_h, tile_w, n_th, n_tw = spec
    row_a, row_b, _ = neighbour_rows(place, n_th, tile_h)
    lane = place[COL] % sides
    for table, out in zip(tables, outs):
        side, kind = table[0:1, :], table[1:2, :]
        col, row = table[2:3, :], table[3:4, :]
        row = jnp.where(kind == 1, row_a, jnp.where(kind == 2, row_b, row))
        for query_side in range(sides):
            spot = lane if query_side == 0 else 1 - lane
            tile_col = place[COL] - lane + spot
            cols = (side - query_side) * (1 - 2 * lane) * tile_w + col
            cols = jnp.where(kind == 3, -1 - spot * tile_w, cols)
            cols = jnp.where(kind == 4, (sides - spot) * tile_w, cols)
            block = (
                ((row >= 0).astype(jnp.int32) + (row >= tile_h).astype(jnp.int32)) * 3
                + (cols >= 0).astype(jnp.int32)
                + (cols >= tile_w).astype(jnp.int32)
            )
            flag = jnp.zeros(block.shape, jnp.float32)
            for index in range(9):
                pattern = patterns[query_side]
                if len(pattern.shape) == 3:
                    last = pattern.shape[0] - 1
                    value = pattern[last, 0:1, index : index + 1].astype(jnp.float32)
                else:
                    value = pattern[0, index].astype(jnp.float32)
                flag = jnp.where(block == index, value, flag)
            grid_row, grid_col = row + place[ROW] * tile_h, cols + tile_col * tile_w
            inside = (grid_row >= 0) & (grid_row < n_th * tile_h)
            inside &= (grid_col >= 0) & (grid_col < n_tw * tile_w)
            inside &= (cols >= -HALO) & (cols < tile_w + HALO)
            out[query_side : query_side + 1, :] = jnp.where(inside, flag, 0.0)


def row_order(tile_h):
    return [0, tile_h - 1] + list(range(1, tile_h - 1))


def key_value_kernel(live, spec, sources, chosen, place, *refs):
    sides, tile_h, _, n_th, _ = spec
    count = sum(pieces for _, pieces in sources)
    parts, (mod, weight), refs = refs[:count], refs[count : count + 2], refs[count + 2 :]
    x_out, modded, kv = refs[:3]
    inner = kv.shape[1] // 2
    order = row_order(tile_h)
    strip_row = kv.shape[0] // len(chosen)
    base = order.index(chosen[0]) * strip_row

    @pl.when(is_active(place, live))
    def _():
        first = 0
        for holders, pieces in sources:
            if len(parts[first].shape) == 3:
                tile, turned = refs[-2:]

                @pl.when(is_active(place, holders))
                def _(first=first):
                    edge = strip_row // sides
                    for side in range(sides):
                        frames = parts[first + side][: edge].astype(jnp.float32)
                        frames = frames.reshape(tile.shape[1], turned.shape[1])
                        for low in range(0, turned.shape[1], HEAD):
                            lanes = tile.at[low // HEAD]
                            lanes[...] = frames[:, low : low + HEAD]
                            for index, row in enumerate(chosen):
                                start = index * strip_row + side * edge
                                turned[start : start + edge, low : low + HEAD] = lanes[
                                    pl.ds(row, edge, stride=tile_h), :
                                ]

            first += pieces
        gain, shift = 1.0 + mod[1:2, :], mod[0:1, :]
        for start in range(0, kv.shape[0], BLOCK):
            rows = slice(start, start + BLOCK)
            value, first = None, 0
            for holders, pieces in sources:
                if len(parts[first].shape) == 3:
                    part = turned[rows, :]
                else:
                    index, within = divmod(start, parts[first].shape[0])
                    part = parts[first + index][within : within + BLOCK, :].astype(jnp.float32)
                value = part if value is None else jnp.where(is_active(place, holders), part, value)
                first += pieces
            x_out[rows, :] = value.astype(jnp.bfloat16)
            centred = value - jnp.mean(value, axis=-1, keepdims=True)
            variance = jnp.mean(centred * centred, axis=-1, keepdims=True)
            normed = centred * lax.rsqrt(variance + 1e-06)
            modded[rows, :] = (normed * gain + shift).astype(jnp.bfloat16)
        row_a, row_b, _ = neighbour_rows(place, n_th, tile_h)
        low_a, low_b = row_a > 0, row_b > 0
        if n_th % 2:
            low_a, low_b = low_b, low_a
        for start in range(0, 2 * inner, CHUNK):
            projected = jnp.dot(
                modded[...], weight[:, start : start + CHUNK], preferred_element_type=jnp.float32
            )
            for low in range(0, CHUNK, HEAD):
                columns = pl.ds(start + low, HEAD)
                head = projected[:, low : low + HEAD]
                if start < inner:
                    head = head_norm(head)
                head = head.astype(jnp.bfloat16)
                kv[:, columns] = head
                if base == 0:
                    send_a, send_b = refs[3:5]
                    top, bottom = head[:strip_row], head[strip_row : 2 * strip_row]
                    send_a[:, columns] = jnp.where(low_a, bottom, top)
                    send_b[:, columns] = jnp.where(low_b, bottom, top)


def together(parts, columns):
    if len(parts) == 1:
        return parts[0][:, columns]
    return jnp.concatenate([part[:, columns] for part in parts], axis=0)


def masked(mask_ref, tile_h, edge):
    sides, keys = mask_ref.shape
    rows = [jnp.broadcast_to(mask_ref[s : s + 1, :], (edge, keys)) for s in range(sides)]
    return jnp.concatenate(rows * tile_h, axis=0)


def weigh(queries, keys, values, mask):
    scores = [
        lax.dot_general(query, key, (((1,), (1,)), ((), ())), preferred_element_type=jnp.float32)
        for query, key in zip(queries, keys)
    ]
    weights = [
        (jnp.exp2(score * (1.0 / (math.sqrt(HEAD) * math.log(2.0)))) * mask).astype(jnp.bfloat16) for score in scores
    ]
    ones = jnp.ones((values[0].shape[0], HEAD), jnp.bfloat16)
    both = [
        jnp.dot(w, jnp.concatenate([v, ones], axis=1), preferred_element_type=jnp.float32)
        for w, v in zip(weights, values)
    ]
    return [b[:, :HEAD] for b in both], [b[:, HEAD:] for b in both]


def groups(inner):
    heads = [pl.ds(low, HEAD) for low in range(0, inner, HEAD)]
    return [heads[low : low + GROUP] for low in range(0, len(heads), GROUP)]


def first_key_value_kernel(live, spec, sources, chosen, place, qkv, *refs):
    loaded, scratch, sem = refs[-4], refs[-3:-1], refs[-1]
    width = loaded.shape[1]
    copy = pltpu.make_async_copy(qkv.at[:, pl.ds(0, width)], loaded, sem.at[0])
    copy.start()
    key_value_kernel(live, spec, sources, chosen, place, *refs[:-4], *scratch)
    copy.wait()


def first_query_kernel(live, spec, passes, place, *refs):
    tokens = 2 * passes + 1
    sides, tokens, refs = spec[0], refs[:tokens], refs[tokens:]
    patterns, tables, out_weight = refs[:sides], refs[sides : sides + 2], refs[sides + 2]
    queries, top, bottom, own_mask, extra_mask, loaded, sem = refs[sides + 3 :]
    copy = pltpu.make_async_copy(out_weight, loaded, sem.at[0])
    copy.start()
    write_masks(spec, place, patterns, tables, (own_mask, extra_mask))
    query_kernel(live, spec, passes, place, *tokens, own_mask, queries, top, bottom)
    copy.wait()


def second_query_kernel(live, spec, passes, place, *refs):
    tokens = 2 * passes + 1
    sides, tokens, refs = spec[0], refs[:tokens], refs[tokens:]
    patterns, tables, refs = refs[:sides], refs[sides : sides + 2], refs[sides + 2 :]
    queries, top, bottom, own_mask, extra_mask = refs
    write_masks(spec, place, patterns, tables, (own_mask, extra_mask))
    query_kernel(live, spec, passes, place, *tokens, own_mask, queries, top, bottom)


def query_kernel(live, spec, passes, place, *refs):
    modded, kv, refs = refs[:passes], refs[passes : 2 * passes], refs[2 * passes :]
    weight, mask_ref, queries, top, bottom = refs
    sides, tile_h = spec[:2]
    rows, inner = queries.shape

    @pl.when(is_active(place, live))
    def _():
        mask = masked(mask_ref, tile_h, rows // (sides * tile_h))
        tokens = together(modded, slice(None))
        found = []
        for start in range(0, inner, CHUNK):
            projected = jnp.dot(
                tokens, weight[:, start : start + CHUNK], preferred_element_type=jnp.float32
            )
            for low in range(0, CHUNK, HEAD):
                query = head_norm(projected[:, low : low + HEAD]).astype(jnp.bfloat16)
                found.append(query)
                queries[:, start + low : start + low + HEAD] = query
        for group in groups(inner):
            above, below = weigh(
                [found[columns.start // HEAD] for columns in group],
                [together(kv, columns) for columns in group],
                [together(kv, pl.ds(inner + columns.start, HEAD)) for columns in group],
                mask,
            )
            for index, columns in enumerate(group):
                top[:, columns] = above[index]
                bottom[:, columns] = below[index]


def output_kernel(live, spec, extra_count, passes, place, *refs):
    extras, refs = refs[:extra_count], refs[extra_count:]
    (queries, top, bottom, mask_ref), refs = refs[:4], refs[4:]
    x, (mod, weight), refs = refs[:passes], refs[passes : passes + 2], refs[passes + 2 :]
    outs, (attended, turned) = refs[:-2], refs[-2:]
    sides, tile_h, _, n_th, _ = spec
    inner, width = weight.shape
    edge = queries.shape[0] // (sides * tile_h)

    @pl.when(is_active(place, live))
    def _():
        mask = masked(mask_ref, tile_h, edge)
        valid = neighbour_rows(place, n_th, tile_h)[2]

        def received(columns):
            pieces = []
            for index, extra in enumerate(extras):
                piece = extra[:, columns]
                if index < 2:
                    piece = jnp.where(valid[index], piece, jnp.zeros_like(piece))
                pieces.append(piece)
            return jnp.concatenate(pieces, axis=0)

        for heads in groups(inner):
            above, below = weigh(
                [queries[:, columns] for columns in heads],
                [received(columns) for columns in heads],
                [received(pl.ds(inner + columns.start, HEAD)) for columns in heads],
                mask,
            )
            for index, columns in enumerate(heads):
                total = (top[:, columns] + above[index]) / (bottom[:, columns] + below[index])
                attended[:, columns] = total.astype(jnp.bfloat16)
        for start in range(0, width, CHUNK):
            columns = pl.ds(start, CHUNK)
            projected = jnp.dot(
                attended[...], weight[:, start : start + CHUNK], preferred_element_type=jnp.float32
            )
            updated = together(x, columns).astype(jnp.float32)
            updated += mod[2:3, start : start + CHUNK] * projected
            first = 0
            for y in outs:
                if len(y.shape) == 2:
                    y[:, columns] = updated[first : first + y.shape[0]].astype(jnp.bfloat16)
                    first += y.shape[0]
            for side, y in enumerate([y for y in outs if len(y.shape) == 3]):
                for low in range(0, CHUNK, HEAD):
                    lanes = turned.at[(side * CHUNK + low) // HEAD]
                    for index, row in enumerate(row_order(tile_h)):
                        first = (index * sides + side) * edge
                        lanes[pl.ds(row, edge, stride=tile_h), :] = updated[
                            first : first + edge, low : low + HEAD
                        ]
                    tile = lanes[...].reshape(*y.shape[:2], HEAD).astype(jnp.bfloat16)
                    y[:, :, pl.ds(start + low, HEAD)] = tile


def choose_kernel(wanted, place, *refs):
    pieces, out, sem = refs[:-2], refs[-2], refs[-1]
    rows = out.shape[0] // len(wanted)
    for index, options in enumerate(wanted):
        for segment, lane, sides, source in options:

            @pl.when((place[SEG] == segment) & (place[COL] % sides == lane))
            def _(index=index, source=source):
                copy = pltpu.make_async_copy(
                    pieces[source], out.at[pl.ds(index * rows, rows)], sem.at[0]
                )
                copy.start()
                copy.wait()


def gather_copies(place, order, tokens, outs, wanted, sides, sems):
    copies = []
    for slot, (out, (base, other)) in enumerate(zip(outs, wanted)):
        patch = base + (place[COL] + other) % sides
        rows = out.shape[0] // FRAME_PATCH
        for frame in range(FRAME_PATCH):
            source = order[patch * FRAME_PATCH + frame]
            copies.append(
                pltpu.make_async_copy(
                    tokens.at[pl.ds(source * rows, rows)],
                    out.at[pl.ds(frame * rows, rows)],
                    sems.at[slot, frame],
                )
            )
    for copy in copies:
        copy.start()
    return copies


def gather_kernel(wanted, sides, place, tokens, stored_order, stored_pattern, *refs):
    outs, (order, pattern, small, sems) = refs[:-4], refs[-4:]
    fetches = [
        pltpu.make_async_copy(stored_order, order, small.at[0]),
        pltpu.make_async_copy(stored_pattern, pattern, small.at[1]),
    ]
    for fetch in fetches:
        fetch.start()
    for fetch in fetches:
        fetch.wait()
    copies = gather_copies(place, order, tokens, outs, wanted, sides, sems)
    shape = (1,) + outs[0].shape[1:]
    lanes = lax.broadcasted_iota(jnp.int32, shape, 2)
    block = jnp.zeros(shape, jnp.float32)
    for index in range(9):
        block = jnp.where(lanes == index, pattern[0, index].astype(jnp.float32), block)
    for out in outs:
        out[out.shape[0] - 1 :] = block.astype(jnp.bfloat16)
    for copy in copies:
        copy.wait()


def load_kernel(wanted, sides, place, order, tokens, qkv, loaded, *refs):
    outs, frame_sems, sem = refs[:-2], refs[-2], refs[-1]
    columns = loaded.shape[1]
    copy = pltpu.make_async_copy(qkv.at[:, pl.ds(columns // 2, columns)], loaded, sem.at[0])
    copy.start()
    for frame in gather_copies(place, order, tokens, outs, wanted, sides, frame_sems):
        frame.wait()
    copy.wait()


def run(
    kernel,
    scalars,
    operands,
    outs,
    scratch,
    name,
    memory=pltpu.VMEM,
    limit=VMEM_BYTES,
    after=(),
    out_memory=pltpu.VMEM,
    fixed=None,
):
    result, smem = pl.BlockSpec(memory_space=out_memory), pl.BlockSpec(memory_space=pltpu.SMEM)
    if memory is pltpu.HBM:
        operands = [pltpu.with_memory_space_constraint(o, memory) for o in operands]
    skipped = len(after)
    in_specs = [pl.BlockSpec(memory_space=pl.ANY)] * skipped + [smem] * len(scalars)
    for operand in operands:
        small = operand.dtype == jnp.int32 and operand.shape[-1] == 9 and memory is not pltpu.HBM
        large = operand is fixed
        spec = pl.BlockSpec(memory_space=pltpu.HBM if large else memory)
        in_specs.append(smem if small else spec)
    return pl.pallas_call(
        lambda *refs: kernel(tuple(lax.axis_index(a) for a in AXES), *refs[skipped:]),
        out_shape=outs,
        in_specs=in_specs,
        out_specs=jax.tree.map(lambda _: result, outs),
        scratch_shapes=scratch,
        compiler_params=pltpu.CompilerParams(vmem_limit_bytes=limit),
        cost_estimate=pl.CostEstimate(flops=2**31, bytes_accessed=2**20, transcendentals=0),
        name=name,
    )(*after, *scalars, *operands)


def arrays(*shapes):
    return tuple(jax.ShapeDtypeStruct(shape, dtype) for shape, dtype in shapes)


def exchange(value, partner):
    sizes = [lax.axis_size(axis) for axis in AXES]
    places = [(s, t, w) for s in range(sizes[0]) for t in range(sizes[1]) for w in range(sizes[2])]
    number = {place: index for index, place in enumerate(places)}
    links = [(number[p], number[partner(*p)]) for p in places if partner(*p) in number]
    return lax.ppermute(value, AXES, links)


def on_device(tokens, frame_order, tile_pattern, qkv_weight, out_weight, modulation):
    n_seg, n_th, n_tw = [lax.axis_size(axis) for axis in AXES]
    seg, row_tile, col_tile = [lax.axis_index(axis) for axis in AXES]
    frames, tile_h, tile_w, width = tokens.shape
    inner = out_weight.shape[1]
    patches = frames // FRAME_PATCH
    held_patches = patches // n_seg
    sides = 2 if n_tw % 2 == 0 and patches % 2 == 0 else 1
    rounds = patches // sides
    tile_rows = FRAME_PATCH * tile_h * tile_w
    edge_rows = FRAME_PATCH * tile_w
    strip_rows = sides * tile_rows

    lane = col_tile % sides
    bf16, f32 = jnp.bfloat16, jnp.float32

    def beside(w):
        return w + 1 - 2 * (w % 2)

    def patch_base(turn):
        return (rounds - 1 - turn) * sides

    def token_swap(s, t, w):
        if s == n_seg - 1:
            return (s, t, beside(w))
        return (s, t + 1 - 2 * (t % 2), w) if n_th % 2 == 0 else None

    stored = tokens.transpose(0, 2, 1, 3).reshape(frames * tile_w, tile_h, width)
    tile_shape = ((edge_rows, tile_h, width), bf16)
    theirs, pattern = [], tile_pattern[0]
    patterns = [pattern]
    if sides == 2:
        messages = run(
            functools.partial(gather_kernel, [(patch_base(turn), 1) for turn in range(rounds)], sides),
            [],
            [stored, frame_order, pattern],
            arrays(*[((edge_rows + 1, tile_h, width), bf16)] * rounds),
            [
                pltpu.SMEM(frame_order.shape, jnp.int32),
                pltpu.SMEM(pattern.shape, jnp.int32),
                pltpu.SemaphoreType.DMA((2,)),
                pltpu.SemaphoreType.DMA((rounds, FRAME_PATCH)),
            ],
            "gather",
            pltpu.HBM,
            2**20,
        )
        theirs = [exchange(message, token_swap) for message in messages]
        patterns.append(exchange(pattern, lambda s, t, w: (s, t, beside(w))))
        messages, qkv_weight = lax.optimization_barrier((messages, qkv_weight))
    wanted = [(patch_base(turn), 0) for turn in range(rounds)]
    kv_w, *tiles = run(
        functools.partial(load_kernel, wanted, sides),
        [frame_order],
        [stored, qkv_weight[0]],
        (pltpu.VMEM((width, 2 * inner), bf16),)
        + arrays(*[tile_shape] * rounds),
        [pltpu.SemaphoreType.DMA((rounds, FRAME_PATCH)), pltpu.SemaphoreType.DMA((1,))],
        "load_weights",
        pltpu.HBM,
        2**20,
    )
    kv_w = pltpu.with_memory_space_constraint(kv_w, pltpu.VMEM)
    fresh = [[tiles[turn]] + ([theirs[turn]] if sides == 2 else []) for turn in range(rounds)]
    stored_qkv, stored_out = [
        pltpu.with_memory_space_constraint(w[0], pltpu.HBM) for w in (qkv_weight, out_weight)
    ]
    mod = modulation[0]

    side_halo = n_tw > sides
    order = row_order(tile_h)
    grid = np.indices((tile_h, sides, FRAME_PATCH, tile_w)).reshape(4, -1)
    own_table = np.stack([grid[1], 0 * grid[1], grid[3], np.asarray(order)[grid[0]]])
    strip_edge = np.indices((sides, FRAME_PATCH, tile_w)).reshape(3, -1)
    extra = [
        np.stack([strip_edge[0], 0 * strip_edge[0] + kind, strip_edge[2], 0 * strip_edge[0]])
        for kind in (1, 2)
    ]
    if side_halo:
        tall = np.repeat(np.arange(-HALO, tile_h + HALO), FRAME_PATCH)
        extra += [np.stack([0 * tall, 0 * tall + kind, 0 * tall, tall]) for kind in (3, 4)]
    tables = [jnp.asarray(t, jnp.int32) for t in (own_table, np.concatenate(extra, axis=1))]

    first = {n_seg - 1: 0}
    for s in range(n_seg - 1, 0, -1):
        first[s - 1] = first[s] + (1 if s % 2 else 2)
    steps = first[0] + rounds
    spec = (sides, tile_h, tile_w, n_th, n_tw)
    paired_rows, paired_segs = n_th % 2 == 0, n_seg % 2 == 0

    def running(step):
        return [s for s in range(n_seg) if 0 <= step - first[s] < rounds]

    def sources_of(step):
        live = running(step)
        found = []
        if n_seg - 1 in live:
            found.append(("fresh", [n_seg - 1]))
        near_to = [s for s in live if s % 2 == 0 and s != n_seg - 1]
        far_to = [s for s in live if s % 2 == 1 and s != n_seg - 1]
        return found + [("near", near_to)] * bool(near_to) + [("far", far_to)] * bool(far_to)

    def spare(live, s, t, w):
        if paired_segs and s ^ 1 not in live:
            return (s ^ 1, t, w)
        return (s, t, beside(w)) if n_tw % 2 == 0 else None

    def rows_a(live):
        def partner(s, t, w):
            if not paired_rows:
                return (s, t + 1, w)
            return (s, t + 1 - 2 * (t % 2), w) if s in live else spare(live, s, t, w)

        return partner

    def rows_b(live):
        def partner(s, t, w):
            other = t - 1 + 2 * (t % 2) if paired_rows else t - 1
            if paired_rows and not 0 <= other < n_th:
                return (s ^ 1, t, w) if paired_segs else None
            if s in live or not paired_rows:
                return (s, other, w)
            if live == [n_seg - 1] and n_seg == 4:
                return (3 - s, t, w) if s in (1, 2) else (s, t, beside(w))
            return spare(live, s, t, w)

        return partner

    def near_hop(s, t, w):
        return (s ^ 1, t, w) if paired_segs else (s - 1, t, w) if s % 2 else None

    def far_hop(s, t, w):
        return (s - 1, t, w) if s % 2 == 0 and s > 0 else None

    def far_swap(s, t, w):
        return (s + 1, t, w) if s % 2 and s < n_seg - 1 else far_hop(s, t, w)

    def edge_column(kv, above, below, which):
        shape = (-1, sides, FRAME_PATCH, tile_w, 2 * inner)
        rows = jnp.concatenate(kv, axis=0).reshape(shape)
        edge, middle = rows[:2], rows[2:]
        ends = [part.reshape(shape) for part in (above, below)]
        tall = jnp.concatenate([ends[0], edge[:1], middle, edge[1:], ends[1]], axis=0)
        if which == 0:
            column = jnp.where(lane == 0, tall[:, 0, :, 0], tall[:, sides - 1, :, 0])
        else:
            column = jnp.where(lane == 0, tall[:, sides - 1, :, -1], tall[:, 0, :, -1])
        return column.reshape(-1, 2 * inner)

    kept = []

    def layer(step, live, sources, before):
        strip, edges = strip_rows, sides * edge_rows

        def key_value(chosen, sends, **rest):
            rows = len(chosen) * edges
            operands, counts = [], []
            for holders, source in sources:
                if source[0].ndim == 2 and len(chosen) < tile_h:
                    source = source[:1] if chosen[0] == 0 else source[1:]
                operands += source
                counts.append((holders, len(source)))
            operands += [mod, kv_w]
            outs = [((rows, width), bf16), ((rows, width), bf16), ((rows, 2 * inner), bf16)]
            native = any(part.ndim == 3 for part in operands)
            turn = [((width // HEAD, tile_rows, HEAD), f32), ((rows, width), f32)] * native
            return run(
                functools.partial(rest.pop("kernel"), live, spec, counts, chosen),
                [],
                rest.pop("first", []) + operands,
                arrays(*outs, *[((edges, 2 * inner), bf16)] * sends) + rest.pop("more", ()),
                [pltpu.VMEM(shape, kind) for shape, kind in turn] + rest.pop("scratch", []),
                "key_value",
                **rest,
            )

        passes = [order[:2], order[2:]] if 0 < step < steps - 1 else [order]
        x, modded, kv = [], [], []
        if step == 0:
            *found, send_a, send_b, q_w = key_value(
                order,
                2,
                kernel=first_key_value_kernel,
                first=[stored_qkv],
                more=(pltpu.VMEM((width, inner), bf16),),
                scratch=[pltpu.SemaphoreType.DMA((1,))],
                fixed=stored_qkv,
            )
            kept.append(pltpu.with_memory_space_constraint(q_w, pltpu.VMEM))
            for held, part in zip((x, modded, kv), found):
                held.append(part)
        else:
            for index, chosen in enumerate(passes):
                found = key_value(
                    chosen,
                    0 if index else 2,
                    kernel=key_value_kernel,
                    after=[send_a] if index else before,
                )
                for held, part in zip((x, modded, kv), found):
                    held.append(part)
                if not index:
                    send_a, send_b = found[3:]
        tokens = modded + kv
        count = len(passes)
        extra_a = exchange(send_a, rows_a(live))
        extra_b = exchange(send_b, rows_b(live))
        outs = arrays(((strip, inner), bf16), ((strip, inner), f32), ((strip, inner), f32))
        if step == 0:
            made = arrays(*[((sides, table.shape[1]), f32) for table in tables])
            queries, top, bottom, own_mask, extra_mask, out_w = run(
                functools.partial(first_query_kernel, live, spec, count),
                [],
                tokens + [kept[0], pattern] + fresh[0][1:] + tables + [stored_out],
                outs + made + (pltpu.VMEM((inner, width), bf16),),
                [pltpu.SemaphoreType.DMA((1,))],
                "query",
                fixed=stored_out,
            )
            out_w = pltpu.with_memory_space_constraint(out_w, pltpu.VMEM)
            kept.extend([own_mask, extra_mask, out_w])
        elif step == 1:
            made = arrays(*[((sides, table.shape[1]), f32) for table in tables])
            queries, top, bottom, *kept[1:3] = run(
                functools.partial(second_query_kernel, live, spec, count),
                [],
                tokens + [kept[0]] + patterns + tables,
                outs + made,
                [],
                "query",
            )
        else:
            queries, top, bottom = run(
                functools.partial(query_kernel, live, spec, count),
                [],
                tokens + kept[:2],
                outs,
                [],
                "query",
            )
        extra_mask, out_w = kept[2:]
        extras = [extra_a, extra_b]
        if side_halo:
            flip = (row_tile % 2 == 1) if paired_rows else jnp.array(True)
            above = jnp.where(flip, extra_a, extra_b)
            below = jnp.where(flip, extra_b, extra_a)
            above = jnp.where(row_tile > 0, above, jnp.zeros_like(above))
            below = jnp.where(row_tile < n_th - 1, below, jnp.zeros_like(below))
            left = edge_column(kv, above, below, 0)
            right = edge_column(kv, above, below, 1)
            from_left = exchange(right, lambda s, t, w: (s, t, w + sides))
            from_right = exchange(left, lambda s, t, w: (s, t, w - sides))
            extras.append(jnp.concatenate([from_left, from_right], axis=0))
        shapes = [((2 * edges, width), bf16), ((strip - 2 * edges, width), bf16)]
        shapes = shapes * (live != [0]) + [tile_shape] * (sides * (0 in live))
        found = run(
            functools.partial(output_kernel, live, spec, len(extras), count),
            [],
            extras + [queries, top, bottom, extra_mask] + x + [mod, out_w],
            arrays(*shapes),
            [pltpu.VMEM((strip, inner), bf16), pltpu.VMEM((sides * CHUNK // HEAD, tile_rows, HEAD), f32)],
            "output",
            after=[turn[-1] for turn in fresh[1:]] if step == 0 and sides == 2 else (),
        )
        return (found[:2], found[2:]) if live != [0] else ((), found)

    def owner_of(turn, w):
        return (patch_base(turn) + w % sides) // held_patches

    def beside_chip(turn):
        return sides == 2 and paired_segs and all(owner_of(turn, w) < 2 for w in range(sides))

    def deliver(turn, tiles):
        sent = [
            exchange(
                tile,
                lambda s, t, w: (owner_of(turn, w), t, beside(w) if side else w)
                if s == 0
                else None,
            )
            for side, tile in enumerate(tiles)
            if side or not beside_chip(turn)
        ]
        if beside_chip(turn):
            return [tiles[0]] + sent + [exchange(tiles[0], near_hop)]
        return sent

    near = far = far_next = None
    finished = {}
    y = ()
    for step in range(steps):
        live = running(step)
        options = {"near": near, "far": far}
        if step < rounds:
            options["fresh"] = fresh[step]
        found = [(holders, options[kind]) for kind, holders in sources_of(step)]
        y, finals = layer(step, live, found, y)
        near, far, far_next = None, far_next, None
        if any(s % 2 == 1 for s in live):
            near = [exchange(part, near_hop) for part in y]
        if any(s % 2 == 0 and s > 0 for s in live):
            far_next = [exchange(y[0], far_hop), exchange(y[1], far_swap)]
        if 0 in live:
            turn = step - first[0]
            finished[turn] = deliver(turn, finals)
    pieces, wanted = [], []
    for held in range(held_patches):
        options = []
        for owner in range(n_seg):
            patch = owner * held_patches + held
            turn, member = rounds - 1 - patch // sides, patch % sides
            base = sum(len(finished[other]) for other in range(turn))
            for w in range(sides):
                own = 2 * owner if beside_chip(turn) else 0
                options.append((owner, w, sides, base + (own if w == member else 1)))
        wanted.append(options)
    for turn in range(rounds):
        pieces += finished[turn]
    (chosen,) = run(
        functools.partial(choose_kernel, wanted),
        [],
        pieces,
        arrays(((held_patches * edge_rows, tile_h, width), bf16)),
        [pltpu.SemaphoreType.DMA((1,))],
        "choose",
        pl.ANY,
        out_memory=pl.ANY,
    )
    shaped = chosen.reshape(held_patches * FRAME_PATCH, tile_w, tile_h, width)
    return shaped.transpose(0, 2, 1, 3)


def solution(mesh):
    in_specs = (
        P(None, "th", "tw", None),
        P(),
        P("th", "tw", None),
        P("segment", None, None),
        P("segment", None, None),
        P("segment", None, None),
    )
    out_specs = P("segment", "th", "tw", None)
    return jax.shard_map(
        on_device, mesh=mesh, in_specs=in_specs, out_specs=out_specs, check_vma=False
    )
```

```python
import functools
import math

import jax
import jax.numpy as jnp
import numpy as np
from jax import lax
from jax.experimental import pallas as pl
from jax.experimental.pallas import tpu as pltpu
from jax.sharding import PartitionSpec as P

HEAD = 128
HALO = 1
FRAME_PATCH = 4
CHUNK = 512
BLOCK = 16
GROUP = 12
VMEM_BYTES = 10 * 2**20
AXES = ("segment", "th", "tw")
SEG, ROW, COL = range(3)


def head_norm(values):
    mean_square = jnp.mean(values * values, axis=-1, keepdims=True)
    return values * lax.rsqrt(mean_square + 1e-06)


def is_active(place, live):
    return functools.reduce(jnp.logical_or, [place[SEG] == s for s in live])


def neighbour_rows(place, n_th, tile_h):
    below_first = place[ROW] % 2 == 0 if n_th % 2 == 0 else place[ROW] < 0
    row_a = jnp.where(below_first, tile_h, -1)
    row_b = jnp.where(below_first, -1, tile_h)
    valid = []
    for row in (row_a, row_b):
        tile = place[ROW] + jnp.where(row < 0, -1, 1)
        valid.append((tile >= 0) & (tile < n_th))
    return row_a, row_b, valid


def write_masks(spec, place, patterns, tables, outs):
    sides, tile_h, tile_w, n_th, n_tw = spec
    row_a, row_b, _ = neighbour_rows(place, n_th, tile_h)
    lane = place[COL] % sides
    for table, out in zip(tables, outs):
        side, kind = table[0:1, :], table[1:2, :]
        col, row = table[2:3, :], table[3:4, :]
        row = jnp.where(kind == 1, row_a, jnp.where(kind == 2, row_b, row))
        for query_side in range(sides):
            spot = lane if query_side == 0 else 1 - lane
            tile_col = place[COL] - lane + spot
            cols = (side - query_side) * (1 - 2 * lane) * tile_w + col
            cols = jnp.where(kind == 3, -1 - spot * tile_w, cols)
            cols = jnp.where(kind == 4, (sides - spot) * tile_w, cols)
            block = (
                ((row >= 0).astype(jnp.int32) + (row >= tile_h).astype(jnp.int32)) * 3
                + (cols >= 0).astype(jnp.int32)
                + (cols >= tile_w).astype(jnp.int32)
            )
            flag = jnp.zeros(block.shape, jnp.float32)
            for index in range(9):
                pattern = patterns[query_side]
                if len(pattern.shape) == 3:
                    last = pattern.shape[0] - 1
                    value = pattern[last, 0:1, index : index + 1].astype(jnp.float32)
                else:
                    value = pattern[0, index].astype(jnp.float32)
                flag = jnp.where(block == index, value, flag)
            grid_row, grid_col = row + place[ROW] * tile_h, cols + tile_col * tile_w
            inside = (grid_row >= 0) & (grid_row < n_th * tile_h)
            inside &= (grid_col >= 0) & (grid_col < n_tw * tile_w)
            inside &= (cols >= -HALO) & (cols < tile_w + HALO)
            out[query_side : query_side + 1, :] = jnp.where(inside, flag, 0.0)


def row_order(tile_h):
    return [0, tile_h - 1] + list(range(1, tile_h - 1))


def key_value_kernel(live, spec, sources, chosen, place, *refs):
    sides, tile_h, _, n_th, _ = spec
    count = sum(pieces for _, pieces in sources)
    parts, (mod, weight), refs = refs[:count], refs[count : count + 2], refs[count + 2 :]
    x_out, modded, kv = refs[:3]
    inner = kv.shape[1] // 2
    order = row_order(tile_h)
    strip_row = kv.shape[0] // len(chosen)
    base = order.index(chosen[0]) * strip_row

    @pl.when(is_active(place, live))
    def _():
        first = 0
        for holders, pieces in sources:
            if len(parts[first].shape) == 3:
                tile, turned = refs[-2:]

                @pl.when(is_active(place, holders))
                def _(first=first):
                    edge = strip_row // sides
                    for side in range(sides):
                        frames = parts[first + side][: edge].astype(jnp.float32)
                        frames = frames.reshape(tile.shape[1], turned.shape[1])
                        for low in range(0, turned.shape[1], HEAD):
                            lanes = tile.at[low // HEAD]
                            lanes[...] = frames[:, low : low + HEAD]
                            for index, row in enumerate(chosen):
                                start = index * strip_row + side * edge
                                turned[start : start + edge, low : low + HEAD] = lanes[
                                    pl.ds(row, edge, stride=tile_h), :
                                ]

            first += pieces
        gain, shift = 1.0 + mod[1:2, :], mod[0:1, :]
        for start in range(0, kv.shape[0], BLOCK):
            rows = slice(start, start + BLOCK)
            value, first = None, 0
            for holders, pieces in sources:
                if len(parts[first].shape) == 3:
                    part = turned[rows, :]
                else:
                    index, within = divmod(start, parts[first].shape[0])
                    part = parts[first + index][within : within + BLOCK, :].astype(jnp.float32)
                value = part if value is None else jnp.where(is_active(place, holders), part, value)
                first += pieces
            x_out[rows, :] = value.astype(jnp.bfloat16)
            centred = value - jnp.mean(value, axis=-1, keepdims=True)
            variance = jnp.mean(centred * centred, axis=-1, keepdims=True)
            normed = centred * lax.rsqrt(variance + 1e-06)
            modded[rows, :] = (normed * gain + shift).astype(jnp.bfloat16)
        row_a, row_b, _ = neighbour_rows(place, n_th, tile_h)
        low_a, low_b = row_a > 0, row_b > 0
        if n_th % 2:
            low_a, low_b = low_b, low_a
        for start in range(0, 2 * inner, CHUNK):
            projected = jnp.dot(
                modded[...], weight[:, start : start + CHUNK], preferred_element_type=jnp.float32
            )
            for low in range(0, CHUNK, HEAD):
                columns = pl.ds(start + low, HEAD)
                head = projected[:, low : low + HEAD]
                if start < inner:
                    head = head_norm(head)
                head = head.astype(jnp.bfloat16)
                kv[:, columns] = head
                if base == 0:
                    send_a, send_b = refs[3:5]
                    top, bottom = head[:strip_row], head[strip_row : 2 * strip_row]
                    send_a[:, columns] = jnp.where(low_a, bottom, top)
                    send_b[:, columns] = jnp.where(low_b, bottom, top)


def together(parts, columns):
    if len(parts) == 1:
        return parts[0][:, columns]
    return jnp.concatenate([part[:, columns] for part in parts], axis=0)


def masked(mask_ref, tile_h, edge):
    sides, keys = mask_ref.shape
    rows = [jnp.broadcast_to(mask_ref[s : s + 1, :], (edge, keys)) for s in range(sides)]
    return jnp.concatenate(rows * tile_h, axis=0)


def weigh(queries, keys, values, mask):
    scores = [
        lax.dot_general(query, key, (((1,), (1,)), ((), ())), preferred_element_type=jnp.float32)
        for query, key in zip(queries, keys)
    ]
    weights = [
        (jnp.exp2(score * (1.0 / (math.sqrt(HEAD) * math.log(2.0)))) * mask).astype(jnp.bfloat16) for score in scores
    ]
    ones = jnp.ones((values[0].shape[0], HEAD), jnp.bfloat16)
    both = [
        jnp.dot(w, jnp.concatenate([v, ones], axis=1), preferred_element_type=jnp.float32)
        for w, v in zip(weights, values)
    ]
    return [b[:, :HEAD] for b in both], [b[:, HEAD:] for b in both]


def groups(inner):
    heads = [pl.ds(low, HEAD) for low in range(0, inner, HEAD)]
    return [heads[low : low + GROUP] for low in range(0, len(heads), GROUP)]


def first_key_value_kernel(live, spec, sources, chosen, place, qkv, *refs):
    loaded, scratch, sem = refs[-4], refs[-3:-1], refs[-1]
    width = loaded.shape[1]
    copy = pltpu.make_async_copy(qkv.at[:, pl.ds(0, width)], loaded, sem.at[0])
    copy.start()
    key_value_kernel(live, spec, sources, chosen, place, *refs[:-4], *scratch)
    copy.wait()


def first_query_kernel(live, spec, passes, place, *refs):
    tokens = 2 * passes + 1
    sides, tokens, refs = spec[0], refs[:tokens], refs[tokens:]
    patterns, tables, out_weight = refs[:sides], refs[sides : sides + 2], refs[sides + 2]
    queries, top, bottom, own_mask, extra_mask, loaded, sem = refs[sides + 3 :]
    copy = pltpu.make_async_copy(out_weight, loaded, sem.at[0])
    copy.start()
    write_masks(spec, place, patterns, tables, (own_mask, extra_mask))
    query_kernel(live, spec, passes, place, *tokens, own_mask, queries, top, bottom)
    copy.wait()


def second_query_kernel(live, spec, passes, place, *refs):
    tokens = 2 * passes + 1
    sides, tokens, refs = spec[0], refs[:tokens], refs[tokens:]
    patterns, tables, refs = refs[:sides], refs[sides : sides + 2], refs[sides + 2 :]
    queries, top, bottom, own_mask, extra_mask = refs
    write_masks(spec, place, patterns, tables, (own_mask, extra_mask))
    query_kernel(live, spec, passes, place, *tokens, own_mask, queries, top, bottom)


def query_kernel(live, spec, passes, place, *refs):
    modded, kv, refs = refs[:passes], refs[passes : 2 * passes], refs[2 * passes :]
    weight, mask_ref, queries, top, bottom = refs
    sides, tile_h = spec[:2]
    rows, inner = queries.shape

    @pl.when(is_active(place, live))
    def _():
        mask = masked(mask_ref, tile_h, rows // (sides * tile_h))
        tokens = together(modded, slice(None))
        found = []
        for start in range(0, inner, CHUNK):
            projected = jnp.dot(
                tokens, weight[:, start : start + CHUNK], preferred_element_type=jnp.float32
            )
            for low in range(0, CHUNK, HEAD):
                query = head_norm(projected[:, low : low + HEAD]).astype(jnp.bfloat16)
                found.append(query)
                queries[:, start + low : start + low + HEAD] = query
        for group in groups(inner):
            above, below = weigh(
                [found[columns.start // HEAD] for columns in group],
                [together(kv, columns) for columns in group],
                [together(kv, pl.ds(inner + columns.start, HEAD)) for columns in group],
                mask,
            )
            for index, columns in enumerate(group):
                top[:, columns] = above[index]
                bottom[:, columns] = below[index]


def output_kernel(live, spec, extra_count, passes, place, *refs):
    extras, refs = refs[:extra_count], refs[extra_count:]
    (queries, top, bottom, mask_ref), refs = refs[:4], refs[4:]
    x, (mod, weight), refs = refs[:passes], refs[passes : passes + 2], refs[passes + 2 :]
    outs, (attended, turned) = refs[:-2], refs[-2:]
    sides, tile_h, _, n_th, _ = spec
    inner, width = weight.shape
    edge = queries.shape[0] // (sides * tile_h)

    @pl.when(is_active(place, live))
    def _():
        mask = masked(mask_ref, tile_h, edge)
        valid = neighbour_rows(place, n_th, tile_h)[2]

        def received(columns):
            pieces = []
            for index, extra in enumerate(extras):
                piece = extra[:, columns]
                if index < 2:
                    piece = jnp.where(valid[index], piece, jnp.zeros_like(piece))
                pieces.append(piece)
            return jnp.concatenate(pieces, axis=0)

        for heads in groups(inner):
            above, below = weigh(
                [queries[:, columns] for columns in heads],
                [received(columns) for columns in heads],
                [received(pl.ds(inner + columns.start, HEAD)) for columns in heads],
                mask,
            )
            for index, columns in enumerate(heads):
                total = (top[:, columns] + above[index]) / (bottom[:, columns] + below[index])
                attended[:, columns] = total.astype(jnp.bfloat16)
        for start in range(0, width, CHUNK):
            columns = pl.ds(start, CHUNK)
            projected = jnp.dot(
                attended[...], weight[:, start : start + CHUNK], preferred_element_type=jnp.float32
            )
            updated = together(x, columns).astype(jnp.float32)
            updated += mod[2:3, start : start + CHUNK] * projected
            first = 0
            for y in outs:
                if len(y.shape) == 2:
                    y[:, columns] = updated[first : first + y.shape[0]].astype(jnp.bfloat16)
                    first += y.shape[0]
            for side, y in enumerate([y for y in outs if len(y.shape) == 3]):
                for low in range(0, CHUNK, HEAD):
                    lanes = turned.at[(side * CHUNK + low) // HEAD]
                    for index, row in enumerate(row_order(tile_h)):
                        first = (index * sides + side) * edge
                        lanes[pl.ds(row, edge, stride=tile_h), :] = updated[
                            first : first + edge, low : low + HEAD
                        ]
                    tile = lanes[...].reshape(*y.shape[:2], HEAD).astype(jnp.bfloat16)
                    y[:, :, pl.ds(start + low, HEAD)] = tile


def choose_kernel(wanted, place, *refs):
    pieces, out, sem = refs[:-2], refs[-2], refs[-1]
    rows = out.shape[0] // len(wanted)
    for index, options in enumerate(wanted):
        for segment, lane, sides, source in options:

            @pl.when((place[SEG] == segment) & (place[COL] % sides == lane))
            def _(index=index, source=source):
                copy = pltpu.make_async_copy(
                    pieces[source], out.at[pl.ds(index * rows, rows)], sem.at[0]
                )
                copy.start()
                copy.wait()


def gather_copies(place, order, tokens, outs, wanted, sides, sems):
    copies = []
    for slot, (out, (base, other)) in enumerate(zip(outs, wanted)):
        patch = base + (place[COL] + other) % sides
        rows = out.shape[0] // FRAME_PATCH
        for frame in range(FRAME_PATCH):
            source = order[patch * FRAME_PATCH + frame]
            copies.append(
                pltpu.make_async_copy(
                    tokens.at[pl.ds(source * rows, rows)],
                    out.at[pl.ds(frame * rows, rows)],
                    sems.at[slot, frame],
                )
            )
    for copy in copies:
        copy.start()
    return copies


def gather_kernel(wanted, sides, place, tokens, stored_order, stored_pattern, *refs):
    outs, (order, pattern, small, sems) = refs[:-4], refs[-4:]
    fetches = [
        pltpu.make_async_copy(stored_order, order, small.at[0]),
        pltpu.make_async_copy(stored_pattern, pattern, small.at[1]),
    ]
    for fetch in fetches:
        fetch.start()
    for fetch in fetches:
        fetch.wait()
    copies = gather_copies(place, order, tokens, outs, wanted, sides, sems)
    shape = (1,) + outs[0].shape[1:]
    lanes = lax.broadcasted_iota(jnp.int32, shape, 2)
    block = jnp.zeros(shape, jnp.float32)
    for index in range(9):
        block = jnp.where(lanes == index, pattern[0, index].astype(jnp.float32), block)
    for out in outs:
        out[out.shape[0] - 1 :] = block.astype(jnp.bfloat16)
    for copy in copies:
        copy.wait()


def load_kernel(wanted, sides, place, order, tokens, qkv, loaded, *refs):
    outs, frame_sems, sem = refs[:-2], refs[-2], refs[-1]
    columns = loaded.shape[1]
    copy = pltpu.make_async_copy(qkv.at[:, pl.ds(columns // 2, columns)], loaded, sem.at[0])
    copy.start()
    for frame in gather_copies(place, order, tokens, outs, wanted, sides, frame_sems):
        frame.wait()
    copy.wait()


def run(
    kernel,
    scalars,
    operands,
    outs,
    scratch,
    name,
    memory=pltpu.VMEM,
    limit=VMEM_BYTES,
    after=(),
    out_memory=pltpu.VMEM,
    fixed=None,
):
    result, smem = pl.BlockSpec(memory_space=out_memory), pl.BlockSpec(memory_space=pltpu.SMEM)
    if memory is pltpu.HBM:
        operands = [pltpu.with_memory_space_constraint(o, memory) for o in operands]
    skipped = len(after)
    in_specs = [pl.BlockSpec(memory_space=pl.ANY)] * skipped + [smem] * len(scalars)
    for operand in operands:
        small = operand.dtype == jnp.int32 and operand.shape[-1] == 9 and memory is not pltpu.HBM
        large = operand is fixed
        spec = pl.BlockSpec(memory_space=pltpu.HBM if large else memory)
        in_specs.append(smem if small else spec)
    return pl.pallas_call(
        lambda *refs: kernel(tuple(lax.axis_index(a) for a in AXES), *refs[skipped:]),
        out_shape=outs,
        in_specs=in_specs,
        out_specs=jax.tree.map(lambda _: result, outs),
        scratch_shapes=scratch,
        compiler_params=pltpu.CompilerParams(vmem_limit_bytes=limit),
        cost_estimate=pl.CostEstimate(flops=2**32, bytes_accessed=2**20, transcendentals=0),
        name=name,
    )(*after, *scalars, *operands)


def arrays(*shapes):
    return tuple(jax.ShapeDtypeStruct(shape, dtype) for shape, dtype in shapes)


def exchange(value, partner):
    sizes = [lax.axis_size(axis) for axis in AXES]
    places = [(s, t, w) for s in range(sizes[0]) for t in range(sizes[1]) for w in range(sizes[2])]
    number = {place: index for index, place in enumerate(places)}
    links = [(number[p], number[partner(*p)]) for p in places if partner(*p) in number]
    return lax.ppermute(value, AXES, links)


def on_device(tokens, frame_order, tile_pattern, qkv_weight, out_weight, modulation):
    n_seg, n_th, n_tw = [lax.axis_size(axis) for axis in AXES]
    seg, row_tile, col_tile = [lax.axis_index(axis) for axis in AXES]
    frames, tile_h, tile_w, width = tokens.shape
    inner = out_weight.shape[1]
    patches = frames // FRAME_PATCH
    held_patches = patches // n_seg
    sides = 2 if n_tw % 2 == 0 and patches % 2 == 0 else 1
    rounds = patches // sides
    tile_rows = FRAME_PATCH * tile_h * tile_w
    edge_rows = FRAME_PATCH * tile_w
    strip_rows = sides * tile_rows

    lane = col_tile % sides
    bf16, f32 = jnp.bfloat16, jnp.float32

    def beside(w):
        return w + 1 - 2 * (w % 2)

    def patch_base(turn):
        return (rounds - 1 - turn) * sides

    def token_swap(s, t, w):
        if s == n_seg - 1:
            return (s, t, beside(w))
        return (s, t + 1 - 2 * (t % 2), w) if n_th % 2 == 0 else None

    stored = tokens.transpose(0, 2, 1, 3).reshape(frames * tile_w, tile_h, width)
    tile_shape = ((edge_rows, tile_h, width), bf16)
    theirs, pattern = [], tile_pattern[0]
    patterns = [pattern]
    if sides == 2:
        messages = run(
            functools.partial(gather_kernel, [(patch_base(turn), 1) for turn in range(rounds)], sides),
            [],
            [stored, frame_order, pattern],
            arrays(*[((edge_rows + 1, tile_h, width), bf16)] * rounds),
            [
                pltpu.SMEM(frame_order.shape, jnp.int32),
                pltpu.SMEM(pattern.shape, jnp.int32),
                pltpu.SemaphoreType.DMA((2,)),
                pltpu.SemaphoreType.DMA((rounds, FRAME_PATCH)),
            ],
            "gather",
            pltpu.HBM,
            2**20,
        )
        theirs = [exchange(message, token_swap) for message in messages]
        patterns.append(exchange(pattern, lambda s, t, w: (s, t, beside(w))))
        messages, qkv_weight = lax.optimization_barrier((messages, qkv_weight))
    wanted = [(patch_base(turn), 0) for turn in range(rounds)]
    kv_w, *tiles = run(
        functools.partial(load_kernel, wanted, sides),
        [frame_order],
        [stored, qkv_weight[0]],
        (pltpu.VMEM((width, 2 * inner), bf16),)
        + arrays(*[tile_shape] * rounds),
        [pltpu.SemaphoreType.DMA((rounds, FRAME_PATCH)), pltpu.SemaphoreType.DMA((1,))],
        "load_weights",
        pltpu.HBM,
        2**20,
    )
    kv_w = pltpu.with_memory_space_constraint(kv_w, pltpu.VMEM)
    fresh = [[tiles[turn]] + ([theirs[turn]] if sides == 2 else []) for turn in range(rounds)]
    stored_qkv, stored_out = [
        pltpu.with_memory_space_constraint(w[0], pltpu.HBM) for w in (qkv_weight, out_weight)
    ]
    mod = modulation[0]

    side_halo = n_tw > sides
    order = row_order(tile_h)
    grid = np.indices((tile_h, sides, FRAME_PATCH, tile_w)).reshape(4, -1)
    own_table = np.stack([grid[1], 0 * grid[1], grid[3], np.asarray(order)[grid[0]]])
    strip_edge = np.indices((sides, FRAME_PATCH, tile_w)).reshape(3, -1)
    extra = [
        np.stack([strip_edge[0], 0 * strip_edge[0] + kind, strip_edge[2], 0 * strip_edge[0]])
        for kind in (1, 2)
    ]
    if side_halo:
        tall = np.repeat(np.arange(-HALO, tile_h + HALO), FRAME_PATCH)
        extra += [np.stack([0 * tall, 0 * tall + kind, 0 * tall, tall]) for kind in (3, 4)]
    tables = [jnp.asarray(t, jnp.int32) for t in (own_table, np.concatenate(extra, axis=1))]

    first = {n_seg - 1: 0}
    for s in range(n_seg - 1, 0, -1):
        first[s - 1] = first[s] + (1 if s % 2 else 2)
    steps = first[0] + rounds
    spec = (sides, tile_h, tile_w, n_th, n_tw)
    paired_rows, paired_segs = n_th % 2 == 0, n_seg % 2 == 0

    def running(step):
        return [s for s in range(n_seg) if 0 <= step - first[s] < rounds]

    def sources_of(step):
        live = running(step)
        found = []
        if n_seg - 1 in live:
            found.append(("fresh", [n_seg - 1]))
        near_to = [s for s in live if s % 2 == 0 and s != n_seg - 1]
        far_to = [s for s in live if s % 2 == 1 and s != n_seg - 1]
        return found + [("near", near_to)] * bool(near_to) + [("far", far_to)] * bool(far_to)

    def spare(live, s, t, w):
        if paired_segs and s ^ 1 not in live:
            return (s ^ 1, t, w)
        return (s, t, beside(w)) if n_tw % 2 == 0 else None

    def rows_a(live):
        def partner(s, t, w):
            if not paired_rows:
                return (s, t + 1, w)
            return (s, t + 1 - 2 * (t % 2), w) if s in live else spare(live, s, t, w)

        return partner

    def rows_b(live):
        def partner(s, t, w):
            other = t - 1 + 2 * (t % 2) if paired_rows else t - 1
            if paired_rows and not 0 <= other < n_th:
                return (s ^ 1, t, w) if paired_segs else None
            if s in live or not paired_rows:
                return (s, other, w)
            if live == [n_seg - 1] and n_seg == 4:
                return (3 - s, t, w) if s in (1, 2) else (s, t, beside(w))
            return spare(live, s, t, w)

        return partner

    def near_hop(s, t, w):
        return (s ^ 1, t, w) if paired_segs else (s - 1, t, w) if s % 2 else None

    def far_hop(s, t, w):
        return (s - 1, t, w) if s % 2 == 0 and s > 0 else None

    def far_swap(s, t, w):
        return (s + 1, t, w) if s % 2 and s < n_seg - 1 else far_hop(s, t, w)

    def edge_column(kv, above, below, which):
        shape = (-1, sides, FRAME_PATCH, tile_w, 2 * inner)
        rows = jnp.concatenate(kv, axis=0).reshape(shape)
        edge, middle = rows[:2], rows[2:]
        ends = [part.reshape(shape) for part in (above, below)]
        tall = jnp.concatenate([ends[0], edge[:1], middle, edge[1:], ends[1]], axis=0)
        if which == 0:
            column = jnp.where(lane == 0, tall[:, 0, :, 0], tall[:, sides - 1, :, 0])
        else:
            column = jnp.where(lane == 0, tall[:, sides - 1, :, -1], tall[:, 0, :, -1])
        return column.reshape(-1, 2 * inner)

    kept = []

    def layer(step, live, sources, before):
        strip, edges = strip_rows, sides * edge_rows

        def key_value(chosen, sends, **rest):
            rows = len(chosen) * edges
            operands, counts = [], []
            for holders, source in sources:
                if source[0].ndim == 2 and len(chosen) < tile_h:
                    source = source[:1] if chosen[0] == 0 else source[1:]
                operands += source
                counts.append((holders, len(source)))
            operands += [mod, kv_w]
            outs = [((rows, width), bf16), ((rows, width), bf16), ((rows, 2 * inner), bf16)]
            native = any(part.ndim == 3 for part in operands)
            turn = [((width // HEAD, tile_rows, HEAD), f32), ((rows, width), f32)] * native
            return run(
                functools.partial(rest.pop("kernel"), live, spec, counts, chosen),
                [],
                rest.pop("first", []) + operands,
                arrays(*outs, *[((edges, 2 * inner), bf16)] * sends) + rest.pop("more", ()),
                [pltpu.VMEM(shape, kind) for shape, kind in turn] + rest.pop("scratch", []),
                "key_value",
                **rest,
            )

        passes = [order[:2], order[2:]] if 0 < step < steps - 1 else [order]
        x, modded, kv = [], [], []
        if step == 0:
            *found, send_a, send_b, q_w = key_value(
                order,
                2,
                kernel=first_key_value_kernel,
                first=[stored_qkv],
                more=(pltpu.VMEM((width, inner), bf16),),
                scratch=[pltpu.SemaphoreType.DMA((1,))],
                fixed=stored_qkv,
            )
            kept.append(pltpu.with_memory_space_constraint(q_w, pltpu.VMEM))
            for held, part in zip((x, modded, kv), found):
                held.append(part)
        else:
            for index, chosen in enumerate(passes):
                found = key_value(
                    chosen,
                    0 if index else 2,
                    kernel=key_value_kernel,
                    after=[send_a] if index else before,
                )
                for held, part in zip((x, modded, kv), found):
                    held.append(part)
                if not index:
                    send_a, send_b = found[3:]
        tokens = modded + kv
        count = len(passes)
        extra_a = exchange(send_a, rows_a(live))
        extra_b = exchange(send_b, rows_b(live))
        outs = arrays(((strip, inner), bf16), ((strip, inner), f32), ((strip, inner), f32))
        if step == 0:
            made = arrays(*[((sides, table.shape[1]), f32) for table in tables])
            queries, top, bottom, own_mask, extra_mask, out_w = run(
                functools.partial(first_query_kernel, live, spec, count),
                [],
                tokens + [kept[0], pattern] + fresh[0][1:] + tables + [stored_out],
                outs + made + (pltpu.VMEM((inner, width), bf16),),
                [pltpu.SemaphoreType.DMA((1,))],
                "query",
                fixed=stored_out,
            )
            out_w = pltpu.with_memory_space_constraint(out_w, pltpu.VMEM)
            kept.extend([own_mask, extra_mask, out_w])
        elif step == 1:
            made = arrays(*[((sides, table.shape[1]), f32) for table in tables])
            queries, top, bottom, *kept[1:3] = run(
                functools.partial(second_query_kernel, live, spec, count),
                [],
                tokens + [kept[0]] + patterns + tables,
                outs + made,
                [],
                "query",
            )
        else:
            queries, top, bottom = run(
                functools.partial(query_kernel, live, spec, count),
                [],
                tokens + kept[:2],
                outs,
                [],
                "query",
            )
        extra_mask, out_w = kept[2:]
        extras = [extra_a, extra_b]
        if side_halo:
            flip = (row_tile % 2 == 1) if paired_rows else jnp.array(True)
            above = jnp.where(flip, extra_a, extra_b)
            below = jnp.where(flip, extra_b, extra_a)
            above = jnp.where(row_tile > 0, above, jnp.zeros_like(above))
            below = jnp.where(row_tile < n_th - 1, below, jnp.zeros_like(below))
            left = edge_column(kv, above, below, 0)
            right = edge_column(kv, above, below, 1)
            from_left = exchange(right, lambda s, t, w: (s, t, w + sides))
            from_right = exchange(left, lambda s, t, w: (s, t, w - sides))
            extras.append(jnp.concatenate([from_left, from_right], axis=0))
        shapes = [((2 * edges, width), bf16), ((strip - 2 * edges, width), bf16)]
        shapes = shapes * (live != [0]) + [tile_shape] * (sides * (0 in live))
        found = run(
            functools.partial(output_kernel, live, spec, len(extras), count),
            [],
            extras + [queries, top, bottom, extra_mask] + x + [mod, out_w],
            arrays(*shapes),
            [pltpu.VMEM((strip, inner), bf16), pltpu.VMEM((sides * CHUNK // HEAD, tile_rows, HEAD), f32)],
            "output",
            after=[turn[-1] for turn in fresh[1:]] if step == 0 and sides == 2 else (),
        )
        return (found[:2], found[2:]) if live != [0] else ((), found)

    def owner_of(turn, w):
        return (patch_base(turn) + w % sides) // held_patches

    def beside_chip(turn):
        return sides == 2 and paired_segs and all(owner_of(turn, w) < 2 for w in range(sides))

    def deliver(turn, tiles):
        sent = [
            exchange(
                tile,
                lambda s, t, w: (owner_of(turn, w), t, beside(w) if side else w)
                if s == 0
                else None,
            )
            for side, tile in enumerate(tiles)
            if side or not beside_chip(turn)
        ]
        if beside_chip(turn):
            return [tiles[0]] + sent + [exchange(tiles[0], near_hop)]
        return sent

    near = far = far_next = None
    finished = {}
    y = ()
    for step in range(steps):
        live = running(step)
        options = {"near": near, "far": far}
        if step < rounds:
            options["fresh"] = fresh[step]
        found = [(holders, options[kind]) for kind, holders in sources_of(step)]
        y, finals = layer(step, live, found, y)
        near, far, far_next = None, far_next, None
        if any(s % 2 == 1 for s in live):
            near = [exchange(part, near_hop) for part in y]
        if any(s % 2 == 0 and s > 0 for s in live):
            far_next = [exchange(y[0], far_hop), exchange(y[1], far_swap)]
        if 0 in live:
            turn = step - first[0]
            finished[turn] = deliver(turn, finals)
    pieces, wanted = [], []
    for held in range(held_patches):
        options = []
        for owner in range(n_seg):
            patch = owner * held_patches + held
            turn, member = rounds - 1 - patch // sides, patch % sides
            base = sum(len(finished[other]) for other in range(turn))
            for w in range(sides):
                own = 2 * owner if beside_chip(turn) else 0
                options.append((owner, w, sides, base + (own if w == member else 1)))
        wanted.append(options)
    for turn in range(rounds):
        pieces += finished[turn]
    (chosen,) = run(
        functools.partial(choose_kernel, wanted),
        [],
        pieces,
        arrays(((held_patches * edge_rows, tile_h, width), bf16)),
        [pltpu.SemaphoreType.DMA((1,))],
        "choose",
        pl.ANY,
        out_memory=pl.ANY,
    )
    shaped = chosen.reshape(held_patches * FRAME_PATCH, tile_w, tile_h, width)
    return shaped.transpose(0, 2, 1, 3)


def solution(mesh):
    in_specs = (
        P(None, "th", "tw", None),
        P(),
        P("th", "tw", None),
        P("segment", None, None),
        P("segment", None, None),
        P("segment", None, None),
    )
    out_specs = P("segment", "th", "tw", None)
    return jax.shard_map(
        on_device, mesh=mesh, in_specs=in_specs, out_specs=out_specs, check_vma=False
    )
```
